32 devices in a mesh: fsdp: 16 (over z, y, core), tp: 2 (over x).
Axes of the slice: x: 2, y: 2, z: 4, core: 2. Of those that a mesh axis runs over, the one named last changes fastest.
Arguments:
- inputs: bfloat16 [32, 1024, 1024], P('fsdp', 'tp'), may hold values from -6 to 6
- segment_ids: int32 [32, 1024], P('fsdp'), may hold values from 0 to 3, as said below
- valid_mask: int32 [32, 1024], P('fsdp', 'tp'), may hold values from 0 to 1
- teacher: bfloat16 [32, 1024, 1024], P('fsdp', 'tp'), may hold values from -6 to 6
- w_query: bfloat16 [1024, 1024], P('fsdp', 'tp'), may hold values from -0.1875 to 0.1875
- w_key: bfloat16 [1024, 1024], P('fsdp', 'tp'), may hold values from -0.1875 to 0.1875
- w_value: bfloat16 [1024, 1024], P('fsdp', 'tp'), may hold values from -0.1875 to 0.1875
- w_out: bfloat16 [1024, 1024], P('tp', 'fsdp'), may hold values from -0.75 to 0.75
- b_query: bfloat16 [1024], P(('tp', 'fsdp')), may hold values from -3 to 3
- b_value: bfloat16 [1024], P(('tp', 'fsdp')), may hold values from -3 to 3
- w_up: bfloat16 [1024, 4096], P('fsdp', 'tp'), may hold values from -0.1875 to 0.1875
- b_up: bfloat16 [4096], P(('tp', 'fsdp')), may hold values from -3 to 3
- w_down: bfloat16 [4096, 1024], P('tp', 'fsdp'), may hold values from -0.09375 to 0.09375
- ln_gains: bfloat16 [2, 1024], P(None, 'fsdp'), may hold values from 0.5 to 1.5
- ln_shifts: bfloat16 [4, 1024], P(None, 'fsdp'), may hold values from -2 to 2
Outputs:
- hidden_out: bfloat16 [32, 1024, 1024], P('fsdp', 'tp')
- loss_value: float32 [], replicated
- grad_inputs: bfloat16 [32, 1024, 1024], P('fsdp', 'tp')
- grad_w_query: float32 [1024, 1024], P('fsdp', 'tp')
- grad_w_key: float32 [1024, 1024], P('fsdp', 'tp')
- grad_w_value: float32 [1024, 1024], P('fsdp', 'tp')
- grad_w_out: float32 [1024, 1024], P('tp', 'fsdp')
- grad_b_query: float32 [1024], P(('tp', 'fsdp'))
- grad_b_value: float32 [1024], P(('tp', 'fsdp'))
- grad_w_up: float32 [1024, 4096], P('fsdp', 'tp')
- grad_b_up: float32 [4096], P(('tp', 'fsdp'))
- grad_w_down: float32 [4096, 1024], P('tp', 'fsdp')
- grad_ln_gains: float32 [2, 1024], P(None, 'fsdp')
- grad_ln_shifts: float32 [4, 1024], P(None, 'fsdp')
The draws below stay inside these ranges and needn't reach their ends.
Inputs may be any that keep to these rules, and one draw needn't show every extreme that they name: `segment_ids`: ids never fall along a row.
All inputs are finite; a program needn't handle non-finite values.
Results may differ from the reference program's by a relative error of at most 0.022.
Values may be sent and summed in bfloat16 or wider, within the bound.
No kernel may reach another device: no remote copies, remote signals or barrier semaphores. Data moves between devices by JAX's collectives and lax.ppermute only.
A program may use at most 384 MiB of HBM per device.

```python
import math
import jax
import jax.numpy as jnp
from jax import lax

D = 1024
HEAD_DIM = 64
FF = 4096
LENGTH = 1024
WINDOW = 512
SEQS_DEV = 2
ROWS = 32
TOKENS = 32768
N_FSDP = 16
N_TP = 2


def draw_segment_ids(key, part):
    key = jax.random.fold_in(key, 11)
    cut_key, edge_key, pick_key = jax.random.split(key, 3)
    piece_len = LENGTH // N_TP
    cut_points = jax.random.randint(cut_key, (ROWS, 3), 1, LENGTH)
    first_cut = jax.random.randint(edge_key, (ROWS, 1), 1, piece_len)
    late_cuts = jax.random.randint(jax.random.fold_in(edge_key, 1), (ROWS, 2), LENGTH - piece_len + 1, LENGTH)
    spanning = jnp.concatenate([first_cut, late_cuts], axis=1)
    chosen = jax.random.randint(pick_key, (N_FSDP, 1), 0, SEQS_DEV)
    row_number = jnp.arange(SEQS_DEV, dtype=jnp.int32)[None, :]
    picked = (row_number == chosen).reshape(ROWS, 1)
    cut_points = jnp.where(picked, spanning, cut_points)
    position = jnp.arange(LENGTH, dtype=jnp.int32)
    return jnp.sum((position[None, :, None] >= cut_points[:, None, :]).astype(jnp.int32), axis=-1).astype(jnp.int32)


def draw_valid_mask(key, part):
    key = jax.random.fold_in(key, 23)
    row_number = jnp.arange(ROWS, dtype=jnp.int32)[:, None]
    position = jnp.arange(LENGTH, dtype=jnp.int32)[None, :]
    limit = 128 + 384 * row_number // ROWS + 384 * position // LENGTH
    return (jax.random.randint(key, (ROWS, LENGTH), 0, 1024) < limit).astype(jnp.int32)


def strengthened(drawn, key, source, target, parts, factor):
    def block_of(dim):
        return (jnp.arange(drawn.shape[dim]) // (drawn.shape[dim] // parts)).reshape((-1,) + (1,) * (drawn.ndim - 1 - dim))

    one_side = jax.random.permutation(key, parts)[block_of(target)]
    other_side = (block_of(target) + parts // 2) % parts
    return jnp.where((block_of(source) == one_side) | (block_of(source) == other_side), factor * drawn, drawn)


def block_levels(rng, shape, cuts, smallest, high):
    factor_of = 1.0
    for dim, blocks in cuts:
        steps = jax.random.uniform(jax.random.fold_in(jax.random.fold_in(rng, 6), dim), (blocks,), jnp.float32, smallest / len(cuts), high / len(cuts))
        factor_of = factor_of * jnp.repeat(jnp.exp(steps), shape[dim] // blocks).reshape((-1,) + (1,) * (len(shape) - 1 - dim))
    return factor_of


def gaussian(stream_key, dims, scale, most, cuts=(), kind=jnp.bfloat16):
    level = block_levels(stream_key, dims, cuts, -0.22, 0.18) if cuts else 1.0
    drawn = jax.random.normal(stream_key, dims, jnp.float32) * scale * level
    return jnp.minimum(jnp.maximum(drawn, -most), most).astype(kind)


def gaussian_with(key, extent, deviation, bound, cuts, heavy, kind=jnp.bfloat16):
    array = deviation * jax.random.normal(key, extent, jnp.float32)
    if cuts:
        array = array * block_levels(key, extent, cuts, -0.22, 0.18)
    return jnp.clip(strengthened(array, jax.random.fold_in(key, 3), *heavy), -bound, bound).astype(kind)


def setup_inputs(seed: int = 0) -> dict:
    arg_keys = jax.random.split(jax.random.key(seed), 16)
    inputs = gaussian_with(arg_keys[0], (ROWS, LENGTH, D), 1.0, 6.0, ((0, 16), (1, 2)), (0, 2, 16, 2.0))
    segment_ids = draw_segment_ids(jax.random.fold_in(arg_keys[15], 71), 0)
    valid_mask = draw_valid_mask(jax.random.fold_in(arg_keys[15], 71), 0)
    teacher = gaussian(arg_keys[3], (ROWS, LENGTH, D), 1.0, 6.0, ((0, 16), (1, 2)))
    w_query = gaussian(arg_keys[4], (D, D), D ** -0.5, 0.1875, ((0, 16), (1, 2)))
    w_key = gaussian(arg_keys[5], (D, D), D ** -0.5, 0.1875, ((0, 16), (1, 2)))
    w_value = gaussian(arg_keys[6], (D, D), D ** -0.5, 0.1875, ((0, 16), (1, 2)))
    w_out = gaussian(arg_keys[7], (D, D), (D // 16) ** -0.5, 0.75, ((0, 2), (1, 16)))
    b_query = gaussian(arg_keys[8], (D,), 0.5, 3.0, ((0, 32),))
    b_value = gaussian(arg_keys[9], (D,), 0.5, 3.0, ((0, 32),))
    w_up = gaussian(arg_keys[10], (D, FF), D ** -0.5, 0.1875, ((0, 16), (1, 2)))
    b_up = gaussian(arg_keys[11], (FF,), 0.5, 3.0, ((0, 32),))
    w_down = gaussian(arg_keys[12], (FF, D), FF ** -0.5, 0.09375, ((0, 2), (1, 16)))
    ln_gains = jnp.clip(1.0 + 0.1 * jax.random.normal(arg_keys[13], (2, D), jnp.float32), 0.5, 1.5).astype(jnp.bfloat16)
    ln_shifts = gaussian(arg_keys[14], (4, D), 0.3, 2.0, ((1, 16),))
    return dict(inputs=inputs, segment_ids=segment_ids, valid_mask=valid_mask, teacher=teacher, w_query=w_query, w_key=w_key, w_value=w_value, w_out=w_out, b_query=b_query, b_value=b_value, w_up=w_up, b_up=b_up, w_down=w_down, ln_gains=ln_gains, ln_shifts=ln_shifts)


@jax.custom_vjp
def low(v):
    return lax.optimization_barrier(v.astype(jnp.bfloat16)).astype(jnp.float32)

@jax.custom_vjp
def low_back(v):
    return v

def low_keep(v):
    return (low(v), None)

def low_pass(kept, grad):
    return (grad,)

def back_keep(v):
    return (v, None)

def back_low(kept, grad):
    return (low(grad),)
low.defvjp(low_keep, low_pass)
low_back.defvjp(back_keep, back_low)
EPSILON = 1e-05
MASKED = -1e+30
PRECISE = lax.Precision.HIGHEST

def matmul(left_side, right_side):
    return jnp.dot(left_side, right_side, precision=PRECISE, preferred_element_type=jnp.float32)

def round_both(values):
    return low(low_back(values))

def layer_norm(values, gain_row, shift_row):
    centre = lax.optimization_barrier(jnp.mean(values, axis=-1, keepdims=True))
    centred = values - centre
    spread = lax.optimization_barrier(jnp.mean(centred * centred, axis=-1, keepdims=True))
    return centred * lax.rsqrt(spread + EPSILON) * gain_row + shift_row

def attend_row(queries, key_rows, value_rows, seg_row):
    length = queries.shape[0]
    block_len = min(512, length)
    head_count = queries.shape[1] // HEAD_DIM
    query_heads = queries.reshape(length, head_count, HEAD_DIM)
    key_heads = key_rows.reshape(length, head_count, HEAD_DIM)
    value_heads = value_rows.reshape(length, head_count, HEAD_DIM)
    position = jnp.arange(length, dtype=jnp.int32)

    def one_block(offset):
        query_part = lax.dynamic_slice_in_dim(query_heads, offset, block_len, 0)
        seg_part = lax.dynamic_slice_in_dim(seg_row, offset, block_len, 0)
        query_pos = offset + jnp.arange(block_len, dtype=jnp.int32)
        scores = jnp.einsum('qhd,khd->hqk', query_part, key_heads, precision=PRECISE) / math.sqrt(HEAD_DIM)
        scores = low_back(scores)
        allowed = (seg_part[:, None] == seg_row[None, :]) & (jnp.abs(query_pos[:, None] - position[None, :]) < WINDOW)
        scores = jnp.where(allowed[None], scores, MASKED)
        row_top = lax.optimization_barrier(jnp.max(scores, axis=-1, keepdims=True))
        raised = jnp.exp(scores - row_top)
        softened = low(raised / lax.optimization_barrier(jnp.sum(raised, axis=-1, keepdims=True)))
        mixed_heads = jnp.einsum('hqk,khd->qhd', softened, value_heads, precision=PRECISE)
        return mixed_heads.reshape(block_len, head_count * HEAD_DIM)
    offsets = (jnp.arange(length // block_len, dtype=jnp.int32) * block_len).astype(jnp.int32)
    blocks = lax.map(jax.checkpoint(one_block), offsets)
    return blocks.reshape(length, head_count * HEAD_DIM)

def layer_forward(param_set, input_rows, seg_rows, mask_rows, teacher_rows, loss_scale):
    w_query, w_key, w_value, w_out, b_query, b_value, w_up, b_up, w_down, ln_gains, ln_shifts = param_set
    row_count, length, features = input_rows.shape
    flat_rows = input_rows.reshape(row_count * length, features)
    queries = round_both(matmul(flat_rows, w_query) + b_query)
    key_all = round_both(matmul(flat_rows, w_key))
    value_all = round_both(matmul(flat_rows, w_value) + b_value)
    shaped = (row_count, length, features)
    mixed_heads = jax.vmap(attend_row)(queries.reshape(shaped), key_all.reshape(shaped), value_all.reshape(shaped), seg_rows)
    mixed_heads = round_both(mixed_heads.reshape(row_count * length, features))
    pre_first = flat_rows + low_back(matmul(mixed_heads, w_out)) + ln_shifts[2]
    normed_first = layer_norm(pre_first, ln_gains[0], ln_shifts[0])
    up_all = low_back(matmul(low(normed_first), w_up) + b_up)
    active = low(jax.nn.gelu(up_all, approximate=False))
    pre_second = normed_first + low_back(matmul(active, w_down)) + ln_shifts[3]
    result = layer_norm(pre_second, ln_gains[1], ln_shifts[1])
    differ = result - teacher_rows.reshape(row_count * length, features)
    weighted = mask_rows.reshape(row_count * length, 1).astype(jnp.float32) * differ * differ
    squares = jnp.sum(weighted)
    return (squares * loss_scale, (result.reshape(shaped), squares))

def reference(inputs, segment_ids, valid_mask, teacher, w_query, w_key, w_value, w_out, b_query, b_value, w_up, b_up, w_down, ln_gains, ln_shifts):
    params = tuple((member.astype(jnp.float32) for member in (w_query, w_key, w_value, w_out, b_query, b_value, w_up, b_up, w_down, ln_gains, ln_shifts)))
    valid_count = jnp.sum(valid_mask).astype(jnp.float32)
    loss_scale = TOKENS / (2.0 * valid_count)
    group_rows = math.gcd(ROWS, max(1, 4096 // LENGTH))
    group_count = ROWS // group_rows

    def regroup(source):
        return source.reshape((group_count, group_rows) + source.shape[1:])

    def one_group(state_pair, pieces):
        gradients, squares = state_pair
        inputs_group, seg_group, mask_group, teacher_group = pieces

        def objective(param_set, input_rows):
            return layer_forward(param_set, input_rows, seg_group, mask_group, teacher_group.astype(jnp.float32), loss_scale)
        scaled_loss, pullback, extras = jax.vjp(objective, params, inputs_group.astype(jnp.float32), has_aux=True)
        grad_params, grad_rows = pullback(jnp.ones_like(scaled_loss))
        gradients = jax.tree.map(jnp.add, gradients, grad_params)
        return ((gradients, squares + extras[1]), (extras[0].astype(jnp.bfloat16), grad_rows.astype(jnp.bfloat16)))
    start_pair = (tuple((jnp.zeros_like(member) for member in params)), jnp.zeros((), jnp.float32))
    (gradients, squares), (outputs, grad_inputs) = lax.scan(one_group, start_pair, (regroup(inputs), regroup(segment_ids), regroup(valid_mask), regroup(teacher)))
    loss_value = squares / (D * valid_count)
    full_shape = inputs.shape
    return (outputs.reshape(full_shape), loss_value, grad_inputs.reshape(full_shape), gradients[0], gradients[1], gradients[2], gradients[3], gradients[4], gradients[5], gradients[6], gradients[7], gradients[8], gradients[9], gradients[10])
```

```python
from functools import partial
import math

import jax
import jax.numpy as jnp
from jax import lax
from jax.experimental import pallas as pl
from jax.experimental.pallas import tpu as pltpu
from jax.sharding import PartitionSpec as P

HEAD_DIM = 64
WINDOW = 512


EPSILON = 1e-05
MASKED = -1e30


def layer_norm_parts(values, gain_row, shift_row):
    centre = jnp.mean(values, axis=-1, keepdims=True)
    centred = values - centre
    inverse = lax.rsqrt(jnp.mean(centred * centred, axis=-1, keepdims=True) + EPSILON)
    normed = centred * inverse
    return (normed * gain_row + shift_row, normed, inverse)


def norm_backward(normed, inverse, gain_row, grad_out):
    scaled = grad_out * gain_row
    return inverse * (
        scaled
        - jnp.mean(scaled, axis=-1, keepdims=True)
        - normed * jnp.mean(scaled * normed, axis=-1, keepdims=True)
    )


def dot_first(left_side, right_side):
    return lax.dot_general(
        left_side, right_side, (((0,), (0,)), ((), ())), preferred_element_type=jnp.float32
    )


def dot_last(left_side, right_side):
    return lax.dot_general(
        left_side, right_side, (((1,), (1,)), ((), ())), preferred_element_type=jnp.float32
    )


def own_rows(source, offset_own, piece_len):
    return lax.dynamic_slice_in_dim(source, offset_own, piece_len, 1)


def allowed_mask(seg_row, offset, block_len):
    length = seg_row.shape[0]
    position = jnp.arange(length, dtype=jnp.int32)
    query_pos = offset + jnp.arange(block_len, dtype=jnp.int32)
    same_doc = seg_row[offset : offset + block_len][:, None] == seg_row[None, :]
    return same_doc & (jnp.abs(query_pos[:, None] - position[None, :]) < WINDOW)


def block_scores(query_part, key_heads, allowed):
    scores = jnp.einsum(
        "qhd,khd->hqk", query_part, key_heads, preferred_element_type=jnp.float32
    ) / math.sqrt(HEAD_DIM)
    return jnp.where(allowed[None], scores, MASKED)


def attention_forward(queries, key_all, value_all, segment_ids):
    seq_count, length = (queries.shape[0], queries.shape[1])
    block_len = min(512, length)
    outputs, summaries = ([], [])
    for row_index in range(seq_count):
        row_out, row_lse = ([], [])
        for offset in range(0, length, block_len):
            allowed = allowed_mask(segment_ids[row_index], offset, block_len)
            scores = block_scores(
                queries[row_index, offset : offset + block_len], key_all[row_index], allowed
            )
            row_top = jnp.max(scores, axis=-1, keepdims=True)
            raised = jnp.exp(scores - row_top)
            norm_sum = jnp.sum(raised, axis=-1, keepdims=True)
            softened = (raised / norm_sum).astype(jnp.bfloat16)
            row_out.append(
                jnp.einsum(
                    "hqk,khd->qhd",
                    softened,
                    value_all[row_index],
                    preferred_element_type=jnp.float32,
                )
            )
            row_lse.append(row_top + jnp.log(norm_sum))
        outputs.append(jnp.concatenate(row_out, axis=0))
        summaries.append(jnp.concatenate(row_lse, axis=1))
    return (jnp.stack(outputs), jnp.stack(summaries))


def attention_backward(queries, key_all, value_all, segment_ids, summaries, grad_mixed):
    seq_count, length = (queries.shape[0], queries.shape[1])
    block_len = min(512, length)
    root_dim = math.sqrt(HEAD_DIM)
    query_rows, key_rows, value_rows = ([], [], [])
    for row_index in range(seq_count):
        key_grad = jnp.zeros(key_all.shape[1:], jnp.float32)
        value_grad = jnp.zeros(value_all.shape[1:], jnp.float32)
        query_parts = []
        for offset in range(0, length, block_len):
            allowed = allowed_mask(segment_ids[row_index], offset, block_len)
            query_part = queries[row_index, offset : offset + block_len]
            scores = block_scores(query_part, key_all[row_index], allowed)
            softened = jnp.exp(scores - summaries[row_index, :, offset : offset + block_len])
            grad_part = grad_mixed[row_index, offset : offset + block_len]
            value_grad = value_grad + jnp.einsum(
                "hqk,qhd->khd",
                softened.astype(jnp.bfloat16),
                grad_part,
                preferred_element_type=jnp.float32,
            )
            grad_soft = jnp.einsum(
                "qhd,khd->hqk", grad_part, value_all[row_index], preferred_element_type=jnp.float32
            )
            grad_score = (
                softened * (grad_soft - jnp.sum(softened * grad_soft, axis=-1, keepdims=True))
            ).astype(jnp.bfloat16)
            query_parts.append(
                jnp.einsum(
                    "hqk,khd->qhd",
                    grad_score,
                    key_all[row_index],
                    preferred_element_type=jnp.float32,
                )
                / root_dim
            )
            key_grad = (
                key_grad
                + jnp.einsum(
                    "hqk,qhd->khd", grad_score, query_part, preferred_element_type=jnp.float32
                )
                / root_dim
            )
        query_rows.append(jnp.concatenate(query_parts, axis=0))
        key_rows.append(key_grad)
        value_rows.append(value_grad)
    return (jnp.stack(query_rows), jnp.stack(key_rows), jnp.stack(value_rows))


def on_device_heads(
    inputs,
    segment_ids,
    valid_mask,
    teacher,
    w_query,
    w_key,
    w_value,
    w_out,
    b_query,
    b_value,
    w_up,
    b_up,
    w_down,
    ln_gains,
    ln_shifts,
):
    seq_count, piece_len, features = inputs.shape
    tp_count = lax.axis_size("tp")
    tp_rank = lax.axis_index("tp")
    length = piece_len * tp_count
    total_tokens = seq_count * length * lax.axis_size("fsdp")
    offset_own = tp_rank * piece_len
    (
        full_query,
        full_key,
        full_value,
        full_out,
        full_bquery,
        full_bvalue,
        full_up,
        full_bup,
        full_down,
        full_gains,
        full_shifts,
    ) = (
        lax.all_gather(w_query, "fsdp", axis=0, tiled=True),
        lax.all_gather(w_key, "fsdp", axis=0, tiled=True),
        lax.all_gather(w_value, "fsdp", axis=0, tiled=True),
        lax.all_gather(w_out, "fsdp", axis=1, tiled=True),
        lax.all_gather(b_query, "fsdp", axis=0, tiled=True),
        lax.all_gather(b_value, "fsdp", axis=0, tiled=True),
        lax.all_gather(w_up, "fsdp", axis=0, tiled=True),
        lax.all_gather(b_up, "fsdp", axis=0, tiled=True),
        lax.all_gather(w_down, "fsdp", axis=1, tiled=True),
        lax.all_gather(ln_gains, "fsdp", axis=1, tiled=True),
        lax.all_gather(ln_shifts, "fsdp", axis=1, tiled=True),
    )
    gains = full_gains.astype(jnp.float32)
    shifts = full_shifts.astype(jnp.float32)
    local_width = full_query.shape[1]
    head_local = local_width // HEAD_DIM
    token_count = seq_count * length
    token_full = lax.all_gather(inputs, "tp", axis=1, tiled=True)
    flat_in = token_full.reshape(token_count, features)
    query_flat = (
        jnp.dot(flat_in, full_query, preferred_element_type=jnp.float32)
        + full_bquery.astype(jnp.float32)
    ).astype(jnp.bfloat16)
    key_flat = jnp.dot(flat_in, full_key, preferred_element_type=jnp.float32).astype(jnp.bfloat16)
    value_flat = (
        jnp.dot(flat_in, full_value, preferred_element_type=jnp.float32)
        + full_bvalue.astype(jnp.float32)
    ).astype(jnp.bfloat16)
    head_shape = (seq_count, length, head_local, HEAD_DIM)
    query_heads = query_flat.reshape(head_shape)
    key_heads = key_flat.reshape(head_shape)
    value_heads = value_flat.reshape(head_shape)
    mixed_heads, summaries = attention_forward(query_heads, key_heads, value_heads, segment_ids)
    mixed_low = mixed_heads.reshape(token_count, local_width).astype(jnp.bfloat16)
    attend_part = jnp.dot(mixed_low, full_out, preferred_element_type=jnp.float32).reshape(
        seq_count, length, features
    )
    attend_all = lax.psum(attend_part.astype(jnp.bfloat16), "tp").astype(jnp.float32)
    pre_first = token_full.astype(jnp.float32) + attend_all + shifts[2]
    normed_first, unit_first, inverse_first = layer_norm_parts(pre_first, gains[0], shifts[0])
    hidden_full = normed_first.astype(jnp.bfloat16)
    normed_own = own_rows(normed_first, offset_own, piece_len)
    hidden_flat = hidden_full.reshape(token_count, features)
    up_all = jnp.dot(hidden_flat, full_up, preferred_element_type=jnp.float32) + full_bup.astype(
        jnp.float32
    )
    active = jax.nn.gelu(up_all, approximate=False).astype(jnp.bfloat16)
    down_part = jnp.dot(active, full_down, preferred_element_type=jnp.float32).reshape(
        seq_count, length, features
    )
    down_own = lax.psum_scatter(
        down_part.astype(jnp.bfloat16), "tp", scatter_dimension=1, tiled=True
    ).astype(jnp.float32)
    pre_second = normed_own + down_own + shifts[3]
    result, unit_second, inverse_second = layer_norm_parts(pre_second, gains[1], shifts[1])
    differ = result - teacher.astype(jnp.float32)
    mask_float = valid_mask.astype(jnp.float32)[..., None]
    squares, valid_count = lax.psum(
        (jnp.sum(mask_float * differ * differ), jnp.sum(mask_float)), ("fsdp", "tp")
    )
    loss_value = squares / (features * valid_count)
    grad_result = mask_float * differ * (total_tokens / valid_count)
    grad_second = norm_backward(unit_second, inverse_second, gains[1], grad_result)
    grad_down_full = lax.all_gather(grad_second.astype(jnp.bfloat16), "tp", axis=1, tiled=True)
    grad_down_flat = grad_down_full.reshape(token_count, features)
    weight_down = dot_first(active, grad_down_flat)
    grad_active = dot_last(grad_down_flat, full_down)
    gelu_back = jax.vjp(partial(jax.nn.gelu, approximate=False), up_all)[1]
    grad_up = gelu_back(grad_active)[0].astype(jnp.bfloat16)
    weight_up = dot_first(hidden_flat, grad_up)
    bias_up = jnp.sum(grad_up.astype(jnp.float32), axis=0)
    hidden_part = dot_last(grad_up, full_up).reshape(seq_count, length, features)
    current = own_rows(hidden_part, offset_own, piece_len)
    hidden_part = lax.dynamic_update_slice_in_dim(hidden_part, current + grad_second, offset_own, 1)
    grad_hidden_all = lax.psum(hidden_part.astype(jnp.bfloat16), "tp").astype(jnp.float32)
    grad_first_all = norm_backward(unit_first, inverse_first, gains[0], grad_hidden_all)
    grad_mix_full = grad_first_all.astype(jnp.bfloat16)
    grad_first_own = own_rows(grad_first_all, offset_own, piece_len)
    grad_hidden_own = own_rows(grad_hidden_all, offset_own, piece_len)
    unit_first_own = own_rows(unit_first, offset_own, piece_len)
    grad_mix_flat = grad_mix_full.reshape(token_count, features)
    weight_out = dot_first(mixed_low, grad_mix_flat)
    grad_mixed = dot_last(grad_mix_flat, full_out).astype(jnp.bfloat16).reshape(head_shape)
    grad_query, grad_key, grad_value = attention_backward(
        query_heads, key_heads, value_heads, segment_ids, summaries, grad_mixed
    )
    query_low = grad_query.astype(jnp.bfloat16).reshape(token_count, local_width)
    key_low = grad_key.astype(jnp.bfloat16).reshape(token_count, local_width)
    value_low = grad_value.astype(jnp.bfloat16).reshape(token_count, local_width)
    weight_query = dot_first(flat_in, query_low)
    weight_key = dot_first(flat_in, key_low)
    weight_value = dot_first(flat_in, value_low)
    bias_query = jnp.sum(query_low.astype(jnp.float32), axis=0)
    bias_value = jnp.sum(value_low.astype(jnp.float32), axis=0)
    input_part = (
        dot_last(query_low, full_query)
        + dot_last(key_low, full_key)
        + dot_last(value_low, full_value)
    )
    grad_inputs = (
        lax.psum_scatter(
            input_part.reshape(seq_count, length, features).astype(jnp.bfloat16),
            "tp",
            scatter_dimension=1,
            tiled=True,
        ).astype(jnp.float32)
        + grad_first_own
    )
    gain_part = jnp.stack(
        [
            jnp.sum(grad_hidden_own * unit_first_own, axis=(0, 1)),
            jnp.sum(grad_result * unit_second, axis=(0, 1)),
        ]
    )
    shift_part = jnp.stack(
        [
            jnp.sum(grad_hidden_own, axis=(0, 1)),
            jnp.sum(grad_result, axis=(0, 1)),
            jnp.sum(grad_first_own, axis=(0, 1)),
            jnp.sum(grad_second, axis=(0, 1)),
        ]
    )
    gain_sum, shift_sum = lax.psum((gain_part, shift_part), "tp")
    gradients = (
        lax.psum_scatter(
            weight_query.astype(jnp.bfloat16), "fsdp", scatter_dimension=0, tiled=True
        ).astype(jnp.float32),
        lax.psum_scatter(
            weight_key.astype(jnp.bfloat16), "fsdp", scatter_dimension=0, tiled=True
        ).astype(jnp.float32),
        lax.psum_scatter(
            weight_value.astype(jnp.bfloat16), "fsdp", scatter_dimension=0, tiled=True
        ).astype(jnp.float32),
        lax.psum_scatter(
            weight_out.astype(jnp.bfloat16), "fsdp", scatter_dimension=1, tiled=True
        ).astype(jnp.float32),
        lax.psum_scatter(
            bias_query.astype(jnp.bfloat16), "fsdp", scatter_dimension=0, tiled=True
        ).astype(jnp.float32),
        lax.psum_scatter(
            bias_value.astype(jnp.bfloat16), "fsdp", scatter_dimension=0, tiled=True
        ).astype(jnp.float32),
        lax.psum_scatter(
            weight_up.astype(jnp.bfloat16), "fsdp", scatter_dimension=0, tiled=True
        ).astype(jnp.float32),
        lax.psum_scatter(
            bias_up.astype(jnp.bfloat16), "fsdp", scatter_dimension=0, tiled=True
        ).astype(jnp.float32),
        lax.psum_scatter(
            weight_down.astype(jnp.bfloat16), "fsdp", scatter_dimension=1, tiled=True
        ).astype(jnp.float32),
        lax.psum_scatter(
            gain_sum.astype(jnp.bfloat16), "fsdp", scatter_dimension=1, tiled=True
        ).astype(jnp.float32),
        lax.psum_scatter(
            shift_sum.astype(jnp.bfloat16), "fsdp", scatter_dimension=1, tiled=True
        ).astype(jnp.float32),
    )
    return (
        result.astype(jnp.bfloat16),
        loss_value,
        grad_inputs.astype(jnp.bfloat16),
        gradients[0],
        gradients[1],
        gradients[2],
        gradients[3],
        gradients[4],
        gradients[5],
        gradients[6],
        gradients[7],
        gradients[8],
        gradients[9],
        gradients[10],
    )


BLOCK = 256
LOG2E = math.log2(math.e)
SHARD_ROWS_PARTS = 2


def rows_plan_fits(mesh):
    fsdp_count, tp_count = (mesh.shape["fsdp"], mesh.shape["tp"])
    return tp_count == 2 and fsdp_count >= 8 and fsdp_count & (fsdp_count - 1) == 0


def dot_plain(left_side, right_side):
    return lax.dot_general(
        left_side, right_side, (((1,), (0,)), ((), ())), preferred_element_type=jnp.float32
    )


def exchange(values, step):
    axis, bit = step
    count = lax.axis_size(axis)
    return lax.ppermute(values, axis, [(index, index ^ bit) for index in range(count)])


def step_orders():
    count = lax.axis_size("fsdp")
    across = ("tp", 1)
    core = ("fsdp", 1)
    side = ("fsdp", 2)
    far = [("fsdp", 1 << place) for place in range(2, count.bit_length() - 1)]
    far.reverse()
    first = tuple(far) + (across, side)
    second = (far[0], across, side) + tuple(far[1:])
    return core, (first, second)


def order_masks(order):
    masks = [(0, 0)]
    for axis, bit in order:
        fsdp_bit, tp_bit = (bit, 0) if axis == "fsdp" else (0, bit)
        masks = masks + [(high ^ fsdp_bit, low ^ tp_bit) for high, low in masks]
    return masks


def gather_part(shard, order, core):
    held = shard[None]
    for step in order[:-1]:
        held = jnp.concatenate([held, exchange(held, step)], axis=0)
    other = exchange(held, order[-1])
    return [held, other, exchange(held, core), exchange(other, core)]


def gather_masks(order, core):
    masks = order_masks(order)
    half = len(masks) // 2
    near = [masks[:half], masks[half:]]
    return near + [[(high ^ core[1], low) for high, low in group] for group in near]


def add_low(left_side, right_side):
    return (left_side.astype(jnp.float32) + right_side.astype(jnp.float32)).astype(jnp.bfloat16)


def scatter_part(kept, sent, order, core):
    received = exchange(sent, core)
    for step in order:
        half = kept.shape[0] // 2
        outgoing = add_low(kept[half:], received[half:])
        arrived = exchange(outgoing, step)
        kept, received = (add_low(kept[:half], received[:half]), arrived)
    return kept[0].astype(jnp.float32) + received[0].astype(jnp.float32)


def scatter_masks(order):
    return order_masks(tuple(reversed(order)))


def assemble_kernel(plan, place_ref, *refs):
    sources, targets, sem = (refs[: plan["sources"]], refs[plan["sources"] : -1], refs[-1])
    me_fsdp, me_tp = (place_ref[0], place_ref[1])
    rows = plan["rows"]
    copies = []
    for source, place, start, width, high, low, target, per_tp, column in plan["copies"]:
        row = pl.multiple_of((me_fsdp ^ high) * rows, rows)
        lane = pl.multiple_of((me_tp ^ low) * per_tp + column, 128)
        full = (target, pl.ds(row, rows), pl.ds(lane, width))
        piece = (source, place, slice(None), pl.ds(start, width))
        if plan["gather"]:
            from_ref = sources[piece[0]].at[piece[1], :, piece[3]]
            to_ref = targets[full[0]].at[full[1], full[2]]
        else:
            from_ref = sources[full[0]].at[full[1], full[2]]
            to_ref = targets[piece[0]].at[piece[1], :, piece[3]]
        copy = pltpu.make_async_copy(from_ref, to_ref, sem)
        copy.start()
        copies.append(copy)
    for copy in copies:
        copy.wait()


def run_assemble(plan, place, sources, out_shapes, name):
    any_spec = pl.BlockSpec(memory_space=pl.ANY)
    moved = sum(math.prod(out.shape) * 2 for out in out_shapes)
    return pl.pallas_call(
        partial(assemble_kernel, plan),
        in_specs=[pl.BlockSpec(memory_space=pltpu.SMEM)] + [any_spec] * len(sources),
        out_specs=[any_spec] * len(out_shapes),
        out_shape=out_shapes,
        scratch_shapes=[pltpu.SemaphoreType.DMA],
        cost_estimate=pl.CostEstimate(flops=0, bytes_accessed=2 * moved, transcendentals=0),
        name=name,
    )(place, *sources)


def gather_group(shard, place, columns, widths, name):
    core, orders = step_orders()
    rows, width = shard.shape
    part_width = width // 2
    sources, copies = ([], [])
    for part, order in enumerate(orders):
        pieces = gather_part(shard[:, part * part_width : (part + 1) * part_width], order, core)
        for piece, masks in zip(pieces, gather_masks(order, core)):
            for place_at, (high, low) in enumerate(masks):
                for start, span_width, target, per_tp, column in columns[part]:
                    copies.append(
                        (len(sources), place_at, start, span_width, high, low, target, per_tp, column)
                    )
            sources.append(piece)
    plan = dict(gather=True, sources=len(sources), rows=rows, copies=copies)
    full_rows = rows * lax.axis_size("fsdp")
    shapes = [jax.ShapeDtypeStruct((full_rows, span), jnp.bfloat16) for span in widths]
    return run_assemble(plan, place, sources, shapes, name)


def scatter_group(fulls, place, columns, rows, part_width, name):
    core, orders = step_orders()
    copies, shapes = ([], [])
    for part, order in enumerate(orders):
        masks = scatter_masks(order)
        for flip in (0, core[1]):
            for place_at, (high, low) in enumerate(masks):
                for start, span_width, target, per_tp, column in columns[part]:
                    copies.append(
                        (len(shapes), place_at, start, span_width, high ^ flip, low, target, per_tp, column)
                    )
            shapes.append(jax.ShapeDtypeStruct((len(masks), rows, part_width), jnp.bfloat16))
    plan = dict(gather=False, sources=len(fulls), rows=rows, copies=copies)
    pieces = run_assemble(plan, place, fulls, shapes, name)
    parts = [
        scatter_part(pieces[2 * part], pieces[2 * part + 1], order, core)
        for part, order in enumerate(orders)
    ]
    return jnp.concatenate(parts, axis=1)


def bit_steps():
    steps = []
    for axis in ("fsdp", "tp"):
        for place in range(lax.axis_size(axis).bit_length() - 1):
            steps.append((axis, 1 << place))
    return steps


def gather_small(values):
    for step in bit_steps():
        mine = (lax.axis_index(step[0]) & step[1]) != 0
        arrived = exchange(values, step)
        values = jnp.concatenate(
            [jnp.where(mine, arrived, values), jnp.where(mine, values, arrived)], axis=0
        )
    return values


def scatter_small(values):
    for step in reversed(bit_steps()):
        mine = (lax.axis_index(step[0]) & step[1]) != 0
        half = values.shape[0] // 2
        low, high = (values[:half], values[half:])
        values = jnp.where(mine, high, low) + exchange(jnp.where(mine, low, high), step)
    return values[0]


def block_span(block, count):
    reach = -(-WINDOW // BLOCK)
    return max(0, block - reach), min(count - 1, block + reach)


def split_three(values):
    high = values.astype(jnp.bfloat16)
    rest = values - high.astype(jnp.float32)
    mid = rest.astype(jnp.bfloat16)
    low = (rest - mid.astype(jnp.float32)).astype(jnp.bfloat16)
    return high, mid, low


def window_edge(tile, row_block, column_block):
    if (abs(row_block - column_block) + 1) * BLOCK - 1 < WINDOW:
        return tile
    row = lax.broadcasted_iota(jnp.int32, tile.shape, 0) + row_block * BLOCK
    column = lax.broadcasted_iota(jnp.int32, tile.shape, 1) + column_block * BLOCK
    return jnp.where(jnp.abs(row - column) < WINDOW, tile, MASKED)


def attend_kernel(seg_ref, q_ref, k_ref, v_ref, out_ref, qx_ref, kx_ref, held_ref):
    length = q_ref.shape[0]
    count = length // BLOCK
    lane = lax.broadcasted_iota(jnp.int32, (length, 128), 1)
    seg = seg_ref[...]
    q_heads, k_heads, v_heads = ([], [], [])
    for head in range(2):
        own = (lane < 64) if head == 0 else (lane >= 64)
        extra = lane - 64 if head == 0 else lane
        same = extra == seg
        q_extra = jnp.where(same, 1.0, 0.0).astype(jnp.bfloat16)
        k_extra = jnp.where(
            extra < 4, jnp.where(same, 0.0, MASKED), jnp.where(extra < 7, -1.0, 0.0)
        ).astype(jnp.bfloat16)
        v_extra = jnp.where(extra == 0, 1.0, 0.0).astype(jnp.bfloat16)
        q_heads.append(jnp.where(own, q_ref[...], q_extra))
        k_heads.append(jnp.where(own, k_ref[...], k_extra))
        v_heads.append(jnp.where(own, v_ref[...], v_extra))
        kx_ref[head] = k_heads[head]
    units = [(head, block) for head in range(2) for block in range(count)]

    def score(unit):
        head, block = unit
        low, high = block_span(block, count)
        rows = slice(block * BLOCK, (block + 1) * BLOCK)
        tile = dot_last(q_heads[head][rows], k_heads[head][low * BLOCK : (high + 1) * BLOCK])
        return [
            window_edge(tile[:, (at - low) * BLOCK : (at - low + 1) * BLOCK], block, at)
            for at in range(low, high + 1)
        ]

    def finish(unit, tiles):
        head, block = unit
        low, high = block_span(block, count)
        rows = slice(block * BLOCK, (block + 1) * BLOCK)
        most = tiles[0]
        for tile in tiles[1:]:
            most = jnp.maximum(most, tile)
        top = jnp.max(most, axis=1, keepdims=True)
        raised = jnp.concatenate(
            [jnp.exp2(tile - top).astype(jnp.bfloat16) for tile in tiles], axis=1
        )
        mixed = dot_plain(raised, v_heads[head][low * BLOCK : (high + 1) * BLOCK])
        norm_sum = mixed[:, 64:65] if head == 0 else mixed[:, 0:1]
        held_ref[head, rows, :] = mixed * (1.0 / norm_sum)
        first, second, third = split_three(top + jnp.log2(norm_sum))
        extra = lane[:BLOCK] - 64 if head == 0 else lane[:BLOCK]
        qx_ref[head, rows, :] = jnp.where(
            extra == 4,
            first,
            jnp.where(extra == 5, second, jnp.where(extra == 6, third, q_heads[head][rows])),
        )

    tiles = score(units[0])
    for at, unit in enumerate(units):
        following = score(units[at + 1]) if at + 1 < len(units) else None
        finish(unit, tiles)
        tiles = following
    out_ref[...] = jnp.where(lane < 64, held_ref[0], held_ref[1]).astype(jnp.bfloat16)


def attend(queries, keys, values, seg):
    length, width = queries.shape
    heads = width // HEAD_DIM
    pair = pl.BlockSpec((length, 128), lambda step: (0, step))
    padded = pl.BlockSpec((2, length, 128), lambda step: (step, 0, 0))
    return pl.pallas_call(
        attend_kernel,
        grid=(heads // 2,),
        in_specs=[pl.BlockSpec((length, 1), lambda step: (0, 0)), pair, pair, pair],
        out_specs=[pair, padded, padded],
        out_shape=[
            jax.ShapeDtypeStruct((length, width), jnp.bfloat16),
            jax.ShapeDtypeStruct((heads, length, 128), jnp.bfloat16),
            jax.ShapeDtypeStruct((heads, length, 128), jnp.bfloat16),
        ],
        scratch_shapes=[pltpu.VMEM((2, length, 128), jnp.float32)],
        compiler_params=pltpu.CompilerParams(vmem_limit_bytes=40 << 20),
        cost_estimate=pl.CostEstimate(
            flops=28 * 10**9, bytes_accessed=16 << 20, transcendentals=heads * length * length
        ),
        name="attend",
    )(seg, queries, keys, values)


def attend_back_kernel(qx_ref, kx_ref, v_ref, out_ref, grad_ref, dq_ref, dk_ref, dv_ref, held_ref):
    length = v_ref.shape[0]
    count = length // BLOCK
    lane = lax.broadcasted_iota(jnp.int32, (length, 128), 1)
    grad = grad_ref[...]
    for head in range(2):
        mine = slice(head * 64, (head + 1) * 64)
        own = (lane < 64) if head == 0 else (lane >= 64)
        extra = lane - 64 if head == 0 else lane
        product = jnp.where(
            own, grad.astype(jnp.float32) * out_ref[...].astype(jnp.float32), 0.0
        )
        first, second, third = split_three(-jnp.sum(product, axis=1, keepdims=True))
        grad_head = jnp.where(
            own,
            grad,
            jnp.where(
                extra == 0,
                first,
                jnp.where(extra == 1, second, jnp.where(extra == 2, third, jnp.zeros_like(grad))),
            ),
        )
        v_head = jnp.where(own, v_ref[...], jnp.where(extra < 3, 1.0, 0.0).astype(jnp.bfloat16))
        q_head, k_head = (qx_ref[head], kx_ref[head])
        k_turned = k_head.T[mine]
        for block in range(count):
            low, high = block_span(block, count)
            keys = slice(block * BLOCK, (block + 1) * BLOCK)
            span = slice(low * BLOCK, (high + 1) * BLOCK)
            tile = dot_last(k_head[keys], q_head[span])
            soft = jnp.concatenate(
                [
                    jnp.exp2(
                        window_edge(tile[:, (at - low) * BLOCK : (at - low + 1) * BLOCK], block, at)
                    )
                    for at in range(low, high + 1)
                ],
                axis=1,
            )
            grad_soft = dot_last(v_head[keys], grad_head[span])
            grad_score = (soft * grad_soft).astype(jnp.bfloat16)
            grad_value = dot_plain(soft.astype(jnp.bfloat16), grad_head[span])
            grad_key = dot_plain(grad_score, q_head[span]) * (1.0 / LOG2E)
            dv_ref[keys, mine] = grad_value[:, mine].astype(jnp.bfloat16)
            dk_ref[keys, mine] = grad_key[:, mine].astype(jnp.bfloat16)
            grad_query = dot_plain(k_turned[:, keys], grad_score)
            if block == 0:
                held_ref[mine, span] = grad_query
                if high + 1 < count:
                    held_ref[mine, (high + 1) * BLOCK :] = jnp.zeros(
                        (64, length - (high + 1) * BLOCK), jnp.float32
                    )
            else:
                held_ref[mine, span] += grad_query
    dq_ref[...] = (held_ref[...] * (1.0 / math.sqrt(HEAD_DIM))).T.astype(jnp.bfloat16)


def attend_back(q_padded, k_padded, values, mixed, grad_mixed):
    length, width = values.shape
    heads = width // HEAD_DIM
    pair = pl.BlockSpec((length, 128), lambda step: (0, step))
    padded = pl.BlockSpec((2, length, 128), lambda step: (step, 0, 0))
    return pl.pallas_call(
        attend_back_kernel,
        grid=(heads // 2,),
        in_specs=[padded, padded, pair, pair, pair],
        out_specs=[pair, pair, pair],
        out_shape=[jax.ShapeDtypeStruct((length, width), jnp.bfloat16)] * 3,
        scratch_shapes=[pltpu.VMEM((128, length), jnp.float32)],
        compiler_params=pltpu.CompilerParams(vmem_limit_bytes=40 << 20),
        cost_estimate=pl.CostEstimate(
            flops=40 * 10**9, bytes_accessed=20 << 20, transcendentals=heads * length * length
        ),
        name="attend_back",
    )(q_padded, k_padded, values, mixed, grad_mixed)


def up_kernel(x_ref, w_ref, b_ref, active_ref, slope_ref):
    length = x_ref.shape[0]
    count = length // BLOCK

    def product(block):
        rows = slice(block * BLOCK, (block + 1) * BLOCK)
        return dot_plain(x_ref[rows], w_ref[...]) + b_ref[...]

    up = product(0)
    for block in range(count):
        following = product(block + 1) if block + 1 < count else None
        rows = slice(block * BLOCK, (block + 1) * BLOCK)
        cumulative = 0.5 * (1.0 + lax.erf(up * math.sqrt(0.5)))
        density = jnp.exp2(up * up * (-0.5 * LOG2E)) * (1.0 / math.sqrt(2.0 * math.pi))
        active_ref[rows] = (up * cumulative).astype(jnp.bfloat16)
        slope_ref[rows] = (cumulative + up * density).astype(jnp.bfloat16)
        up = following


def up_project(hidden, weight, bias):
    length, features = hidden.shape
    width = weight.shape[1]
    block_width = math.gcd(width, 512)
    column = pl.BlockSpec((length, block_width), lambda step: (0, step))
    return pl.pallas_call(
        up_kernel,
        grid=(width // block_width,),
        in_specs=[
            pl.BlockSpec((length, features), lambda step: (0, 0)),
            pl.BlockSpec((features, block_width), lambda step: (0, step)),
            pl.BlockSpec((1, block_width), lambda step: (0, step)),
        ],
        out_specs=[column, column],
        out_shape=[jax.ShapeDtypeStruct((length, width), jnp.bfloat16)] * 2,
        compiler_params=pltpu.CompilerParams(vmem_limit_bytes=40 << 20),
        cost_estimate=pl.CostEstimate(
            flops=2 * length * features * width,
            bytes_accessed=2 * (length * features + features * width + 2 * length * width),
            transcendentals=2 * length * width,
        ),
        name="up_project",
    )(hidden, weight, bias)


def own_first(row_values, tp_rank, piece_len):
    mine = lax.dynamic_slice_in_dim(row_values, tp_rank * piece_len, piece_len, 0)
    theirs = lax.dynamic_slice_in_dim(row_values, (1 - tp_rank) * piece_len, piece_len, 0)
    return mine, theirs


def swap_in(pieces, tp_rank):
    mine = lax.dynamic_index_in_dim(pieces, tp_rank, 0, keepdims=False)
    theirs = lax.dynamic_index_in_dim(pieces, 1 - tp_rank, 0, keepdims=False)
    arrived = exchange(theirs, ("tp", 1))
    first = tp_rank == 0
    return jnp.concatenate(
        [jnp.where(first, mine, arrived), jnp.where(first, arrived, mine)], axis=0
    )


def swap_out(row_values, tp_rank, piece_len):
    mine, theirs = own_first(row_values, tp_rank, piece_len)
    arrived = exchange(theirs, ("tp", 1))
    first = tp_rank == 0
    return jnp.stack([jnp.where(first, mine, arrived), jnp.where(first, arrived, mine)])


def on_device_rows(
    inputs,
    segment_ids,
    valid_mask,
    teacher,
    w_query,
    w_key,
    w_value,
    w_out,
    b_query,
    b_value,
    w_up,
    b_up,
    w_down,
    ln_gains,
    ln_shifts,
):
    seq_count, piece_len, features = inputs.shape
    fsdp_count, tp_count = (lax.axis_size("fsdp"), lax.axis_size("tp"))
    fsdp_rank, tp_rank = (lax.axis_index("fsdp"), lax.axis_index("tp"))
    assert seq_count == tp_count
    total_tokens = seq_count * piece_len * tp_count * fsdp_count
    shard_rows, local_width = w_query.shape
    local_hidden = w_up.shape[1]
    width, hidden_units = (local_width * tp_count, local_hidden * tp_count)
    place = jnp.stack([fsdp_rank, tp_rank]).astype(jnp.int32)

    row_low = swap_in(inputs, tp_rank)
    seg = lax.dynamic_index_in_dim(segment_ids, tp_rank, 0, keepdims=False)[:, None]

    half = local_width
    attend_shard = jnp.concatenate([w_query, w_key, w_value, w_out.T], axis=1)
    attend_columns = [
        [(0, half, 0, half, 0), (half, half, 0, half, width)],
        [(0, half, 0, half, 2 * width), (half, half, 1, half, 0)],
    ]
    full_qkv, full_out = gather_group(
        attend_shard, place, attend_columns, [3 * width, width], "gather_attend"
    )
    part_width = local_hidden // 2
    wide_columns = [
        [(0, part_width, 0, local_hidden, part * part_width)] for part in range(2)
    ]
    (full_up,) = gather_group(w_up, place, wide_columns, [hidden_units], "gather_up")
    (full_down,) = gather_group(w_down.T, place, wide_columns, [hidden_units], "gather_down")

    valid_row = swap_in(valid_mask[..., None], tp_rank).astype(jnp.float32)
    small = jnp.concatenate(
        [
            b_query.astype(jnp.float32),
            b_value.astype(jnp.float32),
            b_up.astype(jnp.float32),
            ln_gains.astype(jnp.float32).reshape(-1),
            ln_shifts.astype(jnp.float32).reshape(-1),
            jnp.sum(valid_mask.astype(jnp.float32))[None],
        ]
    )
    small_len = small.shape[0]
    padded_len = -(-small_len // 128) * 128
    small = jnp.pad(small, (0, padded_len - small_len)).reshape(1, padded_len // 128, 128)
    small_all = gather_small(small).reshape(tp_count * fsdp_count, padded_len)
    cuts = []
    at = 0
    for count in (b_query.size, b_value.size, b_up.size, ln_gains.size, ln_shifts.size, 1):
        cuts.append(small_all[:, at : at + count])
        at += count
    bias_query, bias_value, bias_up = (cuts[0].reshape(-1), cuts[1].reshape(-1), cuts[2].reshape(-1))

    def feature_rows(columns, rows):
        return (
            columns[:fsdp_count]
            .reshape(fsdp_count, rows, features // fsdp_count)
            .transpose(1, 0, 2)
            .reshape(rows, features)
        )

    gains = feature_rows(cuts[3], 2)
    shifts = feature_rows(cuts[4], 4)
    valid_count = jnp.sum(cuts[5])
    teacher_row = swap_in(teacher, tp_rank).astype(jnp.float32)

    scale = LOG2E / math.sqrt(HEAD_DIM)
    queries = (
        (dot_plain(row_low, full_qkv[:, :width]) + bias_query) * scale
    ).astype(jnp.bfloat16)
    keys = dot_plain(row_low, full_qkv[:, width : 2 * width]).astype(jnp.bfloat16)
    values = (dot_plain(row_low, full_qkv[:, 2 * width :]) + bias_value).astype(jnp.bfloat16)
    mixed, q_padded, k_padded = attend(queries, keys, values, seg)
    pre_first = row_low.astype(jnp.float32) + dot_last(mixed, full_out) + shifts[2]
    normed_first, unit_first, inverse_first = layer_norm_parts(pre_first, gains[0], shifts[0])
    hidden_low = normed_first.astype(jnp.bfloat16)
    active, slope = up_project(hidden_low, full_up, bias_up[None])
    pre_second = normed_first + dot_last(active, full_down) + shifts[3]
    result, unit_second, inverse_second = layer_norm_parts(pre_second, gains[1], shifts[1])
    hidden_out = swap_out(result.astype(jnp.bfloat16), tp_rank, piece_len)

    differ = result - teacher_row
    grad_result = valid_row * differ * (total_tokens / valid_count)
    squares = jnp.sum(valid_row * differ * differ)
    grad_second = norm_backward(unit_second, inverse_second, gains[1], grad_result)
    grad_down = grad_second.astype(jnp.bfloat16)
    weight_down = dot_first(grad_down, active).astype(jnp.bfloat16)
    grad_w_down = scatter_group(
        [weight_down], place, wide_columns, shard_rows, part_width, "scatter_down"
    ).T
    grad_up = (dot_plain(grad_down, full_down) * slope.astype(jnp.float32)).astype(jnp.bfloat16)
    grad_b_up = jnp.sum(grad_up.astype(jnp.float32), axis=0)
    weight_up = dot_first(hidden_low, grad_up).astype(jnp.bfloat16)
    grad_w_up = scatter_group(
        [weight_up], place, wide_columns, shard_rows, part_width, "scatter_up"
    )
    grad_hidden = grad_second + dot_last(grad_up, full_up)
    grad_first = norm_backward(unit_first, inverse_first, gains[0], grad_hidden)
    grad_attend = grad_first.astype(jnp.bfloat16)
    weight_out = dot_first(grad_attend, mixed).astype(jnp.bfloat16)
    grad_mixed = dot_plain(grad_attend, full_out).astype(jnp.bfloat16)
    grad_query, grad_key, grad_value = attend_back(q_padded, k_padded, values, mixed, grad_mixed)
    grad_row = (
        grad_first
        + dot_last(grad_query, full_qkv[:, :width])
        + dot_last(grad_key, full_qkv[:, width : 2 * width])
        + dot_last(grad_value, full_qkv[:, 2 * width :])
    ).astype(jnp.bfloat16)
    grad_inputs = swap_out(grad_row, tp_rank, piece_len)
    weight_qkv = [
        dot_first(row_low, part).astype(jnp.bfloat16) for part in (grad_query, grad_key, grad_value)
    ]
    split_columns = [
        [(0, half, 0, half, 0), (half, half, 1, half, 0)],
        [(0, half, 2, half, 0), (half, half, 3, half, 0)],
    ]
    grad_attend_shard = scatter_group(
        weight_qkv + [weight_out], place, split_columns, shard_rows, 2 * half, "scatter_attend"
    )
    grad_w_query, grad_w_key, grad_w_value, grad_w_out = [
        grad_attend_shard[:, at * half : (at + 1) * half] for at in range(4)
    ]

    def feature_pieces(rows):
        pieces = rows.reshape(rows.shape[0], fsdp_count, -1).transpose(1, 0, 2).reshape(fsdp_count, -1)
        return jnp.concatenate([pieces] * tp_count, axis=0)

    devices = tp_count * fsdp_count
    pieces = jnp.concatenate(
        [
            jnp.sum(grad_query.astype(jnp.float32), axis=0).reshape(devices, -1),
            jnp.sum(grad_value.astype(jnp.float32), axis=0).reshape(devices, -1),
            grad_b_up.reshape(devices, -1),
            feature_pieces(
                jnp.stack(
                    [
                        jnp.sum(grad_hidden * unit_first, axis=0),
                        jnp.sum(grad_result * unit_second, axis=0),
                    ]
                )
            ),
            feature_pieces(
                jnp.stack(
                    [
                        jnp.sum(grad_hidden, axis=0),
                        jnp.sum(grad_result, axis=0),
                        jnp.sum(grad_first, axis=0),
                        jnp.sum(grad_second, axis=0),
                    ]
                )
            ),
            jnp.full((devices, 1), squares),
        ],
        axis=1,
    )
    pieces = jnp.pad(pieces, ((0, 0), (0, padded_len - small_len)))
    own = scatter_small(pieces.reshape(devices, padded_len // 128, 128)).reshape(padded_len)
    results = []
    at = 0
    for count in (b_query.size, b_value.size, b_up.size, ln_gains.size, ln_shifts.size, 1):
        results.append(own[at : at + count])
        at += count
    loss_value = results[5][0] / (features * valid_count)
    return (
        hidden_out,
        loss_value,
        grad_inputs,
        grad_w_query,
        grad_w_key,
        grad_w_value,
        grad_w_out.T,
        results[0],
        results[1],
        grad_w_up,
        results[2],
        grad_w_down,
        results[3].reshape(ln_gains.shape),
        results[4].reshape(ln_shifts.shape),
    )


def solution(mesh):
    in_specs = (
        P("fsdp", "tp", None),
        P("fsdp", None),
        P("fsdp", "tp"),
        P("fsdp", "tp", None),
        P("fsdp", "tp"),
        P("fsdp", "tp"),
        P("fsdp", "tp"),
        P("tp", "fsdp"),
        P(("tp", "fsdp")),
        P(("tp", "fsdp")),
        P("fsdp", "tp"),
        P(("tp", "fsdp")),
        P("tp", "fsdp"),
        P(None, "fsdp"),
        P(None, "fsdp"),
    )
    out_specs = (
        P("fsdp", "tp", None),
        P(),
        P("fsdp", "tp", None),
        P("fsdp", "tp"),
        P("fsdp", "tp"),
        P("fsdp", "tp"),
        P("tp", "fsdp"),
        P(("tp", "fsdp")),
        P(("tp", "fsdp")),
        P("fsdp", "tp"),
        P(("tp", "fsdp")),
        P("tp", "fsdp"),
        P(None, "fsdp"),
        P(None, "fsdp"),
    )
    rows_plan = rows_plan_fits(mesh)
    return jax.shard_map(
        on_device_rows if rows_plan else on_device_heads, mesh=mesh, in_specs=in_specs, out_specs=out_specs, check_vma=False
    )
```

```python
from functools import partial
import math

import jax
import jax.numpy as jnp
from jax import lax
from jax.experimental import pallas as pl
from jax.experimental.pallas import tpu as pltpu
from jax.sharding import PartitionSpec as P

HEAD_DIM = 64
WINDOW = 512


EPSILON = 1e-05
MASKED = -1e30


def layer_norm_parts(values, gain_row, shift_row):
    centre = jnp.mean(values, axis=-1, keepdims=True)
    centred = values - centre
    inverse = lax.rsqrt(jnp.mean(centred * centred, axis=-1, keepdims=True) + EPSILON)
    normed = centred * inverse
    return (normed * gain_row + shift_row, normed, inverse)


def norm_backward(normed, inverse, gain_row, grad_out):
    scaled = grad_out * gain_row
    return inverse * (
        scaled
        - jnp.mean(scaled, axis=-1, keepdims=True)
        - normed * jnp.mean(scaled * normed, axis=-1, keepdims=True)
    )


def dot_first(left_side, right_side):
    return lax.dot_general(
        left_side, right_side, (((0,), (0,)), ((), ())), preferred_element_type=jnp.float32
    )


def dot_last(left_side, right_side):
    return lax.dot_general(
        left_side, right_side, (((1,), (1,)), ((), ())), preferred_element_type=jnp.float32
    )


def own_rows(source, offset_own, piece_len):
    return lax.dynamic_slice_in_dim(source, offset_own, piece_len, 1)


def allowed_mask(seg_row, offset, block_len):
    length = seg_row.shape[0]
    position = jnp.arange(length, dtype=jnp.int32)
    query_pos = offset + jnp.arange(block_len, dtype=jnp.int32)
    same_doc = seg_row[offset : offset + block_len][:, None] == seg_row[None, :]
    return same_doc & (jnp.abs(query_pos[:, None] - position[None, :]) < WINDOW)


def block_scores(query_part, key_heads, allowed):
    scores = jnp.einsum(
        "qhd,khd->hqk", query_part, key_heads, preferred_element_type=jnp.float32
    ) / math.sqrt(HEAD_DIM)
    return jnp.where(allowed[None], scores, MASKED)


def attention_forward(queries, key_all, value_all, segment_ids):
    seq_count, length = (queries.shape[0], queries.shape[1])
    block_len = min(512, length)
    outputs, summaries = ([], [])
    for row_index in range(seq_count):
        row_out, row_lse = ([], [])
        for offset in range(0, length, block_len):
            allowed = allowed_mask(segment_ids[row_index], offset, block_len)
            scores = block_scores(
                queries[row_index, offset : offset + block_len], key_all[row_index], allowed
            )
            row_top = jnp.max(scores, axis=-1, keepdims=True)
            raised = jnp.exp(scores - row_top)
            norm_sum = jnp.sum(raised, axis=-1, keepdims=True)
            softened = (raised / norm_sum).astype(jnp.bfloat16)
            row_out.append(
                jnp.einsum(
                    "hqk,khd->qhd",
                    softened,
                    value_all[row_index],
                    preferred_element_type=jnp.float32,
                )
            )
            row_lse.append(row_top + jnp.log(norm_sum))
        outputs.append(jnp.concatenate(row_out, axis=0))
        summaries.append(jnp.concatenate(row_lse, axis=1))
    return (jnp.stack(outputs), jnp.stack(summaries))


def attention_backward(queries, key_all, value_all, segment_ids, summaries, grad_mixed):
    seq_count, length = (queries.shape[0], queries.shape[1])
    block_len = min(512, length)
    root_dim = math.sqrt(HEAD_DIM)
    query_rows, key_rows, value_rows = ([], [], [])
    for row_index in range(seq_count):
        key_grad = jnp.zeros(key_all.shape[1:], jnp.float32)
        value_grad = jnp.zeros(value_all.shape[1:], jnp.float32)
        query_parts = []
        for offset in range(0, length, block_len):
            allowed = allowed_mask(segment_ids[row_index], offset, block_len)
            query_part = queries[row_index, offset : offset + block_len]
            scores = block_scores(query_part, key_all[row_index], allowed)
            softened = jnp.exp(scores - summaries[row_index, :, offset : offset + block_len])
            grad_part = grad_mixed[row_index, offset : offset + block_len]
            value_grad = value_grad + jnp.einsum(
                "hqk,qhd->khd",
                softened.astype(jnp.bfloat16),
                grad_part,
                preferred_element_type=jnp.float32,
            )
            grad_soft = jnp.einsum(
                "qhd,khd->hqk", grad_part, value_all[row_index], preferred_element_type=jnp.float32
            )
            grad_score = (
                softened * (grad_soft - jnp.sum(softened * grad_soft, axis=-1, keepdims=True))
            ).astype(jnp.bfloat16)
            query_parts.append(
                jnp.einsum(
                    "hqk,khd->qhd",
                    grad_score,
                    key_all[row_index],
                    preferred_element_type=jnp.float32,
                )
                / root_dim
            )
            key_grad = (
                key_grad
                + jnp.einsum(
                    "hqk,qhd->khd", grad_score, query_part, preferred_element_type=jnp.float32
                )
                / root_dim
            )
        query_rows.append(jnp.concatenate(query_parts, axis=0))
        key_rows.append(key_grad)
        value_rows.append(value_grad)
    return (jnp.stack(query_rows), jnp.stack(key_rows), jnp.stack(value_rows))


def on_device_heads(
    inputs,
    segment_ids,
    valid_mask,
    teacher,
    w_query,
    w_key,
    w_value,
    w_out,
    b_query,
    b_value,
    w_up,
    b_up,
    w_down,
    ln_gains,
    ln_shifts,
):
    seq_count, piece_len, features = inputs.shape
    tp_count = lax.axis_size("tp")
    tp_rank = lax.axis_index("tp")
    length = piece_len * tp_count
    total_tokens = seq_count * length * lax.axis_size("fsdp")
    offset_own = tp_rank * piece_len
    (
        full_query,
        full_key,
        full_value,
        full_out,
        full_bquery,
        full_bvalue,
        full_up,
        full_bup,
        full_down,
        full_gains,
        full_shifts,
    ) = (
        lax.all_gather(w_query, "fsdp", axis=0, tiled=True),
        lax.all_gather(w_key, "fsdp", axis=0, tiled=True),
        lax.all_gather(w_value, "fsdp", axis=0, tiled=True),
        lax.all_gather(w_out, "fsdp", axis=1, tiled=True),
        lax.all_gather(b_query, "fsdp", axis=0, tiled=True),
        lax.all_gather(b_value, "fsdp", axis=0, tiled=True),
        lax.all_gather(w_up, "fsdp", axis=0, tiled=True),
        lax.all_gather(b_up, "fsdp", axis=0, tiled=True),
        lax.all_gather(w_down, "fsdp", axis=1, tiled=True),
        lax.all_gather(ln_gains, "fsdp", axis=1, tiled=True),
        lax.all_gather(ln_shifts, "fsdp", axis=1, tiled=True),
    )
    gains = full_gains.astype(jnp.float32)
    shifts = full_shifts.astype(jnp.float32)
    local_width = full_query.shape[1]
    head_local = local_width // HEAD_DIM
    token_count = seq_count * length
    token_full = lax.all_gather(inputs, "tp", axis=1, tiled=True)
    flat_in = token_full.reshape(token_count, features)
    query_flat = (
        jnp.dot(flat_in, full_query, preferred_element_type=jnp.float32)
        + full_bquery.astype(jnp.float32)
    ).astype(jnp.bfloat16)
    key_flat = jnp.dot(flat_in, full_key, preferred_element_type=jnp.float32).astype(jnp.bfloat16)
    value_flat = (
        jnp.dot(flat_in, full_value, preferred_element_type=jnp.float32)
        + full_bvalue.astype(jnp.float32)
    ).astype(jnp.bfloat16)
    head_shape = (seq_count, length, head_local, HEAD_DIM)
    query_heads = query_flat.reshape(head_shape)
    key_heads = key_flat.reshape(head_shape)
    value_heads = value_flat.reshape(head_shape)
    mixed_heads, summaries = attention_forward(query_heads, key_heads, value_heads, segment_ids)
    mixed_low = mixed_heads.reshape(token_count, local_width).astype(jnp.bfloat16)
    attend_part = jnp.dot(mixed_low, full_out, preferred_element_type=jnp.float32).reshape(
        seq_count, length, features
    )
    attend_all = lax.psum(attend_part.astype(jnp.bfloat16), "tp").astype(jnp.float32)
    pre_first = token_full.astype(jnp.float32) + attend_all + shifts[2]
    normed_first, unit_first, inverse_first = layer_norm_parts(pre_first, gains[0], shifts[0])
    hidden_full = normed_first.astype(jnp.bfloat16)
    normed_own = own_rows(normed_first, offset_own, piece_len)
    hidden_flat = hidden_full.reshape(token_count, features)
    up_all = jnp.dot(hidden_flat, full_up, preferred_element_type=jnp.float32) + full_bup.astype(
        jnp.float32
    )
    active = jax.nn.gelu(up_all, approximate=False).astype(jnp.bfloat16)
    down_part = jnp.dot(active, full_down, preferred_element_type=jnp.float32).reshape(
        seq_count, length, features
    )
    down_own = lax.psum_scatter(
        down_part.astype(jnp.bfloat16), "tp", scatter_dimension=1, tiled=True
    ).astype(jnp.float32)
    pre_second = normed_own + down_own + shifts[3]
    result, unit_second, inverse_second = layer_norm_parts(pre_second, gains[1], shifts[1])
    differ = result - teacher.astype(jnp.float32)
    mask_float = valid_mask.astype(jnp.float32)[..., None]
    squares, valid_count = lax.psum(
        (jnp.sum(mask_float * differ * differ), jnp.sum(mask_float)), ("fsdp", "tp")
    )
    loss_value = squares / (features * valid_count)
    grad_result = mask_float * differ * (total_tokens / valid_count)
    grad_second = norm_backward(unit_second, inverse_second, gains[1], grad_result)
    grad_down_full = lax.all_gather(grad_second.astype(jnp.bfloat16), "tp", axis=1, tiled=True)
    grad_down_flat = grad_down_full.reshape(token_count, features)
    weight_down = dot_first(active, grad_down_flat)
    grad_active = dot_last(grad_down_flat, full_down)
    gelu_back = jax.vjp(partial(jax.nn.gelu, approximate=False), up_all)[1]
    grad_up = gelu_back(grad_active)[0].astype(jnp.bfloat16)
    weight_up = dot_first(hidden_flat, grad_up)
    bias_up = jnp.sum(grad_up.astype(jnp.float32), axis=0)
    hidden_part = dot_last(grad_up, full_up).reshape(seq_count, length, features)
    current = own_rows(hidden_part, offset_own, piece_len)
    hidden_part = lax.dynamic_update_slice_in_dim(hidden_part, current + grad_second, offset_own, 1)
    grad_hidden_all = lax.psum(hidden_part.astype(jnp.bfloat16), "tp").astype(jnp.float32)
    grad_first_all = norm_backward(unit_first, inverse_first, gains[0], grad_hidden_all)
    grad_mix_full = grad_first_all.astype(jnp.bfloat16)
    grad_first_own = own_rows(grad_first_all, offset_own, piece_len)
    grad_hidden_own = own_rows(grad_hidden_all, offset_own, piece_len)
    unit_first_own = own_rows(unit_first, offset_own, piece_len)
    grad_mix_flat = grad_mix_full.reshape(token_count, features)
    weight_out = dot_first(mixed_low, grad_mix_flat)
    grad_mixed = dot_last(grad_mix_flat, full_out).astype(jnp.bfloat16).reshape(head_shape)
    grad_query, grad_key, grad_value = attention_backward(
        query_heads, key_heads, value_heads, segment_ids, summaries, grad_mixed
    )
    query_low = grad_query.astype(jnp.bfloat16).reshape(token_count, local_width)
    key_low = grad_key.astype(jnp.bfloat16).reshape(token_count, local_width)
    value_low = grad_value.astype(jnp.bfloat16).reshape(token_count, local_width)
    weight_query = dot_first(flat_in, query_low)
    weight_key = dot_first(flat_in, key_low)
    weight_value = dot_first(flat_in, value_low)
    bias_query = jnp.sum(query_low.astype(jnp.float32), axis=0)
    bias_value = jnp.sum(value_low.astype(jnp.float32), axis=0)
    input_part = (
        dot_last(query_low, full_query)
        + dot_last(key_low, full_key)
        + dot_last(value_low, full_value)
    )
    grad_inputs = (
        lax.psum_scatter(
            input_part.reshape(seq_count, length, features).astype(jnp.bfloat16),
            "tp",
            scatter_dimension=1,
            tiled=True,
        ).astype(jnp.float32)
        + grad_first_own
    )
    gain_part = jnp.stack(
        [
            jnp.sum(grad_hidden_own * unit_first_own, axis=(0, 1)),
            jnp.sum(grad_result * unit_second, axis=(0, 1)),
        ]
    )
    shift_part = jnp.stack(
        [
            jnp.sum(grad_hidden_own, axis=(0, 1)),
            jnp.sum(grad_result, axis=(0, 1)),
            jnp.sum(grad_first_own, axis=(0, 1)),
            jnp.sum(grad_second, axis=(0, 1)),
        ]
    )
    gain_sum, shift_sum = lax.psum((gain_part, shift_part), "tp")
    gradients = (
        lax.psum_scatter(
            weight_query.astype(jnp.bfloat16), "fsdp", scatter_dimension=0, tiled=True
        ).astype(jnp.float32),
        lax.psum_scatter(
            weight_key.astype(jnp.bfloat16), "fsdp", scatter_dimension=0, tiled=True
        ).astype(jnp.float32),
        lax.psum_scatter(
            weight_value.astype(jnp.bfloat16), "fsdp", scatter_dimension=0, tiled=True
        ).astype(jnp.float32),
        lax.psum_scatter(
            weight_out.astype(jnp.bfloat16), "fsdp", scatter_dimension=1, tiled=True
        ).astype(jnp.float32),
        lax.psum_scatter(
            bias_query.astype(jnp.bfloat16), "fsdp", scatter_dimension=0, tiled=True
        ).astype(jnp.float32),
        lax.psum_scatter(
            bias_value.astype(jnp.bfloat16), "fsdp", scatter_dimension=0, tiled=True
        ).astype(jnp.float32),
        lax.psum_scatter(
            weight_up.astype(jnp.bfloat16), "fsdp", scatter_dimension=0, tiled=True
        ).astype(jnp.float32),
        lax.psum_scatter(
            bias_up.astype(jnp.bfloat16), "fsdp", scatter_dimension=0, tiled=True
        ).astype(jnp.float32),
        lax.psum_scatter(
            weight_down.astype(jnp.bfloat16), "fsdp", scatter_dimension=1, tiled=True
        ).astype(jnp.float32),
        lax.psum_scatter(
            gain_sum.astype(jnp.bfloat16), "fsdp", scatter_dimension=1, tiled=True
        ).astype(jnp.float32),
        lax.psum_scatter(
            shift_sum.astype(jnp.bfloat16), "fsdp", scatter_dimension=1, tiled=True
        ).astype(jnp.float32),
    )
    return (
        result.astype(jnp.bfloat16),
        loss_value,
        grad_inputs.astype(jnp.bfloat16),
        gradients[0],
        gradients[1],
        gradients[2],
        gradients[3],
        gradients[4],
        gradients[5],
        gradients[6],
        gradients[7],
        gradients[8],
        gradients[9],
        gradients[10],
    )


BLOCK = 256
LOG2E = math.log2(math.e)
SHARD_ROWS_PARTS = 2


def rows_plan_fits(mesh):
    fsdp_count, tp_count = (mesh.shape["fsdp"], mesh.shape["tp"])
    return tp_count == 2 and fsdp_count >= 8 and fsdp_count & (fsdp_count - 1) == 0


def dot_plain(left_side, right_side):
    return lax.dot_general(
        left_side, right_side, (((1,), (0,)), ((), ())), preferred_element_type=jnp.float32
    )


def exchange(values, step):
    axis, bit = step
    count = lax.axis_size(axis)
    return lax.ppermute(values, axis, [(index, index ^ bit) for index in range(count)])


def step_orders():
    count = lax.axis_size("fsdp")
    across = ("tp", 1)
    core = ("fsdp", 1)
    side = ("fsdp", 2)
    far = [("fsdp", 1 << place) for place in range(2, count.bit_length() - 1)]
    far.reverse()
    first = tuple(far) + (across, side)
    second = (far[0], across, side) + tuple(far[1:])
    return core, (first, second)


def order_masks(order):
    masks = [(0, 0)]
    for axis, bit in order:
        fsdp_bit, tp_bit = (bit, 0) if axis == "fsdp" else (0, bit)
        masks = masks + [(high ^ fsdp_bit, low ^ tp_bit) for high, low in masks]
    return masks


def tie(values, *others):
    return lax.optimization_barrier((values, others))[0]


class GatherChain:

    def __init__(self, shard):
        self.core, self.orders = step_orders()
        half = shard.shape[1] // 2
        self.part_width = half
        self.held = [shard[None, :, :half], shard[None, :, half:]]
        self.arrived = None
        self.at = 0

    def advance(self, *after):
        if self.arrived is not None:
            self.held = [
                jnp.concatenate(pair, axis=0) for pair in zip(self.held, self.arrived)
            ]
        if after:
            self.held = tie(self.held, *after)
        self.arrived = [
            exchange(held, order[self.at]) for held, order in zip(self.held, self.orders)
        ]
        self.at += 1

    def finish(self, *after):
        if after:
            self.arrived = tie(self.arrived, *after)
        self.pieces = []
        for held, arrived in zip(self.held, self.arrived):
            self.pieces.append(
                [held, arrived, exchange(held, self.core), exchange(arrived, self.core)]
            )

    def marks(self):
        return self.held


def gather_masks(order, core):
    masks = order_masks(order)
    half = len(masks) // 2
    near = [masks[:half], masks[half:]]
    return near + [[(high ^ core[1], low) for high, low in group] for group in near]


def add_low(left_side, right_side):
    return (left_side.astype(jnp.float32) + right_side.astype(jnp.float32)).astype(jnp.bfloat16)


class ScatterChain:

    def __init__(self, pieces):
        self.core, orders = step_orders()
        self.orders = [tuple(reversed(order)) for order in orders]
        self.kept = [pieces[0], pieces[2]]
        self.sent = [pieces[1], pieces[3]]
        self.arrived = [exchange(sent, self.core) for sent in self.sent]
        self.at = 0

    def advance(self, *after):
        if after:
            self.arrived = tie(self.arrived, *after)
        half = self.kept[0].shape[0] // 2
        self.sent = [
            add_low(kept[half:], arrived[half:]) for kept, arrived in zip(self.kept, self.arrived)
        ]
        self.kept = [
            add_low(kept[:half], arrived[:half]) for kept, arrived in zip(self.kept, self.arrived)
        ]
        self.arrived = [
            exchange(sent, order[self.at]) for sent, order in zip(self.sent, self.orders)
        ]
        self.at += 1

    def done(self):
        return self.at == len(self.orders[0])

    def finish(self):
        return jnp.concatenate(
            [
                kept[0].astype(jnp.float32) + arrived[0].astype(jnp.float32)
                for kept, arrived in zip(self.kept, self.arrived)
            ],
            axis=1,
        )

    def marks(self):
        return (self.kept, self.sent)


def scatter_masks(order):
    return order_masks(order)


def assemble_kernel(plan, place_ref, *refs):
    count = plan["sources"]
    sources, targets, (held, in_sems, out_sems) = (refs[:count], refs[count:-3], refs[-3:])
    me_fsdp, me_tp = (place_ref[0], place_ref[1])
    rows = plan["rows"]
    arriving, leaving = ([], [])
    for at, entry in enumerate(plan["copies"]):
        source, place, start, width, high, low, target, per_tp, column = entry
        row = pl.multiple_of((me_fsdp ^ high) * rows, rows)
        lane = pl.multiple_of((me_tp ^ low) * per_tp + column, 128)
        between = held.at[plan["slots"][at], :, pl.ds(start, width)]
        if plan["gather"]:
            from_ref = sources[source].at[place, :, pl.ds(start, width)]
            to_ref = targets[target].at[pl.ds(row, rows), pl.ds(lane, width)]
        else:
            from_ref = sources[target].at[pl.ds(row, rows), pl.ds(lane, width)]
            to_ref = targets[source].at[place, :, pl.ds(start, width)]
        copy = pltpu.make_async_copy(from_ref, between, in_sems.at[at])
        copy.start()
        arriving.append(copy)
        leaving.append(pltpu.make_async_copy(between, to_ref, out_sems.at[at]))
    for first, second in zip(arriving, leaving):
        first.wait()
        second.start()
    for second in leaving:
        second.wait()


def run_assemble(plan, place, sources, out_shapes, name):
    any_spec = pl.BlockSpec(memory_space=pl.ANY)
    moved = sum(math.prod(out.shape) * 2 for out in out_shapes)
    copies = len(plan["copies"])
    slots = {}
    plan["slots"] = [slots.setdefault(entry[:2], len(slots)) for entry in plan["copies"]]
    return pl.pallas_call(
        partial(assemble_kernel, plan),
        in_specs=[pl.BlockSpec(memory_space=pltpu.SMEM)] + [any_spec] * len(sources),
        out_specs=[any_spec] * len(out_shapes),
        out_shape=out_shapes,
        scratch_shapes=[
            pltpu.VMEM((len(slots), plan["rows"], plan["span"]), jnp.bfloat16),
            pltpu.SemaphoreType.DMA((copies,)),
            pltpu.SemaphoreType.DMA((copies,)),
        ],
        compiler_params=pltpu.CompilerParams(vmem_limit_bytes=24 << 20),
        cost_estimate=pl.CostEstimate(flops=0, bytes_accessed=2 * moved, transcendentals=0),
        name=name,
    )(place, *sources)


def gather_group(chain, place, rows, columns, widths, name):
    sources, copies = ([], [])
    for part, order in enumerate(chain.orders):
        for piece, masks in zip(chain.pieces[part], gather_masks(order, chain.core)):
            for place_at, (high, low) in enumerate(masks):
                for entry in columns[part]:
                    start, width, target, per_tp, column = entry
                    copies.append(
                        (len(sources), place_at, start, width, high, low, target, per_tp, column)
                    )
            sources.append(piece)
    plan = dict(gather=True, sources=len(sources), rows=rows, copies=copies, span=chain.part_width)
    full_rows = rows * lax.axis_size("fsdp")
    shapes = [jax.ShapeDtypeStruct((full_rows, span), jnp.bfloat16) for span in widths]
    return run_assemble(plan, place, sources, shapes, name)


def scatter_group(fulls, place, columns, rows, part_width, name):
    core, orders = step_orders()
    copies, shapes = ([], [])
    for part, order in enumerate(orders):
        masks = scatter_masks(order)
        for flip in (0, core[1]):
            for place_at, (high, low) in enumerate(masks):
                for start, width, target, per_tp, column in columns[part]:
                    copies.append(
                        (len(shapes), place_at, start, width, high ^ flip, low, target, per_tp, column)
                    )
            shapes.append(jax.ShapeDtypeStruct((len(masks), rows, part_width), jnp.bfloat16))
    plan = dict(gather=False, sources=len(fulls), rows=rows, copies=copies, span=part_width)
    return ScatterChain(run_assemble(plan, place, fulls, shapes, name))


def bit_steps():
    steps = []
    for axis in ("fsdp", "tp"):
        for place in range(lax.axis_size(axis).bit_length() - 1):
            steps.append((axis, 1 << place))
    return steps


def gather_small(values):
    for step in bit_steps():
        mine = (lax.axis_index(step[0]) & step[1]) != 0
        arrived = exchange(values, step)
        values = jnp.concatenate(
            [jnp.where(mine, arrived, values), jnp.where(mine, values, arrived)], axis=0
        )
    return values


def scatter_small(values):
    for step in reversed(bit_steps()):
        mine = (lax.axis_index(step[0]) & step[1]) != 0
        half = values.shape[0] // 2
        low, high = (values[:half], values[half:])
        values = jnp.where(mine, high, low) + exchange(jnp.where(mine, low, high), step)
    return values[0]


def block_span(block, count):
    reach = -(-WINDOW // BLOCK)
    return max(0, block - reach), min(count - 1, block + reach)


def split_three(values):
    high = values.astype(jnp.bfloat16)
    rest = values - high.astype(jnp.float32)
    mid = rest.astype(jnp.bfloat16)
    low = (rest - mid.astype(jnp.float32)).astype(jnp.bfloat16)
    return high, mid, low


def window_edge(tile, row_block, column_block):
    if (abs(row_block - column_block) + 1) * BLOCK - 1 < WINDOW:
        return tile
    row = lax.broadcasted_iota(jnp.int32, tile.shape, 0) + row_block * BLOCK
    column = lax.broadcasted_iota(jnp.int32, tile.shape, 1) + column_block * BLOCK
    return jnp.where(jnp.abs(row - column) < WINDOW, tile, MASKED)


def attend_kernel(seg_ref, q_ref, k_ref, v_ref, out_ref, qx_ref, kx_ref, held_ref):
    length = q_ref.shape[0]
    count = length // BLOCK
    lane = lax.broadcasted_iota(jnp.int32, (length, 128), 1)
    seg = seg_ref[...]
    q_heads, k_heads, v_heads = ([], [], [])
    for head in range(2):
        own = (lane < 64) if head == 0 else (lane >= 64)
        extra = lane - 64 if head == 0 else lane
        same = extra == seg
        q_extra = jnp.where(same, 1.0, 0.0).astype(jnp.bfloat16)
        k_extra = jnp.where(
            extra < 4, jnp.where(same, 0.0, MASKED), jnp.where(extra < 7, -1.0, 0.0)
        ).astype(jnp.bfloat16)
        v_extra = jnp.where(extra == 0, 1.0, 0.0).astype(jnp.bfloat16)
        q_heads.append(jnp.where(own, q_ref[...], q_extra))
        k_heads.append(jnp.where(own, k_ref[...], k_extra))
        v_heads.append(jnp.where(own, v_ref[...], v_extra))
        kx_ref[head] = k_heads[head]
    units = [(head, block) for head in range(2) for block in range(count)]

    def score(unit):
        head, block = unit
        low, high = block_span(block, count)
        rows = slice(block * BLOCK, (block + 1) * BLOCK)
        tile = dot_last(q_heads[head][rows], k_heads[head][low * BLOCK : (high + 1) * BLOCK])
        return [
            window_edge(tile[:, (at - low) * BLOCK : (at - low + 1) * BLOCK], block, at)
            for at in range(low, high + 1)
        ]

    def finish(unit, tiles):
        head, block = unit
        low, high = block_span(block, count)
        rows = slice(block * BLOCK, (block + 1) * BLOCK)
        most = tiles[0]
        for tile in tiles[1:]:
            most = jnp.maximum(most, tile)
        top = jnp.max(most, axis=1, keepdims=True)
        raised = jnp.concatenate(
            [jnp.exp2(tile - top).astype(jnp.bfloat16) for tile in tiles], axis=1
        )
        mixed = dot_plain(raised, v_heads[head][low * BLOCK : (high + 1) * BLOCK])
        norm_sum = mixed[:, 64:65] if head == 0 else mixed[:, 0:1]
        held_ref[head, rows, :] = mixed * (1.0 / norm_sum)
        first, second, third = split_three(top + jnp.log2(norm_sum))
        extra = lane[:BLOCK] - 64 if head == 0 else lane[:BLOCK]
        qx_ref[head, rows, :] = jnp.where(
            extra == 4,
            first,
            jnp.where(extra == 5, second, jnp.where(extra == 6, third, q_heads[head][rows])),
        )

    tiles = score(units[0])
    for at, unit in enumerate(units):
        following = score(units[at + 1]) if at + 1 < len(units) else None
        finish(unit, tiles)
        tiles = following
    out_ref[...] = jnp.where(lane < 64, held_ref[0], held_ref[1]).astype(jnp.bfloat16)


def attend(queries, keys, values, seg, first, count, earlier=None):
    length, width = queries.shape
    pair = pl.BlockSpec((length, 128), lambda step: (0, first + step))
    padded = pl.BlockSpec((2, length, 128), lambda step: (first + step, 0, 0))
    passed = 0 if earlier is None else 3
    operands = (seg, queries, keys, values) + (earlier or ())

    def kernel(seg_ref, q_ref, k_ref, v_ref, *refs):
        attend_kernel(seg_ref, q_ref, k_ref, v_ref, *refs[passed:])

    return pl.pallas_call(
        kernel,
        grid=(count,),
        in_specs=[pl.BlockSpec((length, 1), lambda step: (0, 0)), pair, pair, pair]
        + [pl.BlockSpec(memory_space=pl.ANY)] * passed,
        out_specs=[pair, padded, padded],
        out_shape=[
            jax.ShapeDtypeStruct((length, width), jnp.bfloat16),
            jax.ShapeDtypeStruct((width // HEAD_DIM, length, 128), jnp.bfloat16),
            jax.ShapeDtypeStruct((width // HEAD_DIM, length, 128), jnp.bfloat16),
        ],
        scratch_shapes=[pltpu.VMEM((2, length, 128), jnp.float32)],
        input_output_aliases={4 + at: at for at in range(passed)},
        compiler_params=pltpu.CompilerParams(vmem_limit_bytes=40 << 20),
        cost_estimate=pl.CostEstimate(
            flops=3_500_000_000 * count,
            bytes_accessed=(2 << 20) * count,
            transcendentals=2 * count * length * length,
        ),
        name="attend",
    )(*operands)


def attend_back_kernel(qx_ref, kx_ref, v_ref, out_ref, grad_ref, dq_ref, dk_ref, dv_ref, held_ref):
    length = v_ref.shape[0]
    count = length // BLOCK
    lane = lax.broadcasted_iota(jnp.int32, (length, 128), 1)
    grad = grad_ref[...]
    for head in range(2):
        mine = slice(head * 64, (head + 1) * 64)
        own = (lane < 64) if head == 0 else (lane >= 64)
        extra = lane - 64 if head == 0 else lane
        product = jnp.where(
            own, grad.astype(jnp.float32) * out_ref[...].astype(jnp.float32), 0.0
        )
        first, second, third = split_three(-jnp.sum(product, axis=1, keepdims=True))
        grad_head = jnp.where(
            own,
            grad,
            jnp.where(
                extra == 0,
                first,
                jnp.where(extra == 1, second, jnp.where(extra == 2, third, jnp.zeros_like(grad))),
            ),
        )
        v_head = jnp.where(own, v_ref[...], jnp.where(extra < 3, 1.0, 0.0).astype(jnp.bfloat16))
        q_head, k_head = (qx_ref[head], kx_ref[head])
        k_turned = k_head.T[mine]
        for block in range(count):
            low, high = block_span(block, count)
            keys = slice(block * BLOCK, (block + 1) * BLOCK)
            span = slice(low * BLOCK, (high + 1) * BLOCK)
            tile = dot_last(k_head[keys], q_head[span])
            soft = jnp.concatenate(
                [
                    jnp.exp2(
                        window_edge(tile[:, (at - low) * BLOCK : (at - low + 1) * BLOCK], block, at)
                    )
                    for at in range(low, high + 1)
                ],
                axis=1,
            )
            grad_soft = dot_last(v_head[keys], grad_head[span])
            grad_score = (soft * grad_soft).astype(jnp.bfloat16)
            grad_value = dot_plain(soft.astype(jnp.bfloat16), grad_head[span])
            grad_key = dot_plain(grad_score, q_head[span]) * (1.0 / LOG2E)
            dv_ref[keys, mine] = grad_value[:, mine].astype(jnp.bfloat16)
            dk_ref[keys, mine] = grad_key[:, mine].astype(jnp.bfloat16)
            grad_query = dot_plain(k_turned[:, keys], grad_score)
            if block == 0:
                held_ref[mine, span] = grad_query
                if high + 1 < count:
                    held_ref[mine, (high + 1) * BLOCK :] = jnp.zeros(
                        (64, length - (high + 1) * BLOCK), jnp.float32
                    )
            else:
                held_ref[mine, span] += grad_query
    dq_ref[...] = (held_ref[...] * (1.0 / math.sqrt(HEAD_DIM))).T.astype(jnp.bfloat16)


def attend_back(q_padded, k_padded, values, mixed, grad_mixed, first, count, out_first, earlier=None):
    length, width = values.shape
    pair = pl.BlockSpec((length, 128), lambda step: (0, first + step))
    out_pair = pl.BlockSpec((length, 128), lambda step: (0, first - out_first + step))
    padded = pl.BlockSpec((2, length, 128), lambda step: (first + step, 0, 0))
    passed = 0 if earlier is None else 3
    operands = (q_padded, k_padded, values, mixed, grad_mixed) + tuple(earlier or ())

    def kernel(qx_ref, kx_ref, v_ref, out_ref, grad_ref, *refs):
        attend_back_kernel(qx_ref, kx_ref, v_ref, out_ref, grad_ref, *refs[passed:])

    return pl.pallas_call(
        kernel,
        grid=(count,),
        in_specs=[padded, padded, pair, pair, pair]
        + [pl.BlockSpec(memory_space=pl.ANY)] * passed,
        out_specs=[out_pair, out_pair, out_pair],
        out_shape=[jax.ShapeDtypeStruct((length, width // 2), jnp.bfloat16)] * 3,
        scratch_shapes=[pltpu.VMEM((128, length), jnp.float32)],
        input_output_aliases={5 + at: at for at in range(passed)},
        compiler_params=pltpu.CompilerParams(vmem_limit_bytes=40 << 20),
        cost_estimate=pl.CostEstimate(
            flops=5_000_000_000 * count,
            bytes_accessed=(2 << 20) * count,
            transcendentals=2 * count * length * length,
        ),
        name="attend_back",
    )(*operands)


def up_kernel(x_ref, w_ref, b_ref, active_ref, slope_ref):
    length = x_ref.shape[0]
    count = length // BLOCK

    def product(block):
        rows = slice(block * BLOCK, (block + 1) * BLOCK)
        return dot_plain(x_ref[rows], w_ref[...]) + b_ref[...]

    up = product(0)
    for block in range(count):
        following = product(block + 1) if block + 1 < count else None
        rows = slice(block * BLOCK, (block + 1) * BLOCK)
        cumulative = 0.5 * (1.0 + lax.erf(up * math.sqrt(0.5)))
        density = jnp.exp2(up * up * (-0.5 * LOG2E)) * (1.0 / math.sqrt(2.0 * math.pi))
        active_ref[rows] = (up * cumulative).astype(jnp.bfloat16)
        slope_ref[rows] = (cumulative + up * density).astype(jnp.bfloat16)
        up = following


def up_project(hidden, weight, bias):
    length, features = hidden.shape
    width = weight.shape[1]
    block_width = math.gcd(width, 512)
    column = pl.BlockSpec((length, block_width), lambda step: (0, step))
    return pl.pallas_call(
        up_kernel,
        grid=(width // block_width,),
        in_specs=[
            pl.BlockSpec((length, features), lambda step: (0, 0)),
            pl.BlockSpec((features, block_width), lambda step: (0, step)),
            pl.BlockSpec((1, block_width), lambda step: (0, step)),
        ],
        out_specs=[column, column],
        out_shape=[jax.ShapeDtypeStruct((length, width), jnp.bfloat16)] * 2,
        compiler_params=pltpu.CompilerParams(vmem_limit_bytes=40 << 20),
        cost_estimate=pl.CostEstimate(
            flops=2 * length * features * width,
            bytes_accessed=2 * (length * features + features * width + 2 * length * width),
            transcendentals=2 * length * width,
        ),
        name="up_project",
    )(hidden, weight, bias)


def own_first(row_values, tp_rank, piece_len):
    mine = lax.dynamic_slice_in_dim(row_values, tp_rank * piece_len, piece_len, 0)
    theirs = lax.dynamic_slice_in_dim(row_values, (1 - tp_rank) * piece_len, piece_len, 0)
    return mine, theirs


def swap_in(pieces, tp_rank):
    mine = lax.dynamic_index_in_dim(pieces, tp_rank, 0, keepdims=False)
    theirs = lax.dynamic_index_in_dim(pieces, 1 - tp_rank, 0, keepdims=False)
    arrived = exchange(theirs, ("tp", 1))
    first = tp_rank == 0
    return jnp.concatenate(
        [jnp.where(first, mine, arrived), jnp.where(first, arrived, mine)], axis=0
    )


def swap_out(row_values, tp_rank, piece_len):
    mine, theirs = own_first(row_values, tp_rank, piece_len)
    arrived = exchange(theirs, ("tp", 1))
    first = tp_rank == 0
    return jnp.stack([jnp.where(first, mine, arrived), jnp.where(first, arrived, mine)])


def on_device_rows(
    inputs,
    segment_ids,
    valid_mask,
    teacher,
    w_query,
    w_key,
    w_value,
    w_out,
    b_query,
    b_value,
    w_up,
    b_up,
    w_down,
    ln_gains,
    ln_shifts,
):
    seq_count, piece_len, features = inputs.shape
    fsdp_count, tp_count = (lax.axis_size("fsdp"), lax.axis_size("tp"))
    fsdp_rank, tp_rank = (lax.axis_index("fsdp"), lax.axis_index("tp"))
    assert seq_count == tp_count
    total_tokens = seq_count * piece_len * tp_count * fsdp_count
    shard_rows, local_width = w_query.shape
    local_hidden = w_up.shape[1]
    width, hidden_units = (local_width * tp_count, local_hidden * tp_count)
    place = jnp.stack([fsdp_rank, tp_rank]).astype(jnp.int32)

    row_low = swap_in(inputs, tp_rank)
    seg = lax.dynamic_index_in_dim(segment_ids, tp_rank, 0, keepdims=False)[:, None]

    quarter = local_width // 2
    part_width = local_hidden // 2
    qkv_spans = [(at // 2 * width + at % 2 * local_width) for at in range(6)]
    qkv_columns = [
        [(at * quarter, quarter, 0, quarter, qkv_spans[3 * part + at]) for at in range(3)]
        for part in range(2)
    ]
    up_cut = (local_hidden + local_width) // 2
    up_rest = local_hidden - up_cut
    up_columns = [
        [(0, up_cut, 0, local_hidden, 0)],
        [
            (0, up_rest, 0, local_hidden, up_cut),
            (up_rest, quarter, 1, quarter, 0),
            (up_rest + quarter, quarter, 1, quarter, local_width),
        ],
    ]
    wide_columns = [
        [(0, part_width, 0, local_hidden, part * part_width)] for part in range(2)
    ]
    chain_qkv = GatherChain(jnp.concatenate([w_query, w_key, w_value], axis=1))
    chain_up = GatherChain(jnp.concatenate([w_up, w_out.T], axis=1))
    chain_down = GatherChain(w_down.T)
    chain_qkv.advance()
    chain_qkv.advance()
    chain_qkv.advance()
    chain_up.advance(chain_qkv.marks())
    chain_qkv.advance()
    chain_up.advance(chain_qkv.marks())
    chain_qkv.finish()
    chain_up.advance(chain_qkv.pieces)
    chain_down.advance(chain_qkv.pieces)

    valid_row = swap_in(valid_mask[..., None], tp_rank).astype(jnp.float32)
    small = jnp.concatenate(
        [
            b_query.astype(jnp.float32),
            b_value.astype(jnp.float32),
            b_up.astype(jnp.float32),
            ln_gains.astype(jnp.float32).reshape(-1),
            ln_shifts.astype(jnp.float32).reshape(-1),
            jnp.sum(valid_mask.astype(jnp.float32))[None],
        ]
    )
    small_len = small.shape[0]
    padded_len = -(-small_len // 128) * 128
    small = jnp.pad(small, (0, padded_len - small_len)).reshape(1, padded_len // 128, 128)
    small_all = gather_small(small).reshape(tp_count * fsdp_count, padded_len)
    cuts = []
    at = 0
    for count in (b_query.size, b_value.size, b_up.size, ln_gains.size, ln_shifts.size, 1):
        cuts.append(small_all[:, at : at + count])
        at += count
    def head_order(columns):
        return columns.reshape(tp_count, 2, quarter).transpose(1, 0, 2).reshape(width)

    bias_query, bias_value = (head_order(cuts[0]), head_order(cuts[1]))
    bias_up = cuts[2].reshape(-1)

    def feature_rows(columns, rows):
        return (
            columns[:fsdp_count]
            .reshape(fsdp_count, rows, features // fsdp_count)
            .transpose(1, 0, 2)
            .reshape(rows, features)
        )

    gains = feature_rows(cuts[3], 2)
    shifts = feature_rows(cuts[4], 4)
    valid_count = jnp.sum(cuts[5])
    teacher_row = swap_in(teacher, tp_rank).astype(jnp.float32)

    scale = LOG2E / math.sqrt(HEAD_DIM)
    (full_qkv,) = gather_group(
        chain_qkv, tie(place, chain_up.marks(), chain_down.marks()), shard_rows, qkv_columns, [3 * width], "gather_qkv"
    )
    queries = (
        (dot_plain(row_low, full_qkv[:, :width]) + bias_query) * scale
    ).astype(jnp.bfloat16)
    keys = dot_plain(row_low, full_qkv[:, width : 2 * width]).astype(jnp.bfloat16)
    values = (dot_plain(row_low, full_qkv[:, 2 * width :]) + bias_value).astype(jnp.bfloat16)
    pairs = width // 128
    chain_up.advance(queries, keys, values)
    chain_down.advance(queries, keys, values)
    queries = tie(queries, chain_up.marks(), chain_down.marks())
    attended = attend(queries, keys, values, seg, 0, pairs // 4)
    chain_down.advance(attended)
    attended = attend(
        queries, keys, tie(values, chain_down.marks()), seg, pairs // 4, pairs // 4, attended
    )
    chain_up.finish(attended)
    attended = attend(
        queries, keys, tie(values, chain_up.pieces), seg, pairs // 2, pairs // 4, attended
    )
    chain_down.advance(attended)
    mixed, q_padded, k_padded = attend(
        queries, keys, tie(values, chain_down.marks()), seg, 3 * pairs // 4, pairs // 4, attended
    )
    full_up, full_out = gather_group(
        chain_up, tie(place, mixed), shard_rows, up_columns, [hidden_units, width], "gather_up"
    )
    pre_first = row_low.astype(jnp.float32) + dot_last(mixed, full_out) + shifts[2]
    normed_first, unit_first, inverse_first = layer_norm_parts(pre_first, gains[0], shifts[0])
    hidden_low = normed_first.astype(jnp.bfloat16)
    chain_down.finish(hidden_low)
    active, slope = up_project(tie(hidden_low, chain_down.pieces), full_up, bias_up[None])
    (full_down,) = gather_group(
        chain_down, tie(place, active), shard_rows, wide_columns, [hidden_units], "gather_down"
    )
    pre_second = normed_first + dot_last(active, full_down) + shifts[3]
    result, unit_second, inverse_second = layer_norm_parts(pre_second, gains[1], shifts[1])
    hidden_out = swap_out(result.astype(jnp.bfloat16), tp_rank, piece_len)

    differ = result - teacher_row
    grad_result = valid_row * differ * (total_tokens / valid_count)
    squares = jnp.sum(valid_row * differ * differ)
    grad_second = norm_backward(unit_second, inverse_second, gains[1], grad_result)
    grad_down = grad_second.astype(jnp.bfloat16)
    weight_down = dot_first(grad_down, active).astype(jnp.bfloat16)
    sum_down = scatter_group(
        [weight_down], place, wide_columns, shard_rows, part_width, "scatter_down"
    )
    grad_down = tie(grad_down, sum_down.marks())
    grad_up = (dot_plain(grad_down, full_down) * slope.astype(jnp.float32)).astype(jnp.bfloat16)
    grad_b_up = jnp.sum(grad_up.astype(jnp.float32), axis=0)
    sum_down.advance(grad_up)
    grad_up = tie(grad_up, sum_down.marks())
    weight_up = dot_first(hidden_low, grad_up).astype(jnp.bfloat16)
    sum_up = scatter_group(
        [weight_up], place, wide_columns, shard_rows, part_width, "scatter_up"
    )
    sum_down.advance(weight_up)
    grad_up = tie(grad_up, sum_up.marks(), sum_down.marks())
    grad_hidden = grad_second + dot_last(grad_up, full_up)
    grad_first = norm_backward(unit_first, inverse_first, gains[0], grad_hidden)
    grad_attend = grad_first.astype(jnp.bfloat16)
    sum_up.advance(grad_attend)
    sum_down.advance(grad_attend)
    grad_attend = tie(grad_attend, sum_up.marks(), sum_down.marks())
    weight_out = dot_first(grad_attend, mixed).astype(jnp.bfloat16)
    grad_mixed = dot_plain(grad_attend, full_out).astype(jnp.bfloat16)
    back = partial(attend_back, q_padded, k_padded, values, mixed)
    sum_down.advance(grad_mixed)
    first_grads = back(tie(grad_mixed, sum_down.marks()), 0, pairs // 4, 0)
    sum_up.advance(first_grads)
    first_grads = back(
        tie(grad_mixed, sum_up.marks()), pairs // 4, pairs // 4, 0, first_grads
    )
    sum_up.advance(first_grads)
    weight_first = [
        dot_first(tie(row_low, sum_up.marks()), part).astype(jnp.bfloat16) for part in first_grads
    ]
    first_columns = [
        [
            (0, quarter, 0, quarter, 0),
            (quarter, quarter, 0, quarter, local_width),
            (2 * quarter, quarter // 2, 1, quarter, 0),
        ],
        [
            (0, quarter // 2, 1, quarter, quarter // 2),
            (quarter // 2, quarter, 2, quarter, 0),
            (quarter // 2 + quarter, quarter, 3, quarter, 0),
        ],
    ]
    sum_first = scatter_group(
        [weight_out] + weight_first, place, first_columns, shard_rows, 5 * quarter // 2, "scatter_first"
    )
    second_grads = back(tie(grad_mixed, sum_first.marks()), pairs // 2, pairs // 4, pairs // 2)
    sum_up.advance(second_grads)
    sum_first.advance(second_grads)
    second_grads = back(
        tie(grad_mixed, sum_up.marks(), sum_first.marks()),
        3 * pairs // 4,
        pairs // 4,
        pairs // 2,
        second_grads,
    )
    sum_first.advance(second_grads)
    second_grads = tie(second_grads, sum_first.marks())
    weight_second = [dot_first(row_low, part).astype(jnp.bfloat16) for part in second_grads]
    second_columns = [
        [(0, quarter, 0, quarter, 0), (quarter, quarter // 2, 1, quarter, 0)],
        [(0, quarter // 2, 1, quarter, quarter // 2), (quarter // 2, quarter, 2, quarter, 0)],
    ]
    sum_second = scatter_group(
        weight_second, place, second_columns, shard_rows, 3 * quarter // 2, "scatter_second"
    )
    sum_first.advance(weight_second)
    halves = [
        jnp.concatenate(pair, axis=1) for pair in zip(first_grads, second_grads)
    ]
    halves = tie(halves, sum_second.marks(), sum_first.marks())
    grad_query, grad_key, grad_value = halves
    grad_row = (
        grad_first
        + dot_last(grad_query, full_qkv[:, :width])
        + dot_last(grad_key, full_qkv[:, width : 2 * width])
        + dot_last(grad_value, full_qkv[:, 2 * width :])
    ).astype(jnp.bfloat16)
    grad_inputs = swap_out(grad_row, tp_rank, piece_len)
    sum_second.advance(grad_row)
    sum_first.advance(grad_row)
    for _ in range(3):
        sum_second.advance()
    grad_w_down = sum_down.finish().T
    grad_w_up = sum_up.finish()
    first_shard, second_shard = (sum_first.finish(), sum_second.finish())
    grad_w_out = first_shard[:, : 2 * quarter]
    grad_w_query, grad_w_key, grad_w_value = [
        jnp.concatenate(
            [
                first_shard[:, (2 + at) * quarter : (3 + at) * quarter],
                second_shard[:, at * quarter : (at + 1) * quarter],
            ],
            axis=1,
        )
        for at in range(3)
    ]

    def device_order(columns):
        return columns.reshape(2, tp_count, quarter).transpose(1, 0, 2).reshape(devices, -1)

    def feature_pieces(rows):
        pieces = rows.reshape(rows.shape[0], fsdp_count, -1).transpose(1, 0, 2).reshape(fsdp_count, -1)
        return jnp.concatenate([pieces] * tp_count, axis=0)

    devices = tp_count * fsdp_count
    pieces = jnp.concatenate(
        [
            device_order(jnp.sum(grad_query.astype(jnp.float32), axis=0)),
            device_order(jnp.sum(grad_value.astype(jnp.float32), axis=0)),
            grad_b_up.reshape(devices, -1),
            feature_pieces(
                jnp.stack(
                    [
                        jnp.sum(grad_hidden * unit_first, axis=0),
                        jnp.sum(grad_result * unit_second, axis=0),
                    ]
                )
            ),
            feature_pieces(
                jnp.stack(
                    [
                        jnp.sum(grad_hidden, axis=0),
                        jnp.sum(grad_result, axis=0),
                        jnp.sum(grad_first, axis=0),
                        jnp.sum(grad_second, axis=0),
                    ]
                )
            ),
            jnp.full((devices, 1), squares),
        ],
        axis=1,
    )
    pieces = jnp.pad(pieces, ((0, 0), (0, padded_len - small_len)))
    own = scatter_small(pieces.reshape(devices, padded_len // 128, 128)).reshape(padded_len)
    results = []
    at = 0
    for count in (b_query.size, b_value.size, b_up.size, ln_gains.size, ln_shifts.size, 1):
        results.append(own[at : at + count])
        at += count
    loss_value = results[5][0] / (features * valid_count)
    return (
        hidden_out,
        loss_value,
        grad_inputs,
        grad_w_query,
        grad_w_key,
        grad_w_value,
        grad_w_out.T,
        results[0],
        results[1],
        grad_w_up,
        results[2],
        grad_w_down,
        results[3].reshape(ln_gains.shape),
        results[4].reshape(ln_shifts.shape),
    )


def solution(mesh):
    in_specs = (
        P("fsdp", "tp", None),
        P("fsdp", None),
        P("fsdp", "tp"),
        P("fsdp", "tp", None),
        P("fsdp", "tp"),
        P("fsdp", "tp"),
        P("fsdp", "tp"),
        P("tp", "fsdp"),
        P(("tp", "fsdp")),
        P(("tp", "fsdp")),
        P("fsdp", "tp"),
        P(("tp", "fsdp")),
        P("tp", "fsdp"),
        P(None, "fsdp"),
        P(None, "fsdp"),
    )
    out_specs = (
        P("fsdp", "tp", None),
        P(),
        P("fsdp", "tp", None),
        P("fsdp", "tp"),
        P("fsdp", "tp"),
        P("fsdp", "tp"),
        P("tp", "fsdp"),
        P(("tp", "fsdp")),
        P(("tp", "fsdp")),
        P("fsdp", "tp"),
        P(("tp", "fsdp")),
        P("tp", "fsdp"),
        P(None, "fsdp"),
        P(None, "fsdp"),
    )
    rows_plan = rows_plan_fits(mesh)
    return jax.shard_map(
        on_device_rows if rows_plan else on_device_heads, mesh=mesh, in_specs=in_specs, out_specs=out_specs, check_vma=False
    )
```

```python
from functools import partial
import math

import jax
import jax.numpy as jnp
from jax import lax
from jax.experimental import pallas as pl
from jax.experimental.pallas import tpu as pltpu
from jax.sharding import PartitionSpec as P

HEAD_DIM = 64
WINDOW = 512


EPSILON = 1e-05
MASKED = -1e30


def layer_norm_parts(values, gain_row, shift_row):
    centre = jnp.mean(values, axis=-1, keepdims=True)
    centred = values - centre
    inverse = lax.rsqrt(jnp.mean(centred * centred, axis=-1, keepdims=True) + EPSILON)
    normed = centred * inverse
    return (normed * gain_row + shift_row, normed, inverse)


def norm_backward(normed, inverse, gain_row, grad_out):
    scaled = grad_out * gain_row
    return inverse * (
        scaled
        - jnp.mean(scaled, axis=-1, keepdims=True)
        - normed * jnp.mean(scaled * normed, axis=-1, keepdims=True)
    )


def dot_first(left_side, right_side):
    return lax.dot_general(
        left_side, right_side, (((0,), (0,)), ((), ())), preferred_element_type=jnp.float32
    )


def dot_last(left_side, right_side):
    return lax.dot_general(
        left_side, right_side, (((1,), (1,)), ((), ())), preferred_element_type=jnp.float32
    )


def own_rows(source, offset_own, piece_len):
    return lax.dynamic_slice_in_dim(source, offset_own, piece_len, 1)


def allowed_mask(seg_row, offset, block_len):
    length = seg_row.shape[0]
    position = jnp.arange(length, dtype=jnp.int32)
    query_pos = offset + jnp.arange(block_len, dtype=jnp.int32)
    same_doc = seg_row[offset : offset + block_len][:, None] == seg_row[None, :]
    return same_doc & (jnp.abs(query_pos[:, None] - position[None, :]) < WINDOW)


def block_scores(query_part, key_heads, allowed):
    scores = jnp.einsum(
        "qhd,khd->hqk", query_part, key_heads, preferred_element_type=jnp.float32
    ) / math.sqrt(HEAD_DIM)
    return jnp.where(allowed[None], scores, MASKED)


def attention_forward(queries, key_all, value_all, segment_ids):
    seq_count, length = (queries.shape[0], queries.shape[1])
    block_len = min(512, length)
    outputs, summaries = ([], [])
    for row_index in range(seq_count):
        row_out, row_lse = ([], [])
        for offset in range(0, length, block_len):
            allowed = allowed_mask(segment_ids[row_index], offset, block_len)
            scores = block_scores(
                queries[row_index, offset : offset + block_len], key_all[row_index], allowed
            )
            row_top = jnp.max(scores, axis=-1, keepdims=True)
            raised = jnp.exp(scores - row_top)
            norm_sum = jnp.sum(raised, axis=-1, keepdims=True)
            softened = (raised / norm_sum).astype(jnp.bfloat16)
            row_out.append(
                jnp.einsum(
                    "hqk,khd->qhd",
                    softened,
                    value_all[row_index],
                    preferred_element_type=jnp.float32,
                )
            )
            row_lse.append(row_top + jnp.log(norm_sum))
        outputs.append(jnp.concatenate(row_out, axis=0))
        summaries.append(jnp.concatenate(row_lse, axis=1))
    return (jnp.stack(outputs), jnp.stack(summaries))


def attention_backward(queries, key_all, value_all, segment_ids, summaries, grad_mixed):
    seq_count, length = (queries.shape[0], queries.shape[1])
    block_len = min(512, length)
    root_dim = math.sqrt(HEAD_DIM)
    query_rows, key_rows, value_rows = ([], [], [])
    for row_index in range(seq_count):
        key_grad = jnp.zeros(key_all.shape[1:], jnp.float32)
        value_grad = jnp.zeros(value_all.shape[1:], jnp.float32)
        query_parts = []
        for offset in range(0, length, block_len):
            allowed = allowed_mask(segment_ids[row_index], offset, block_len)
            query_part = queries[row_index, offset : offset + block_len]
            scores = block_scores(query_part, key_all[row_index], allowed)
            softened = jnp.exp(scores - summaries[row_index, :, offset : offset + block_len])
            grad_part = grad_mixed[row_index, offset : offset + block_len]
            value_grad = value_grad + jnp.einsum(
                "hqk,qhd->khd",
                softened.astype(jnp.bfloat16),
                grad_part,
                preferred_element_type=jnp.float32,
            )
            grad_soft = jnp.einsum(
                "qhd,khd->hqk", grad_part, value_all[row_index], preferred_element_type=jnp.float32
            )
            grad_score = (
                softened * (grad_soft - jnp.sum(softened * grad_soft, axis=-1, keepdims=True))
            ).astype(jnp.bfloat16)
            query_parts.append(
                jnp.einsum(
                    "hqk,khd->qhd",
                    grad_score,
                    key_all[row_index],
                    preferred_element_type=jnp.float32,
                )
                / root_dim
            )
            key_grad = (
                key_grad
                + jnp.einsum(
                    "hqk,qhd->khd", grad_score, query_part, preferred_element_type=jnp.float32
                )
                / root_dim
            )
        query_rows.append(jnp.concatenate(query_parts, axis=0))
        key_rows.append(key_grad)
        value_rows.append(value_grad)
    return (jnp.stack(query_rows), jnp.stack(key_rows), jnp.stack(value_rows))


def on_device_heads(
    inputs,
    segment_ids,
    valid_mask,
    teacher,
    w_query,
    w_key,
    w_value,
    w_out,
    b_query,
    b_value,
    w_up,
    b_up,
    w_down,
    ln_gains,
    ln_shifts,
):
    seq_count, piece_len, features = inputs.shape
    tp_count = lax.axis_size("tp")
    tp_rank = lax.axis_index("tp")
    length = piece_len * tp_count
    total_tokens = seq_count * length * lax.axis_size("fsdp")
    offset_own = tp_rank * piece_len
    (
        full_query,
        full_key,
        full_value,
        full_out,
        full_bquery,
        full_bvalue,
        full_up,
        full_bup,
        full_down,
        full_gains,
        full_shifts,
    ) = (
        lax.all_gather(w_query, "fsdp", axis=0, tiled=True),
        lax.all_gather(w_key, "fsdp", axis=0, tiled=True),
        lax.all_gather(w_value, "fsdp", axis=0, tiled=True),
        lax.all_gather(w_out, "fsdp", axis=1, tiled=True),
        lax.all_gather(b_query, "fsdp", axis=0, tiled=True),
        lax.all_gather(b_value, "fsdp", axis=0, tiled=True),
        lax.all_gather(w_up, "fsdp", axis=0, tiled=True),
        lax.all_gather(b_up, "fsdp", axis=0, tiled=True),
        lax.all_gather(w_down, "fsdp", axis=1, tiled=True),
        lax.all_gather(ln_gains, "fsdp", axis=1, tiled=True),
        lax.all_gather(ln_shifts, "fsdp", axis=1, tiled=True),
    )
    gains = full_gains.astype(jnp.float32)
    shifts = full_shifts.astype(jnp.float32)
    local_width = full_query.shape[1]
    head_local = local_width // HEAD_DIM
    token_count = seq_count * length
    token_full = lax.all_gather(inputs, "tp", axis=1, tiled=True)
    flat_in = token_full.reshape(token_count, features)
    query_flat = (
        jnp.dot(flat_in, full_query, preferred_element_type=jnp.float32)
        + full_bquery.astype(jnp.float32)
    ).astype(jnp.bfloat16)
    key_flat = jnp.dot(flat_in, full_key, preferred_element_type=jnp.float32).astype(jnp.bfloat16)
    value_flat = (
        jnp.dot(flat_in, full_value, preferred_element_type=jnp.float32)
        + full_bvalue.astype(jnp.float32)
    ).astype(jnp.bfloat16)
    head_shape = (seq_count, length, head_local, HEAD_DIM)
    query_heads = query_flat.reshape(head_shape)
    key_heads = key_flat.reshape(head_shape)
    value_heads = value_flat.reshape(head_shape)
    mixed_heads, summaries = attention_forward(query_heads, key_heads, value_heads, segment_ids)
    mixed_low = mixed_heads.reshape(token_count, local_width).astype(jnp.bfloat16)
    attend_part = jnp.dot(mixed_low, full_out, preferred_element_type=jnp.float32).reshape(
        seq_count, length, features
    )
    attend_all = lax.psum(attend_part.astype(jnp.bfloat16), "tp").astype(jnp.float32)
    pre_first = token_full.astype(jnp.float32) + attend_all + shifts[2]
    normed_first, unit_first, inverse_first = layer_norm_parts(pre_first, gains[0], shifts[0])
    hidden_full = normed_first.astype(jnp.bfloat16)
    normed_own = own_rows(normed_first, offset_own, piece_len)
    hidden_flat = hidden_full.reshape(token_count, features)
    up_all = jnp.dot(hidden_flat, full_up, preferred_element_type=jnp.float32) + full_bup.astype(
        jnp.float32
    )
    active = jax.nn.gelu(up_all, approximate=False).astype(jnp.bfloat16)
    down_part = jnp.dot(active, full_down, preferred_element_type=jnp.float32).reshape(
        seq_count, length, features
    )
    down_own = lax.psum_scatter(
        down_part.astype(jnp.bfloat16), "tp", scatter_dimension=1, tiled=True
    ).astype(jnp.float32)
    pre_second = normed_own + down_own + shifts[3]
    result, unit_second, inverse_second = layer_norm_parts(pre_second, gains[1], shifts[1])
    differ = result - teacher.astype(jnp.float32)
    mask_float = valid_mask.astype(jnp.float32)[..., None]
    squares, valid_count = lax.psum(
        (jnp.sum(mask_float * differ * differ), jnp.sum(mask_float)), ("fsdp", "tp")
    )
    loss_value = squares / (features * valid_count)
    grad_result = mask_float * differ * (total_tokens / valid_count)
    grad_second = norm_backward(unit_second, inverse_second, gains[1], grad_result)
    grad_down_full = lax.all_gather(grad_second.astype(jnp.bfloat16), "tp", axis=1, tiled=True)
    grad_down_flat = grad_down_full.reshape(token_count, features)
    weight_down = dot_first(active, grad_down_flat)
    grad_active = dot_last(grad_down_flat, full_down)
    gelu_back = jax.vjp(partial(jax.nn.gelu, approximate=False), up_all)[1]
    grad_up = gelu_back(grad_active)[0].astype(jnp.bfloat16)
    weight_up = dot_first(hidden_flat, grad_up)
    bias_up = jnp.sum(grad_up.astype(jnp.float32), axis=0)
    hidden_part = dot_last(grad_up, full_up).reshape(seq_count, length, features)
    current = own_rows(hidden_part, offset_own, piece_len)
    hidden_part = lax.dynamic_update_slice_in_dim(hidden_part, current + grad_second, offset_own, 1)
    grad_hidden_all = lax.psum(hidden_part.astype(jnp.bfloat16), "tp").astype(jnp.float32)
    grad_first_all = norm_backward(unit_first, inverse_first, gains[0], grad_hidden_all)
    grad_mix_full = grad_first_all.astype(jnp.bfloat16)
    grad_first_own = own_rows(grad_first_all, offset_own, piece_len)
    grad_hidden_own = own_rows(grad_hidden_all, offset_own, piece_len)
    unit_first_own = own_rows(unit_first, offset_own, piece_len)
    grad_mix_flat = grad_mix_full.reshape(token_count, features)
    weight_out = dot_first(mixed_low, grad_mix_flat)
    grad_mixed = dot_last(grad_mix_flat, full_out).astype(jnp.bfloat16).reshape(head_shape)
    grad_query, grad_key, grad_value = attention_backward(
        query_heads, key_heads, value_heads, segment_ids, summaries, grad_mixed
    )
    query_low = grad_query.astype(jnp.bfloat16).reshape(token_count, local_width)
    key_low = grad_key.astype(jnp.bfloat16).reshape(token_count, local_width)
    value_low = grad_value.astype(jnp.bfloat16).reshape(token_count, local_width)
    weight_query = dot_first(flat_in, query_low)
    weight_key = dot_first(flat_in, key_low)
    weight_value = dot_first(flat_in, value_low)
    bias_query = jnp.sum(query_low.astype(jnp.float32), axis=0)
    bias_value = jnp.sum(value_low.astype(jnp.float32), axis=0)
    input_part = (
        dot_last(query_low, full_query)
        + dot_last(key_low, full_key)
        + dot_last(value_low, full_value)
    )
    grad_inputs = (
        lax.psum_scatter(
            input_part.reshape(seq_count, length, features).astype(jnp.bfloat16),
            "tp",
            scatter_dimension=1,
            tiled=True,
        ).astype(jnp.float32)
        + grad_first_own
    )
    gain_part = jnp.stack(
        [
            jnp.sum(grad_hidden_own * unit_first_own, axis=(0, 1)),
            jnp.sum(grad_result * unit_second, axis=(0, 1)),
        ]
    )
    shift_part = jnp.stack(
        [
            jnp.sum(grad_hidden_own, axis=(0, 1)),
            jnp.sum(grad_result, axis=(0, 1)),
            jnp.sum(grad_first_own, axis=(0, 1)),
            jnp.sum(grad_second, axis=(0, 1)),
        ]
    )
    gain_sum, shift_sum = lax.psum((gain_part, shift_part), "tp")
    gradients = (
        lax.psum_scatter(
            weight_query.astype(jnp.bfloat16), "fsdp", scatter_dimension=0, tiled=True
        ).astype(jnp.float32),
        lax.psum_scatter(
            weight_key.astype(jnp.bfloat16), "fsdp", scatter_dimension=0, tiled=True
        ).astype(jnp.float32),
        lax.psum_scatter(
            weight_value.astype(jnp.bfloat16), "fsdp", scatter_dimension=0, tiled=True
        ).astype(jnp.float32),
        lax.psum_scatter(
            weight_out.astype(jnp.bfloat16), "fsdp", scatter_dimension=1, tiled=True
        ).astype(jnp.float32),
        lax.psum_scatter(
            bias_query.astype(jnp.bfloat16), "fsdp", scatter_dimension=0, tiled=True
        ).astype(jnp.float32),
        lax.psum_scatter(
            bias_value.astype(jnp.bfloat16), "fsdp", scatter_dimension=0, tiled=True
        ).astype(jnp.float32),
        lax.psum_scatter(
            weight_up.astype(jnp.bfloat16), "fsdp", scatter_dimension=0, tiled=True
        ).astype(jnp.float32),
        lax.psum_scatter(
            bias_up.astype(jnp.bfloat16), "fsdp", scatter_dimension=0, tiled=True
        ).astype(jnp.float32),
        lax.psum_scatter(
            weight_down.astype(jnp.bfloat16), "fsdp", scatter_dimension=1, tiled=True
        ).astype(jnp.float32),
        lax.psum_scatter(
            gain_sum.astype(jnp.bfloat16), "fsdp", scatter_dimension=1, tiled=True
        ).astype(jnp.float32),
        lax.psum_scatter(
            shift_sum.astype(jnp.bfloat16), "fsdp", scatter_dimension=1, tiled=True
        ).astype(jnp.float32),
    )
    return (
        result.astype(jnp.bfloat16),
        loss_value,
        grad_inputs.astype(jnp.bfloat16),
        gradients[0],
        gradients[1],
        gradients[2],
        gradients[3],
        gradients[4],
        gradients[5],
        gradients[6],
        gradients[7],
        gradients[8],
        gradients[9],
        gradients[10],
    )


BLOCK = 256
LOG2E = math.log2(math.e)
SHARD_ROWS_PARTS = 2


def rows_plan_fits(mesh):
    fsdp_count, tp_count = (mesh.shape["fsdp"], mesh.shape["tp"])
    return tp_count == 2 and fsdp_count >= 8 and fsdp_count & (fsdp_count - 1) == 0


def dot_plain(left_side, right_side):
    return lax.dot_general(
        left_side, right_side, (((1,), (0,)), ((), ())), preferred_element_type=jnp.float32
    )


def exchange(values, move):
    tp_count = lax.axis_size("tp")
    count = lax.axis_size("fsdp") * tp_count
    flip = move[0] * tp_count + move[1]
    if move[1] == 0:
        return lax.ppermute(
            values, "fsdp", [(at, at ^ move[0]) for at in range(lax.axis_size("fsdp"))]
        )
    return lax.ppermute(values, ("fsdp", "tp"), [(at, at ^ flip) for at in range(count)])


ACROSS = (0, 1)
CORE = (1, 0)
SIDE = (2, 0)


def far_moves():
    places = lax.axis_size("fsdp").bit_length() - 1
    return [(1 << place, 0) for place in range(places - 1, 1, -1)]


def gather_steps():
    far = far_moves()
    return (tuple(far) + (ACROSS, SIDE), (far[0], ACROSS, SIDE) + tuple(far[1:]))


def scatter_steps(kind):
    far = list(reversed(far_moves()))
    if kind == "late":
        return ((SIDE,), (ACROSS,), tuple(reversed(far)))
    moves = {
        "across": [ACROSS, SIDE] + far,
        "far": far[:1] + [ACROSS, SIDE] + far[1:],
        "far_side": far[:1] + [SIDE] + far[1:] + [ACROSS],
    }[kind]
    return tuple((move,) for move in moves)


def moves_of(step):
    found = [(0, 0)]
    for high, low in reversed(step):
        found = found + [(one ^ high, two ^ low) for one, two in found]
    return found


def step_masks(steps):
    masks = [(0, 0)]
    for step in steps:
        masks = [
            (high ^ one, low ^ two) for one, two in moves_of(step) for high, low in masks
        ]
    return masks


def tie(values, *others):
    return lax.optimization_barrier((values, others))[0]


class GatherChain:

    def __init__(self, parts):
        self.steps = gather_steps()
        self.held = [part[None] for part in parts]
        self.arrived = None
        self.at = 0

    def advance(self, *after):
        if self.arrived is not None:
            self.held, self.arrived = tie((self.held, self.arrived), *after)
            self.held = [
                jnp.concatenate(pair, axis=0) for pair in zip(self.held, self.arrived)
            ]
        else:
            self.held = tie(self.held, *after)
        self.arrived = [
            exchange(held, steps[self.at]) for held, steps in zip(self.held, self.steps)
        ]
        self.at += 1

    def finish(self, *after):
        if after:
            self.arrived = tie(self.arrived, *after)
        self.pieces = []
        for held, arrived in zip(self.held, self.arrived):
            near = [held, arrived]
            self.pieces.append(near + [exchange(piece, CORE) for piece in near])

    def marks(self):
        return self.held

    def sources(self):
        return [piece for part in self.pieces for piece in part]

    def places(self):
        found = []
        for part, steps in enumerate(self.steps):
            masks = step_masks([(move,) for move in steps])
            size = len(masks) // 2
            for at in range(4):
                for place, (high, low) in enumerate(masks[at % 2 * size : (at % 2 + 1) * size]):
                    flip = CORE[0] if at >= 2 else 0
                    found.append((part, part * 4 + at, place, high ^ flip, low))
        return found


def scatter_places(kinds):
    found = []
    for part, kind in enumerate(kinds):
        masks = step_masks(tuple(reversed(scatter_steps(kind))))
        for at, flip in enumerate((0, CORE[0])):
            for place, (high, low) in enumerate(masks):
                found.append((part, part * 2 + at, place, high ^ flip, low))
    return found


class ScatterChain:

    def __init__(self, kept, sent, kind):
        self.steps = scatter_steps(kind)
        self.sent = [sent]
        self.terms = [kept, exchange(sent, CORE)]
        self.size = kept.shape[0]
        self.at = 0

    def total(self, first):
        terms = [term[first : first + self.size].astype(jnp.float32) for term in self.terms]
        return sum(terms[1:], terms[0])

    def advance(self, *after):
        self.terms = tie(self.terms, *after)
        moves = moves_of(self.steps[self.at])
        self.size //= len(moves)
        self.sent = [
            self.total(at * self.size).astype(jnp.bfloat16) for at in range(1, len(moves))
        ]
        self.terms = self.terms + [
            exchange(sent, move) for sent, move in zip(self.sent, moves[1:])
        ]
        self.at += 1

    def finish(self, *after):
        self.terms = tie(self.terms, *after)
        return self.total(0)[0]

    def marks(self):
        return self.sent


def advance_all(chains, *after):
    terms = tie([chain.terms for chain in chains], *after)
    for chain, found in zip(chains, terms):
        chain.terms = found
        chain.advance()


ANYWHERE = pl.BlockSpec(memory_space=pl.ANY)
SCALARS = pl.BlockSpec(memory_space=pltpu.SMEM)
VMEM_LIMIT = 58 << 20


def cost(flops, moved, transcendentals=0):
    return pl.CostEstimate(flops=flops // 8, bytes_accessed=moved // 8, transcendentals=0)


def low_shape(*shape):
    return jax.ShapeDtypeStruct(shape, jnp.bfloat16)


def wide_shape(*shape):
    return jax.ShapeDtypeStruct(shape, jnp.float32)


def whole(*shape):
    return pl.BlockSpec(shape, lambda *step: (0,) * len(shape))


def block_span(block, count):
    reach = -(-WINDOW // BLOCK)
    return max(0, block - reach), min(count - 1, block + reach)


def split_three(values):
    high = values.astype(jnp.bfloat16)
    rest = values - high.astype(jnp.float32)
    mid = rest.astype(jnp.bfloat16)
    low = (rest - mid.astype(jnp.float32)).astype(jnp.bfloat16)
    return high, mid, low


def window_edge(tile, row_block, column_block):
    if (abs(row_block - column_block) + 1) * BLOCK - 1 < WINDOW:
        return tile
    row = lax.broadcasted_iota(jnp.int32, tile.shape, 0) + row_block * BLOCK
    column = lax.broadcasted_iota(jnp.int32, tile.shape, 1) + column_block * BLOCK
    return jnp.where(jnp.abs(row - column) < WINDOW, tile, MASKED)


def attend_kernel(seg_ref, q_ref, k_ref, v_ref, out_ref, qx_ref, kx_ref, held_ref):
    length = q_ref.shape[0]
    count = length // BLOCK
    lane = lax.broadcasted_iota(jnp.int32, (length, 128), 1)
    seg = seg_ref[...]
    q_heads, k_heads, v_heads = ([], [], [])
    for head in range(2):
        own = (lane < 64) if head == 0 else (lane >= 64)
        extra = lane - 64 if head == 0 else lane
        same = extra == seg
        q_extra = jnp.where(same, 1.0, 0.0).astype(jnp.bfloat16)
        k_extra = jnp.where(
            extra < 4, jnp.where(same, 0.0, MASKED), jnp.where(extra < 7, -1.0, 0.0)
        ).astype(jnp.bfloat16)
        v_extra = jnp.where(extra == 0, 1.0, 0.0).astype(jnp.bfloat16)
        q_heads.append(jnp.where(own, q_ref[...], q_extra))
        k_heads.append(jnp.where(own, k_ref[...], k_extra))
        v_heads.append(jnp.where(own, v_ref[...], v_extra))
        kx_ref[head] = k_heads[head]
    units = [(head, block) for head in range(2) for block in range(count)]

    def score(unit):
        head, block = unit
        low, high = block_span(block, count)
        rows = slice(block * BLOCK, (block + 1) * BLOCK)
        tile = dot_last(q_heads[head][rows], k_heads[head][low * BLOCK : (high + 1) * BLOCK])
        return [
            window_edge(tile[:, (at - low) * BLOCK : (at - low + 1) * BLOCK], block, at)
            for at in range(low, high + 1)
        ]

    def finish(unit, tiles):
        head, block = unit
        low, high = block_span(block, count)
        rows = slice(block * BLOCK, (block + 1) * BLOCK)
        most = tiles[0]
        for tile in tiles[1:]:
            most = jnp.maximum(most, tile)
        top = jnp.max(most, axis=1, keepdims=True)
        raised = jnp.concatenate(
            [jnp.exp2(tile - top).astype(jnp.bfloat16) for tile in tiles], axis=1
        )
        mixed = dot_plain(raised, v_heads[head][low * BLOCK : (high + 1) * BLOCK])
        norm_sum = mixed[:, 64:65] if head == 0 else mixed[:, 0:1]
        held_ref[head, rows, :] = mixed * (1.0 / norm_sum)
        first, second, third = split_three(top + jnp.log2(norm_sum))
        extra = lane[:BLOCK] - 64 if head == 0 else lane[:BLOCK]
        qx_ref[head, rows, :] = jnp.where(
            extra == 4,
            first,
            jnp.where(extra == 5, second, jnp.where(extra == 6, third, q_heads[head][rows])),
        )

    tiles = score(units[0])
    for at, unit in enumerate(units):
        following = score(units[at + 1]) if at + 1 < len(units) else None
        finish(unit, tiles)
        tiles = following
    out_ref[...] = jnp.where(lane < 64, held_ref[0], held_ref[1]).astype(jnp.bfloat16)


def attend(queries, keys, values, seg, first, count, earlier=None):
    length, width = queries.shape
    pair = pl.BlockSpec((length, 128), lambda step: (0, first + step))
    padded = pl.BlockSpec((2, length, 128), lambda step: (first + step, 0, 0))
    passed = 0 if earlier is None else 3
    operands = (seg, queries, keys, values) + (earlier or ())

    def kernel(seg_ref, q_ref, k_ref, v_ref, *refs):
        attend_kernel(seg_ref, q_ref, k_ref, v_ref, *refs[passed:])

    return pl.pallas_call(
        kernel,
        grid=(count,),
        in_specs=[pl.BlockSpec((length, 1), lambda step: (0, 0)), pair, pair, pair]
        + [pl.BlockSpec(memory_space=pl.ANY)] * passed,
        out_specs=[pair, padded, padded],
        out_shape=[
            jax.ShapeDtypeStruct((length, width), jnp.bfloat16),
            jax.ShapeDtypeStruct((width // HEAD_DIM, length, 128), jnp.bfloat16),
            jax.ShapeDtypeStruct((width // HEAD_DIM, length, 128), jnp.bfloat16),
        ],
        scratch_shapes=[pltpu.VMEM((2, length, 128), jnp.float32)],
        input_output_aliases={4 + at: at for at in range(passed)},
        compiler_params=pltpu.CompilerParams(vmem_limit_bytes=VMEM_LIMIT),
        cost_estimate=cost(3_500_000_000 * count, (2 << 20) * count),
        name="attend",
    )(*operands)


def attend_back_kernel(qx_ref, kx_ref, v_ref, out_ref, grad_ref, dq_ref, dk_ref, dv_ref, held_ref):
    length = v_ref.shape[0]
    count = length // BLOCK
    lane = lax.broadcasted_iota(jnp.int32, (length, 128), 1)
    grad = grad_ref[...]
    for head in range(2):
        mine = slice(head * 64, (head + 1) * 64)
        own = (lane < 64) if head == 0 else (lane >= 64)
        extra = lane - 64 if head == 0 else lane
        product = jnp.where(
            own, grad.astype(jnp.float32) * out_ref[...].astype(jnp.float32), 0.0
        )
        first, second, third = split_three(-jnp.sum(product, axis=1, keepdims=True))
        grad_head = jnp.where(
            own,
            grad,
            jnp.where(
                extra == 0,
                first,
                jnp.where(extra == 1, second, jnp.where(extra == 2, third, jnp.zeros_like(grad))),
            ),
        )
        v_head = jnp.where(own, v_ref[...], jnp.where(extra < 3, 1.0, 0.0).astype(jnp.bfloat16))
        q_head, k_head = (qx_ref[head], kx_ref[head])
        k_turned = k_head.T[mine]
        for block in range(count):
            low, high = block_span(block, count)
            keys = slice(block * BLOCK, (block + 1) * BLOCK)
            span = slice(low * BLOCK, (high + 1) * BLOCK)
            tile = dot_last(k_head[keys], q_head[span])
            soft = jnp.concatenate(
                [
                    jnp.exp2(
                        window_edge(tile[:, (at - low) * BLOCK : (at - low + 1) * BLOCK], block, at)
                    )
                    for at in range(low, high + 1)
                ],
                axis=1,
            )
            grad_soft = dot_last(v_head[keys], grad_head[span])
            grad_score = (soft * grad_soft).astype(jnp.bfloat16)
            grad_value = dot_plain(soft.astype(jnp.bfloat16), grad_head[span])
            grad_key = dot_plain(grad_score, q_head[span]) * (1.0 / LOG2E)
            dv_ref[keys, mine] = grad_value[:, mine].astype(jnp.bfloat16)
            dk_ref[keys, mine] = grad_key[:, mine].astype(jnp.bfloat16)
            grad_query = dot_plain(k_turned[:, keys], grad_score)
            if block == 0:
                held_ref[mine, span] = grad_query
                if high + 1 < count:
                    held_ref[mine, (high + 1) * BLOCK :] = jnp.zeros(
                        (64, length - (high + 1) * BLOCK), jnp.float32
                    )
            else:
                held_ref[mine, span] += grad_query
    dq_ref[...] = (held_ref[...] * (1.0 / math.sqrt(HEAD_DIM))).T.astype(jnp.bfloat16)


def attend_back(
    q_padded, k_padded, values, mixed, grad_mixed, first, count, out_first, out_count, earlier=None
):
    length, width = values.shape
    pair = pl.BlockSpec((length, 128), lambda step: (0, first + step))
    out_pair = pl.BlockSpec((length, 128), lambda step: (0, first - out_first + step))
    padded = pl.BlockSpec((2, length, 128), lambda step: (first + step, 0, 0))
    passed = 0 if earlier is None else 3
    operands = (q_padded, k_padded, values, mixed, grad_mixed) + tuple(earlier or ())

    def kernel(qx_ref, kx_ref, v_ref, out_ref, grad_ref, *refs):
        attend_back_kernel(qx_ref, kx_ref, v_ref, out_ref, grad_ref, *refs[passed:])

    return pl.pallas_call(
        kernel,
        grid=(count,),
        in_specs=[padded, padded, pair, pair, pair]
        + [pl.BlockSpec(memory_space=pl.ANY)] * passed,
        out_specs=[out_pair, out_pair, out_pair],
        out_shape=[jax.ShapeDtypeStruct((length, 128 * out_count), jnp.bfloat16)] * 3,
        scratch_shapes=[pltpu.VMEM((128, length), jnp.float32)],
        input_output_aliases={5 + at: at for at in range(passed)},
        compiler_params=pltpu.CompilerParams(vmem_limit_bytes=VMEM_LIMIT),
        cost_estimate=cost(5_000_000_000 * count, (2 << 20) * count),
        name="attend_back",
    )(*operands)


MASK_ROW = 16


def shards_kernel(
    place_ref, wq_ref, wk_ref, wv_ref, wo_ref, wu_ref, wd_ref, bq_ref, bv_ref, bu_ref, gain_ref,
    shift_ref, mask_ref, first_ref, second_ref, wide_ref, low_ref, high_ref,
):
    rows, width = wq_ref.shape
    half = width // 2
    first_ref[:, :width] = wq_ref[...]
    first_ref[:, width : width + half] = wk_ref[:, :half]
    second_ref[:, :half] = wk_ref[:, half:]
    second_ref[:, half:] = wv_ref[...]
    lane = lax.broadcasted_iota(jnp.int32, (1, 128), 1)

    def spread(ref):
        values = ref[...].astype(jnp.float32)
        size = values.shape[1]
        lanes = jnp.concatenate([values] * (128 // size), axis=1)
        return [
            jnp.where((row * 128 + lane) // size == place_ref[0], lanes, 0.0)
            for row in range(width // 128)
        ]

    def flat(ref):
        values = ref[...].astype(jnp.float32)
        return [
            jnp.concatenate([values[at : at + 1], values[at + 1 : at + 2]], axis=1)
            for at in range(0, values.shape[0], 2)
        ]

    count = jnp.sum(mask_ref[...].astype(jnp.float32))
    high = jnp.floor(count / 256.0)
    count_row = jnp.where(lane == 0, high, jnp.where(lane == 1, count - 256.0 * high, 0.0))
    lines = spread(bq_ref) + spread(bv_ref) + [bu_ref[...].astype(jnp.float32)]
    lines = lines + flat(gain_ref) + flat(shift_ref) + [count_row]
    lines = lines + [jnp.zeros((1, 128), jnp.float32)] * (MASK_ROW - len(lines))
    mask = mask_ref[...].astype(jnp.float32)
    for row in range(mask.shape[0]):
        lines = lines + [
            mask[row : row + 1, at : at + 128] for at in range(0, mask.shape[1], 128)
        ]
    lines = lines + [jnp.zeros((1, 128), jnp.float32)] * (rows - len(lines))
    first_ref[:, width + half :] = jnp.concatenate(lines, axis=0).astype(jnp.bfloat16)
    wide_ref[:, : wu_ref.shape[1]] = wu_ref[...]
    wide_ref[:, wu_ref.shape[1] :] = wo_ref[...]
    cut = low_ref.shape[1]
    low_ref[...] = wd_ref[:, :cut]
    high_ref[...] = wd_ref[:, cut:]


def shards(place, w_query, w_key, w_value, w_out, w_up, w_down, small):
    rows, width = w_query.shape
    hidden = w_up.shape[1]
    operands = (w_query, w_key, w_value, w_out, w_up, w_down) + small
    outs = [
        low_shape(rows, width + width // 2 + 128),
        low_shape(rows, width // 2 + width),
        low_shape(rows, hidden + width),
        low_shape(rows, hidden // 2),
        low_shape(rows, hidden // 2),
    ]
    return pl.pallas_call(
        shards_kernel,
        in_specs=[SCALARS] + [whole(*operand.shape) for operand in operands],
        out_specs=[whole(*out.shape) for out in outs],
        out_shape=outs,
        compiler_params=pltpu.CompilerParams(vmem_limit_bytes=VMEM_LIMIT),
        cost_estimate=cost(0, 2 << 20),
        name="shards",
    )(place, *operands)


def qkv_kernel(spans, places, place_ref, row_ref, *refs):
    count = 1 + max(source for _, source, _, _, _ in places)
    sources = refs[:count]
    q_ref, k_ref, v_ref, full_ref, small_out, held, small, sems, out_sem = refs[count:]
    me_fsdp, me_tp = (place_ref[0], place_ref[1])
    rows = sources[0].shape[1]
    width = q_ref.shape[1]
    fsdp_count = held.shape[0] // rows
    copies = {0: [], 1: [], 2: [], 3: []}
    for part, source, place, high, low in places:
        fsdp, tp = (me_fsdp ^ high, me_tp ^ low)
        for start, size, target, per_tp, column in spans[part]:
            if target == 3:
                from_ref = sources[source].at[place, pl.ds(0, small.shape[1]), pl.ds(start, size)]
                to_ref = small.at[tp * fsdp_count + fsdp]
            else:
                row = pl.multiple_of(fsdp * rows, rows)
                lane = pl.multiple_of(tp * per_tp + column, 128)
                from_ref = sources[source].at[place, :, pl.ds(start, size)]
                to_ref = held.at[pl.ds(row, rows), pl.ds(lane, size)]
            total = sum(len(group) for group in copies.values())
            copies[target].append(pltpu.make_async_copy(from_ref, to_ref, sems.at[total]))
            copies[target][-1].start()

    def bias(first):
        halves = [
            jnp.sum(
                small[tp * fsdp_count : (tp + 1) * fsdp_count].astype(jnp.float32), axis=0
            )
            for tp in range(2)
        ]
        count = width // 256
        lanes = [
            half[first + at : first + at + 1]
            for group in (range(count - 1), (count - 1,))
            for half in halves
            for at in group
        ]
        return jnp.concatenate(lanes, axis=1)

    scale = LOG2E / math.sqrt(HEAD_DIM)
    for copy in copies[3]:
        copy.wait()
    out_copies = [pltpu.make_async_copy(small, small_out, out_sem.at[3])]
    out_copies[0].start()
    for target, out_ref in ((0, q_ref), (1, k_ref), (2, v_ref)):
        for copy in copies[target]:
            copy.wait()
        span = pl.ds(target * width, width)
        out_copies.append(
            pltpu.make_async_copy(held.at[:, span], full_ref.at[:, span], out_sem.at[target])
        )
        out_copies[-1].start()
        added = bias(0 if target == 0 else width // 256) if target != 1 else None
        for block in range(row_ref.shape[0] // BLOCK):
            lines = slice(block * BLOCK, (block + 1) * BLOCK)
            found = dot_plain(row_ref[lines], held[:, target * width : (target + 1) * width])
            if added is not None:
                found = found + added
            if target == 0:
                found = found * scale
            out_ref[lines] = found.astype(jnp.bfloat16)
    for copy in out_copies:
        copy.wait()


def qkv_project(chain, spans, place, row_low, width, small_rows):
    length, features = row_low.shape
    sources = chain.sources()
    places = chain.places()
    devices = lax.axis_size("fsdp") * lax.axis_size("tp")
    copies = sum(len(spans[entry[0]]) for entry in places)
    return pl.pallas_call(
        partial(qkv_kernel, spans, places),
        in_specs=[SCALARS, whole(length, features)] + [ANYWHERE] * len(sources),
        out_specs=[whole(length, width)] * 3 + [ANYWHERE] * 2,
        out_shape=[low_shape(length, width)] * 3
        + [low_shape(features, 3 * width), low_shape(devices, small_rows, 128)],
        scratch_shapes=[
            pltpu.VMEM((features, 3 * width), jnp.bfloat16),
            pltpu.VMEM((devices, small_rows, 128), jnp.bfloat16),
            pltpu.SemaphoreType.DMA((copies,)),
            pltpu.SemaphoreType.DMA((4,)),
        ],
        compiler_params=pltpu.CompilerParams(vmem_limit_bytes=VMEM_LIMIT),
        cost_estimate=cost(6 * length * features * width, 24 << 20),
        name="qkv_project",
    )(place, row_low, *sources)


def unit_of(values):
    centred = values - jnp.mean(values, axis=-1, keepdims=True)
    inverse = lax.rsqrt(jnp.mean(centred * centred, axis=-1, keepdims=True) + EPSILON)
    return centred * inverse, inverse


def out_up_kernel(
    mixed_ref, row_ref, out_w_ref, up_w_ref, vector_ref, b_ref,
    active_ref, slope_ref, unit_ref, inverse_ref, hidden_ref, full_out_ref,
):
    length, features = row_ref.shape
    late = out_w_ref.shape[3] // 4
    early = 3 * late

    @pl.when(pl.program_id(0) == 0)
    def _():
        for tp in range(2):
            lanes = pl.ds(tp * early, early)
            full_out_ref[:, lanes] = out_w_ref[:, tp, :, :early].reshape(features, early)
            lanes = pl.ds(2 * early + tp * late, late)
            full_out_ref[:, lanes] = out_w_ref[:, tp, :, early:].reshape(features, late)
        for block in range(length // BLOCK):
            lines = slice(block * BLOCK, (block + 1) * BLOCK)
            before = (
                row_ref[lines].astype(jnp.float32)
                + dot_last(mixed_ref[lines], full_out_ref[...])
                + vector_ref[0:1]
            )
            unit, inverse = unit_of(before)
            unit_ref[lines] = unit
            inverse_ref[lines] = inverse
            hidden_ref[lines] = (unit * vector_ref[1:2] + vector_ref[2:3]).astype(jnp.bfloat16)

    weight = up_w_ref[:, 0].reshape(features, up_w_ref.shape[3])

    def product(block):
        lines = slice(block * BLOCK, (block + 1) * BLOCK)
        return dot_plain(hidden_ref[lines], weight) + b_ref[...]

    up = product(0)
    count = length // BLOCK
    for block in range(count):
        following = product(block + 1) if block + 1 < count else None
        lines = slice(block * BLOCK, (block + 1) * BLOCK)
        cumulative = 0.5 * (1.0 + lax.erf(up * math.sqrt(0.5)))
        density = jnp.exp2(up * up * (-0.5 * LOG2E)) * (1.0 / math.sqrt(2.0 * math.pi))
        active_ref[lines] = (up * cumulative).astype(jnp.bfloat16)
        slope_ref[lines] = (cumulative + up * density).astype(jnp.bfloat16)
        up = following


def out_up_project(mixed, row_low, gathered, vectors, bias, local_hidden, local_width):
    length, features = row_low.shape
    fsdp_count, tp_count, rows, _ = gathered.shape
    hidden_units = local_hidden * tp_count
    block_width = math.gcd(math.gcd(local_hidden, 512), local_width)
    each = local_hidden // block_width
    column = pl.BlockSpec((length, block_width), lambda step: (0, step))
    return pl.pallas_call(
        out_up_kernel,
        grid=(hidden_units // block_width,),
        in_specs=[
            whole(length, features),
            whole(length, features),
            pl.BlockSpec(
                (fsdp_count, tp_count, rows, local_width),
                lambda step: (0, 0, 0, local_hidden // local_width),
            ),
            pl.BlockSpec(
                (fsdp_count, 1, rows, block_width),
                lambda step: (0, step // each, 0, step % each),
            ),
            whole(*vectors.shape),
            pl.BlockSpec((1, block_width), lambda step: (0, step)),
        ],
        out_specs=[column, column]
        + [whole(length, features), whole(length, 1), whole(length, features)]
        + [whole(features, features)],
        out_shape=[
            low_shape(length, hidden_units),
            low_shape(length, hidden_units),
            wide_shape(length, features),
            wide_shape(length, 1),
            low_shape(length, features),
            low_shape(features, features),
        ],
        compiler_params=pltpu.CompilerParams(vmem_limit_bytes=VMEM_LIMIT),
        cost_estimate=cost(
            2 * length * features * (hidden_units + features),
            36 << 20,
            2 * length * hidden_units,
        ),
        name="out_up_project",
    )(mixed, row_low, gathered, gathered, vectors, bias)


def down_kernel(
    places, place_ref, active_ref, unit_ref, teacher_ref, weight_ref, vector_ref, *refs
):
    count = 1 + max(source for _, source, _, _, _ in places)
    sources = refs[:count]
    out_ref, grad_ref, low_ref, sums_ref, full_ref, held, sems, out_sem = refs[count:]
    rows = sources[0].shape[1]
    part_width = sources[0].shape[2]
    step = pl.program_id(0)
    last = pl.num_programs(0) - 1
    full_copy = pltpu.make_async_copy(held, full_ref, out_sem)

    @pl.when(step == 0)
    def _():
        me_fsdp, me_tp = (place_ref[0], place_ref[1])
        copies = []
        for at, (part, source, place, high, low) in enumerate(places):
            row = pl.multiple_of((me_fsdp ^ high) * rows, rows)
            lane = (me_tp ^ low) * (2 * part_width) + part * part_width
            lane = pl.multiple_of(lane, 128)
            copies.append(
                pltpu.make_async_copy(
                    sources[source].at[place],
                    held.at[pl.ds(row, rows), pl.ds(lane, part_width)],
                    sems.at[at],
                )
            )
            copies[-1].start()
        for copy in copies:
            copy.wait()
        full_copy.start()
        sums_ref[...] = jnp.zeros_like(sums_ref)

    normed_first = unit_ref[...] * vector_ref[0:1] + vector_ref[1:2]
    before = normed_first + dot_last(active_ref[...], held[...]) + vector_ref[2:3]
    unit, inverse = unit_of(before)
    gain = vector_ref[3:4]
    result = unit * gain + vector_ref[4:5]
    out_ref[...] = result.astype(jnp.bfloat16)
    differ = result - teacher_ref[...].astype(jnp.float32)
    grad = differ * weight_ref[...]
    scaled = grad * gain
    grad_before = inverse * (
        scaled
        - jnp.mean(scaled, axis=-1, keepdims=True)
        - unit * jnp.mean(scaled * unit, axis=-1, keepdims=True)
    )
    grad_ref[...] = grad_before
    low_ref[...] = grad_before.astype(jnp.bfloat16)
    for at, term in enumerate((grad * unit, grad, grad_before, grad * differ)):
        sums_ref[at : at + 1] += jnp.sum(term, axis=0, keepdims=True)

    @pl.when(step == last)
    def _():
        full_copy.wait()


def down_project(chain, place, active, unit, teacher, weight, vectors):
    length, hidden_units = active.shape
    features = unit.shape[1]
    sources, places = (chain.sources(), chain.places())
    line = lambda width: pl.BlockSpec((BLOCK, width), lambda step: (step, 0))
    return pl.pallas_call(
        partial(down_kernel, places),
        grid=(length // BLOCK,),
        in_specs=[SCALARS, line(hidden_units), line(features), line(features), line(1)]
        + [whole(*vectors.shape)]
        + [ANYWHERE] * len(sources),
        out_specs=[line(features), line(features), line(features), whole(8, features), ANYWHERE],
        out_shape=[
            low_shape(length, features),
            wide_shape(length, features),
            low_shape(length, features),
            wide_shape(8, features),
            low_shape(features, hidden_units),
        ],
        scratch_shapes=[
            pltpu.VMEM((features, hidden_units), jnp.bfloat16),
            pltpu.SemaphoreType.DMA((len(places),)),
            pltpu.SemaphoreType.DMA,
        ],
        compiler_params=pltpu.CompilerParams(vmem_limit_bytes=VMEM_LIMIT),
        cost_estimate=cost(2 * length * features * hidden_units, 36 << 20),
        name="down_project",
    )(place, active, unit, teacher, weight, vectors, *sources)


def column_copies(places, tp_places, each, block_width, me_fsdp, held, pieces, sems, at):
    rows = pieces[0].shape[1]
    found = []
    for number, (_, output, place, high, low) in enumerate(places):
        if low:
            continue
        row = pl.multiple_of((me_fsdp ^ high) * rows, rows)
        lane = pl.multiple_of(at % each * block_width, 128)
        found.append(
            pltpu.make_async_copy(
                held.at[at, pl.ds(row, rows)],
                pieces[output].at[place + at // each * tp_places, :, pl.ds(lane, block_width)],
                sems.at[at, number],
            )
        )
    return found


def down_back_kernel(
    places, tp_places, each, place_ref, grad_ref, active_ref, kept_ref, sent_ref,
    turned, held, sems,
):
    step = pl.program_id(0)

    @pl.when(step == 0)
    def _():
        turned[...] = grad_ref[...].T

    copies = partial(
        column_copies, places, tp_places, each, active_ref.shape[1], place_ref[0], held,
        (kept_ref, sent_ref), sems,
    )
    held[step] = dot_plain(turned[...], active_ref[...]).astype(jnp.bfloat16)
    for copy in copies(step):
        copy.start()

    @pl.when(step == 2 * each - 1)
    def _():
        for at in range(2 * each):
            for copy in copies(at):
                copy.wait()


def up_back_kernel(
    places, tp_places, each, place_ref, grad_ref, hidden_ref, slope_ref, down_ref, up_ref,
    total_ref, bias_ref, kept_ref, sent_ref, turned, held, sems,
):
    step = pl.program_id(0)
    length, features = grad_ref.shape
    block_width = slope_ref.shape[1]

    @pl.when(step == 0)
    def _():
        turned[...] = hidden_ref[...].T
        total_ref[...] = jnp.zeros_like(total_ref)

    copies = partial(
        column_copies, places, tp_places, each, block_width, place_ref[0], held,
        (kept_ref, sent_ref), sems,
    )
    down_weight = down_ref[...]
    up_weight = up_ref[:, 0].reshape(features, block_width)
    spans = [slice(at * BLOCK, (at + 1) * BLOCK) for at in range(length // BLOCK)]
    grads, bias = ([], jnp.zeros((1, block_width), jnp.float32))
    found = dot_plain(grad_ref[spans[0]], down_weight)
    for at, span in enumerate(spans):
        following = (
            dot_plain(grad_ref[spans[at + 1]], down_weight) if at + 1 < len(spans) else None
        )
        grad_up = found * slope_ref[span].astype(jnp.float32)
        bias = bias + jnp.sum(grad_up, axis=0, keepdims=True)
        grads.append(grad_up.astype(jnp.bfloat16))
        found = following
    bias_ref[...] = bias
    grad_up = jnp.concatenate(grads, axis=0)
    held[step] = dot_plain(turned[...], grad_up).astype(jnp.bfloat16)
    for copy in copies(step):
        copy.start()
    total_ref[...] += dot_last(grad_up, up_weight)

    @pl.when(step == 2 * each - 1)
    def _():
        for at in range(2 * each):
            for copy in copies(at):
                copy.wait()


def column_plan(kind, local_hidden):
    block_width = math.gcd(local_hidden, 512)
    each = local_hidden // block_width
    places = scatter_places([kind])
    tp_places = next(place for _, at, place, high, low in places if at == 0 and low and not high)

    def column(step, where):
        return (where[1] ^ (step // each)) * each + step % each

    return block_width, each, places, tp_places, column


def keep(*shape):
    return pl.BlockSpec(shape, lambda step, where: (0,) * len(shape))


def column_scratch(features, length, each, block_width, places):
    return [
        pltpu.VMEM((features, length), jnp.bfloat16),
        pltpu.VMEM((2 * each, features, block_width), jnp.bfloat16),
        pltpu.SemaphoreType.DMA((2 * each, len(places))),
    ]


def down_back(place, grad_down, active, rows, local_hidden, kind):
    length, features = grad_down.shape
    block_width, each, places, tp_places, column = column_plan(kind, local_hidden)
    piece = low_shape(len(places) // 2, rows, local_hidden)
    return pl.pallas_call(
        partial(down_back_kernel, places, tp_places, each),
        grid_spec=pltpu.PrefetchScalarGridSpec(
            num_scalar_prefetch=1,
            grid=(2 * each,),
            in_specs=[
                keep(length, features),
                pl.BlockSpec((length, block_width), lambda step, where: (0, column(step, where))),
            ],
            out_specs=[ANYWHERE] * 2,
            scratch_shapes=column_scratch(features, length, each, block_width, places),
        ),
        out_shape=[piece] * 2,
        compiler_params=pltpu.CompilerParams(vmem_limit_bytes=VMEM_LIMIT),
        cost_estimate=cost(4 * length * features * local_hidden, 20 << 20),
        name="down_back",
    )(place, grad_down, active)


def up_back(place, grad_down, hidden, slope, full_down, gathered, kind):
    length, features = hidden.shape
    fsdp_count, tp_count, rows, _ = gathered.shape
    local_hidden = full_down.shape[1] // tp_count
    block_width, each, places, tp_places, column = column_plan(kind, local_hidden)
    piece = low_shape(len(places) // 2, rows, local_hidden)
    block = pl.BlockSpec((length, block_width), lambda step, where: (0, column(step, where)))
    return pl.pallas_call(
        partial(up_back_kernel, places, tp_places, each),
        grid_spec=pltpu.PrefetchScalarGridSpec(
            num_scalar_prefetch=1,
            grid=(2 * each,),
            in_specs=[
                keep(length, features),
                keep(length, features),
                block,
                pl.BlockSpec((features, block_width), lambda step, where: (0, column(step, where))),
                pl.BlockSpec(
                    (fsdp_count, 1, rows, block_width),
                    lambda step, where: (0, where[1] ^ (step // each), 0, step % each),
                ),
            ],
            out_specs=[
                keep(length, features),
                pl.BlockSpec((1, block_width), lambda step, where: (0, column(step, where))),
            ]
            + [ANYWHERE] * 2,
            scratch_shapes=column_scratch(features, length, each, block_width, places),
        ),
        out_shape=[wide_shape(length, features), wide_shape(1, local_hidden * tp_count)]
        + [piece] * 2,
        compiler_params=pltpu.CompilerParams(vmem_limit_bytes=VMEM_LIMIT),
        cost_estimate=cost(12 * length * features * local_hidden, 40 << 20),
        name="up_back",
    )(place, grad_down, hidden, slope, full_down, gathered)


def norm_back_kernel(
    base_ref, grad_ref, unit_ref, inverse_ref, gain_ref, weight_ref, first_ref, low_ref, mixed_ref, sums_ref
):
    @pl.when(pl.program_id(0) == 0)
    def _():
        sums_ref[...] = jnp.zeros_like(sums_ref)

    grad, unit = (base_ref[...] + grad_ref[...], unit_ref[...])
    scaled = grad * gain_ref[...]
    found = inverse_ref[...] * (
        scaled
        - jnp.mean(scaled, axis=-1, keepdims=True)
        - unit * jnp.mean(scaled * unit, axis=-1, keepdims=True)
    )
    first_ref[...] = found
    low = found.astype(jnp.bfloat16)
    low_ref[...] = low
    mixed_ref[...] = dot_plain(low, weight_ref[...]).astype(jnp.bfloat16)
    for at, term in enumerate((grad * unit, grad, found)):
        sums_ref[at : at + 1] += jnp.sum(term, axis=0, keepdims=True)


def norm_back(grad_second, grad_hidden, unit, inverse, gain, full_out):
    length, features = unit.shape
    line = lambda width: pl.BlockSpec((BLOCK, width), lambda step: (step, 0))
    return pl.pallas_call(
        norm_back_kernel,
        grid=(length // BLOCK,),
        in_specs=[line(features)] * 3 + [line(1), whole(1, features)]
        + [whole(*full_out.shape)],
        out_specs=[line(features), line(features), line(full_out.shape[1]), whole(8, features)],
        out_shape=[
            wide_shape(length, features),
            low_shape(length, features),
            low_shape(length, full_out.shape[1]),
            wide_shape(8, features),
        ],
        compiler_params=pltpu.CompilerParams(vmem_limit_bytes=VMEM_LIMIT),
        cost_estimate=cost(2 * length * features * features, 22 << 20),
        name="norm_back",
    )(grad_second, grad_hidden, unit, inverse, gain, full_out)


def weight_grad_kernel(products, spans, places, extra, place_ref, *refs):
    lefts = 1 + max(left for left, _ in products)
    rights = 1 + max(right for _, right in products)
    left_refs, right_refs = (refs[:lefts], refs[lefts : lefts + rights])
    refs = refs[lefts + rights :]
    if extra:
        extra_ref, refs = (refs[0], refs[1:])
    parts = 2 * len(spans)
    pieces, scratch = (refs[:parts], refs[parts:])
    turned, held, sems = (scratch[:lefts], scratch[lefts:-1], scratch[-1])
    me_fsdp, me_tp = (place_ref[0], place_ref[1])
    rows = pieces[0].shape[1]
    started = []

    def start(target):
        for part, output, place, high, low in places:
            fsdp, tp = (me_fsdp ^ high, me_tp ^ low)
            for begin, size, which, per_tp, column in spans[part]:
                if which != target:
                    continue
                if target == len(products):
                    fsdp_count = extra_ref.shape[0] // 2
                    from_ref = extra_ref.at[tp * fsdp_count + fsdp]
                    row_span = pl.ds(0, extra_ref.shape[1])
                else:
                    row = pl.multiple_of(fsdp * rows, rows)
                    lane = pl.multiple_of(tp * per_tp + column, 128)
                    from_ref = held[target].at[pl.ds(row, rows), pl.ds(lane, size)]
                    row_span = pl.ds(0, rows)
                copy = pltpu.make_async_copy(
                    from_ref,
                    pieces[output].at[place, row_span, pl.ds(begin, size)],
                    sems.at[len(started)],
                )
                copy.start()
                started.append(copy)

    if extra:
        start(len(products))
    for at, left in enumerate(left_refs):
        turned[at][...] = left[...].T
    for target, (left, right) in enumerate(products):
        features = held[target].shape[0]
        for block in range(features // BLOCK):
            lines = slice(block * BLOCK, (block + 1) * BLOCK)
            held[target][lines] = dot_plain(turned[left][lines], right_refs[right][...]).astype(
                jnp.bfloat16
            )
        start(target)
    for copy in started:
        copy.wait()


def weight_grads(place, lefts, rights, products, spans, kinds, rows, part_widths, extra=None):
    length, features = lefts[0].shape
    places = scatter_places(kinds)
    copies = sum(len(spans[entry[0]]) for entry in places)
    devices = lax.axis_size("fsdp") * lax.axis_size("tp")
    outs = [low_shape(devices // 2, rows, part_widths[at // 2]) for at in range(2 * len(spans))]
    operands = list(lefts) + list(rights) + ([] if extra is None else [extra])
    flops = sum(2 * length * features * rights[right].shape[1] for _, right in products)
    return pl.pallas_call(
        partial(weight_grad_kernel, products, spans, places, extra is not None),
        in_specs=[SCALARS] + [whole(*operand.shape) for operand in operands],
        out_specs=[ANYWHERE] * len(outs),
        out_shape=outs,
        scratch_shapes=[pltpu.VMEM((features, length), jnp.bfloat16) for _ in lefts]
        + [pltpu.VMEM((features, rights[right].shape[1]), jnp.bfloat16) for _, right in products]
        + [pltpu.SemaphoreType.DMA((copies,))],
        compiler_params=pltpu.CompilerParams(vmem_limit_bytes=VMEM_LIMIT),
        cost_estimate=cost(flops, 16 << 20),
        name="weight_grads",
    )(place, *operands)


def input_grad_kernel(flip, place_ref, base_ref, *refs):
    grads, weight_ref, out_ref = (refs[:-2], refs[-2], refs[-1])
    total = base_ref[...]
    at = 0
    for grad in grads:
        width = grad.shape[1]
        total = total + dot_last(grad[...], weight_ref[:, at : at + width])
        at += width
    out_ref[...] = total.astype(jnp.bfloat16)


def input_grad(place, base, grads, full_qkv, flip):
    length, features = base.shape
    half = length // 2
    each = half // BLOCK
    line = lambda width: pl.BlockSpec(
        (BLOCK, width), lambda step, where: ((where[1] ^ flip) * each + step, 0)
    )
    return pl.pallas_call(
        partial(input_grad_kernel, flip),
        grid_spec=pltpu.PrefetchScalarGridSpec(
            num_scalar_prefetch=1,
            grid=(each,),
            in_specs=[line(features)]
            + [line(grad.shape[1]) for grad in grads]
            + [pl.BlockSpec(full_qkv.shape, lambda step, where: (0, 0))],
            out_specs=pl.BlockSpec((BLOCK, features), lambda step, where: (step, 0)),
        ),
        out_shape=low_shape(half, features),
        compiler_params=pltpu.CompilerParams(vmem_limit_bytes=VMEM_LIMIT),
        cost_estimate=cost(2 * half * features * full_qkv.shape[1], 14 << 20),
        name="input_grad",
    )(place, base, *grads, full_qkv)


def swap_in(pieces, tp_rank, *after):
    mine = lax.dynamic_index_in_dim(pieces, tp_rank, 0, keepdims=False)
    theirs = lax.dynamic_index_in_dim(pieces, 1 - tp_rank, 0, keepdims=False)
    if after:
        theirs = tie(theirs, *after)
    arrived = exchange(theirs, ACROSS)
    first = tp_rank == 0
    return jnp.concatenate(
        [jnp.where(first, mine, arrived), jnp.where(first, arrived, mine)], axis=0
    )


def both_rows(mine, arrived, tp_rank):
    first = tp_rank == 0
    return jnp.stack([jnp.where(first, mine, arrived), jnp.where(first, arrived, mine)])


def on_device_rows(
    inputs,
    segment_ids,
    valid_mask,
    teacher,
    w_query,
    w_key,
    w_value,
    w_out,
    b_query,
    b_value,
    w_up,
    b_up,
    w_down,
    ln_gains,
    ln_shifts,
):
    seq_count, piece_len, features = inputs.shape
    fsdp_count, tp_count = (lax.axis_size("fsdp"), lax.axis_size("tp"))
    fsdp_rank, tp_rank = (lax.axis_index("fsdp"), lax.axis_index("tp"))
    devices = fsdp_count * tp_count
    assert seq_count == tp_count
    total_tokens = seq_count * piece_len * tp_count * fsdp_count
    shard_rows, local_width = w_query.shape
    local_hidden = w_up.shape[1]
    width = local_width * tp_count
    late_width = local_width // 4
    early_width = 3 * late_width
    half = local_width // 2
    pairs = width // 128
    late_pairs = pairs // 4
    early_pairs = pairs - late_pairs
    place = jnp.stack([fsdp_rank, tp_rank]).astype(jnp.int32)

    late_at = 2 * early_width
    qkv_spans = [
        [
            (0, early_width, 0, early_width, 0),
            (early_width, late_width, 0, late_width, late_at),
            (local_width, half, 1, early_width, width),
            (local_width + half, 128, 3, 0, 0),
        ],
        [
            (0, early_width - half, 1, early_width, width + half),
            (early_width - half, late_width, 1, late_width, width + late_at),
            (half, early_width, 2, early_width, 2 * width),
            (half + early_width, late_width, 2, late_width, 2 * width + late_at),
        ],
    ]
    small_rows = 32
    small = (
        b_query[None],
        b_value[None],
        b_up[None],
        ln_gains,
        ln_shifts,
        valid_mask,
    )
    up_cut = (local_hidden + local_width) // 2
    up_rest = local_hidden - up_cut
    up_spans = [
        [(0, up_cut, 0, local_hidden, 0)],
        [
            (0, up_rest, 0, local_hidden, up_cut),
            (up_rest, early_width, 1, early_width, 0),
            (up_rest + early_width, late_width, 1, late_width, late_at),
        ],
    ]
    qkv_first, qkv_second, up_shard, down_first, down_second = shards(
        place, w_query, w_key, w_value, w_out.T, w_up, w_down.T, small
    )
    chain_qkv = GatherChain([qkv_first, qkv_second])
    chain_down = GatherChain([down_first, down_second])
    row_low = swap_in(inputs, tp_rank)
    seg = lax.dynamic_index_in_dim(segment_ids, tp_rank, 0, keepdims=False)[:, None]
    chain_qkv.advance()
    chain_qkv.advance()
    chain_qkv.advance(row_low)
    chain_qkv.advance()
    gathered = lax.all_gather(
        tie(up_shard, chain_qkv.marks()), ("fsdp", "tp"), axis=0, tiled=False
    ).reshape(fsdp_count, tp_count, shard_rows, local_hidden + local_width)
    chain_qkv.finish()
    chain_down.advance(chain_qkv.arrived)
    queries, keys, values, full_qkv, small_all = qkv_project(
        chain_qkv, qkv_spans, tie(place, chain_down.marks()), row_low, width, small_rows
    )
    valid_row = (
        lax.dynamic_slice(
            small_all.reshape(tp_count, fsdp_count, small_rows, 128),
            (0, fsdp_rank, MASK_ROW + tp_rank * (piece_len // 128), 0),
            (tp_count, 1, piece_len // 128, 128),
        )
        .reshape(-1)
        .astype(jnp.float32)
    )
    small_all = small_all.astype(jnp.float32)
    small_at = 2 * (local_width // 128)
    bias_up = small_all[:, small_at].reshape(1, -1)

    def feature_rows(columns, rows):
        return (
            columns[:fsdp_count]
            .reshape(fsdp_count, rows, features // fsdp_count)
            .transpose(1, 0, 2)
            .reshape(rows, features)
        )

    gains = feature_rows(small_all[:, small_at + 1], 2)
    shifts = feature_rows(small_all[:, small_at + 2 : small_at + 4], 4)
    valid_count = jnp.sum(small_all[:, small_at + 4, 0] * 256.0 + small_all[:, small_at + 4, 1])

    chain_down.advance(queries)
    queries = tie(queries, chain_down.marks())
    attended = attend(queries, keys, values, seg, 0, pairs // 2)
    chain_down.advance(attended)
    mixed, q_padded, k_padded = attend(
        queries, keys, tie(values, chain_down.marks()), seg, pairs // 2, pairs // 2, attended
    )
    teacher_row = swap_in(teacher, tp_rank, attended)
    chain_down.advance(mixed)
    vectors = jnp.stack([shifts[2], gains[0], shifts[0]])
    active, slope, unit_first, inverse_first, hidden_low, full_out = out_up_project(
        tie(mixed, chain_down.marks()),
        row_low,
        gathered,
        vectors,
        bias_up,
        local_hidden,
        local_width,
    )
    chain_down.finish(active)
    weight = (valid_row * (total_tokens / valid_count))[:, None]
    vectors = jnp.stack([gains[0], shifts[0], shifts[3], gains[1], shifts[1]])
    result_low, grad_second, grad_down, sums_second, full_down = down_project(
        chain_down, place, active, unit_first, teacher_row, weight, vectors
    )

    chain_down = ScatterChain(
        *down_back(place, grad_down, active, shard_rows, local_hidden, "across"), "across"
    )
    grad_hidden, grad_b_up, kept, sent = up_back(
        place, tie(grad_down, chain_down.marks()), hidden_low, slope, full_down, gathered, "far"
    )
    chain_up = ScatterChain(kept, sent, "far")
    chain_down.advance(grad_hidden)
    grad_first, grad_attend, grad_mixed, sums_first = norm_back(
        grad_second, tie(grad_hidden, chain_down.marks(), chain_up.marks()), unit_first, inverse_first, gains[:1], full_out
    )
    mine = lax.dynamic_slice_in_dim(result_low, tp_rank * piece_len, piece_len, 0)
    theirs = lax.dynamic_slice_in_dim(result_low, (1 - tp_rank) * piece_len, piece_len, 0)
    back = partial(attend_back, q_padded, k_padded, values, mixed)
    chain_up.advance(grad_mixed)
    early_grads = back(tie(grad_mixed, chain_up.marks()), 0, early_pairs // 2, 0, early_pairs)
    early_grads = back(
        grad_mixed, early_pairs // 2, early_pairs // 2, 0, early_pairs, early_grads
    )
    chain_down.advance(early_grads)
    early_spans = [
        [
            (0, early_width, 0, early_width, 0),
            (early_width, late_width, 0, late_width, late_at),
            (local_width, early_width, 1, early_width, 0),
        ],
        [(0, early_width, 2, early_width, 0), (early_width, early_width, 3, early_width, 0)],
    ]
    early_first = local_width + early_width
    early_kinds = ["across", "far_side"]
    pieces = weight_grads(
        place,
        [grad_attend, tie(row_low, chain_down.marks())],
        [mixed] + list(early_grads),
        [(0, 0), (1, 1), (1, 2), (1, 3)],
        early_spans,
        early_kinds,
        shard_rows,
        [early_first, 2 * early_width],
    )
    early_chains = [
        ScatterChain(pieces[2 * at], pieces[2 * at + 1], kind)
        for at, kind in enumerate(early_kinds)
    ]
    chain_up.advance(pieces)
    chain_down.advance(pieces)
    arrived_out = exchange(tie(theirs, grad_mixed), ACROSS)
    late_grads = back(
        tie(grad_mixed, chain_up.marks(), chain_down.marks(), arrived_out),
        early_pairs,
        late_pairs,
        early_pairs,
        late_pairs,
    )
    advance_all([chain_up, chain_down] + early_chains, late_grads)
    def feature_pieces(rows):
        pieces = rows.reshape(rows.shape[0], fsdp_count, -1).transpose(1, 0, 2)
        pieces = pieces.reshape(fsdp_count, -1, 128)
        return jnp.concatenate([pieces] * tp_count, axis=0)

    def bias_pieces(early, late):
        sums = [
            jnp.sum(part.astype(jnp.float32), axis=0).reshape(tp_count, -1) for part in (early, late)
        ]
        return jnp.concatenate(sums, axis=1).reshape(devices, -1)

    bias_pair = jnp.concatenate(
        [bias_pieces(early_grads[0], late_grads[0]), bias_pieces(early_grads[2], late_grads[2])],
        axis=1,
    )
    bias_pair = jnp.pad(bias_pair, ((0, 0), (0, 128 - bias_pair.shape[1])))
    squares = jnp.sum(sums_second[3]) * (valid_count / total_tokens)
    lane = lax.broadcasted_iota(jnp.int32, (1, 128), 1)
    square_rows = jnp.concatenate(
        [
            jnp.where(lane == tp_rank * fsdp_count + fsdp_rank, term.astype(jnp.float32), 0.0)
            for term in split_three(squares)
        ],
        axis=0,
    )
    small = jnp.concatenate(
        [
            bias_pair[:, None],
            grad_b_up.reshape(devices, 1, 128),
            feature_pieces(
                jnp.stack(
                    [
                        sums_first[0],
                        sums_second[0],
                        sums_first[1],
                        sums_second[1],
                        sums_first[2],
                        sums_second[2],
                    ]
                )
            ),
            jnp.broadcast_to(square_rows[None], (devices, 3, 128)),
        ],
        axis=1,
    )
    small = jnp.pad(small, ((0, 0), (0, 16 - small.shape[1]), (0, 0)))
    late_spans = [
        [(at * late_width, late_width, at, late_width, 0) for at in range(3)]
        + [(3 * late_width, 128, 3, 0, 0)]
    ]
    chain_late = ScatterChain(
        *weight_grads(
            place,
            [
                tie(
                    row_low,
                    chain_up.marks(),
                    chain_down.marks(),
                    [chain.marks() for chain in early_chains],
                )
            ],
            list(late_grads),
            [(0, 0), (0, 1), (0, 2)],
            late_spans,
            ["late"],
            shard_rows,
            [3 * late_width + 128],
            small.astype(jnp.bfloat16),
        ),
        "late",
    )
    grads = [part for pair in zip(early_grads, late_grads) for part in pair]
    input_theirs = input_grad(
        place, tie(grad_first, chain_late.marks()), grads, full_qkv, 1
    )
    arrived_inputs = exchange(input_theirs, ACROSS)
    advance_all([chain_late, chain_up] + early_chains, input_theirs)
    input_mine = input_grad(
        place,
        tie(grad_first, chain_late.marks(), [chain.marks() for chain in early_chains]),
        grads,
        full_qkv,
        0,
    )
    grad_inputs = both_rows(input_mine, arrived_inputs, tp_rank)
    hidden_out = both_rows(mine, tie(arrived_out, input_mine), tp_rank)
    advance_all([chain_late] + early_chains, input_mine)
    waiting = [chain_late] + early_chains
    while waiting:
        advance_all(waiting)
        waiting = [chain for chain in waiting if chain.at < len(chain.steps)]
    for chain in [chain_up, chain_down] + early_chains:
        assert chain.at == len(chain.steps)
    grad_w_down, grad_w_up = (chain_down.finish(input_mine), chain_up.finish(input_mine))
    early_one, early_two = [chain.finish() for chain in early_chains]
    late = chain_late.finish()
    early_qkv = (
        early_one[:, local_width:],
        early_two[:, :early_width],
        early_two[:, early_width:],
    )
    grad_w_query, grad_w_key, grad_w_value = [
        jnp.concatenate([early, late[:, at * late_width : (at + 1) * late_width]], axis=1)
        for at, early in enumerate(early_qkv)
    ]
    own = late[:, 3 * late_width :]
    bias_size, row = (b_query.shape[0], 2)
    gain_rows = ln_gains.size // 128
    shift_rows = ln_shifts.size // 128
    loss_row = row + gain_rows + shift_rows
    loss_value = jnp.sum(own[loss_row : loss_row + 3]) / (features * valid_count)
    return (
        hidden_out,
        loss_value,
        grad_inputs,
        grad_w_query,
        grad_w_key,
        grad_w_value,
        early_one[:, :local_width].T,
        own[0, :bias_size],
        own[0, bias_size : 2 * bias_size],
        grad_w_up,
        own[1],
        grad_w_down.T,
        own[row : row + gain_rows].reshape(ln_gains.shape),
        own[row + gain_rows : loss_row].reshape(ln_shifts.shape),
    )


def solution(mesh):
    in_specs = (
        P("fsdp", "tp", None),
        P("fsdp", None),
        P("fsdp", "tp"),
        P("fsdp", "tp", None),
        P("fsdp", "tp"),
        P("fsdp", "tp"),
        P("fsdp", "tp"),
        P("tp", "fsdp"),
        P(("tp", "fsdp")),
        P(("tp", "fsdp")),
        P("fsdp", "tp"),
        P(("tp", "fsdp")),
        P("tp", "fsdp"),
        P(None, "fsdp"),
        P(None, "fsdp"),
    )
    out_specs = (
        P("fsdp", "tp", None),
        P(),
        P("fsdp", "tp", None),
        P("fsdp", "tp"),
        P("fsdp", "tp"),
        P("fsdp", "tp"),
        P("tp", "fsdp"),
        P(("tp", "fsdp")),
        P(("tp", "fsdp")),
        P("fsdp", "tp"),
        P(("tp", "fsdp")),
        P("tp", "fsdp"),
        P(None, "fsdp"),
        P(None, "fsdp"),
    )
    rows_plan = rows_plan_fits(mesh)
    return jax.shard_map(
        on_device_rows if rows_plan else on_device_heads, mesh=mesh, in_specs=in_specs, out_specs=out_specs, check_vma=False
    )
```

```python
from functools import partial
import math

import jax
import jax.numpy as jnp
from jax import lax
from jax.experimental import pallas as pl
from jax.experimental.pallas import tpu as pltpu
from jax.sharding import PartitionSpec as P

HEAD_DIM = 64
WINDOW = 512


EPSILON = 1e-05
MASKED = -1e30


def layer_norm_parts(values, gain_row, shift_row):
    centre = jnp.mean(values, axis=-1, keepdims=True)
    centred = values - centre
    inverse = lax.rsqrt(jnp.mean(centred * centred, axis=-1, keepdims=True) + EPSILON)
    normed = centred * inverse
    return (normed * gain_row + shift_row, normed, inverse)


def norm_backward(normed, inverse, gain_row, grad_out):
    scaled = grad_out * gain_row
    return inverse * (
        scaled
        - jnp.mean(scaled, axis=-1, keepdims=True)
        - normed * jnp.mean(scaled * normed, axis=-1, keepdims=True)
    )


def dot_first(left_side, right_side):
    return lax.dot_general(
        left_side, right_side, (((0,), (0,)), ((), ())), preferred_element_type=jnp.float32
    )


def dot_last(left_side, right_side):
    return lax.dot_general(
        left_side, right_side, (((1,), (1,)), ((), ())), preferred_element_type=jnp.float32
    )


def own_rows(source, offset_own, piece_len):
    return lax.dynamic_slice_in_dim(source, offset_own, piece_len, 1)


def allowed_mask(seg_row, offset, block_len):
    length = seg_row.shape[0]
    position = jnp.arange(length, dtype=jnp.int32)
    query_pos = offset + jnp.arange(block_len, dtype=jnp.int32)
    same_doc = seg_row[offset : offset + block_len][:, None] == seg_row[None, :]
    return same_doc & (jnp.abs(query_pos[:, None] - position[None, :]) < WINDOW)


def block_scores(query_part, key_heads, allowed):
    scores = jnp.einsum(
        "qhd,khd->hqk", query_part, key_heads, preferred_element_type=jnp.float32
    ) / math.sqrt(HEAD_DIM)
    return jnp.where(allowed[None], scores, MASKED)


def attention_forward(queries, key_all, value_all, segment_ids):
    seq_count, length = (queries.shape[0], queries.shape[1])
    block_len = min(512, length)
    outputs, summaries = ([], [])
    for row_index in range(seq_count):
        row_out, row_lse = ([], [])
        for offset in range(0, length, block_len):
            allowed = allowed_mask(segment_ids[row_index], offset, block_len)
            scores = block_scores(
                queries[row_index, offset : offset + block_len], key_all[row_index], allowed
            )
            row_top = jnp.max(scores, axis=-1, keepdims=True)
            raised = jnp.exp(scores - row_top)
            norm_sum = jnp.sum(raised, axis=-1, keepdims=True)
            softened = (raised / norm_sum).astype(jnp.bfloat16)
            row_out.append(
                jnp.einsum(
                    "hqk,khd->qhd",
                    softened,
                    value_all[row_index],
                    preferred_element_type=jnp.float32,
                )
            )
            row_lse.append(row_top + jnp.log(norm_sum))
        outputs.append(jnp.concatenate(row_out, axis=0))
        summaries.append(jnp.concatenate(row_lse, axis=1))
    return (jnp.stack(outputs), jnp.stack(summaries))


def attention_backward(queries, key_all, value_all, segment_ids, summaries, grad_mixed):
    seq_count, length = (queries.shape[0], queries.shape[1])
    block_len = min(512, length)
    root_dim = math.sqrt(HEAD_DIM)
    query_rows, key_rows, value_rows = ([], [], [])
    for row_index in range(seq_count):
        key_grad = jnp.zeros(key_all.shape[1:], jnp.float32)
        value_grad = jnp.zeros(value_all.shape[1:], jnp.float32)
        query_parts = []
        for offset in range(0, length, block_len):
            allowed = allowed_mask(segment_ids[row_index], offset, block_len)
            query_part = queries[row_index, offset : offset + block_len]
            scores = block_scores(query_part, key_all[row_index], allowed)
            softened = jnp.exp(scores - summaries[row_index, :, offset : offset + block_len])
            grad_part = grad_mixed[row_index, offset : offset + block_len]
            value_grad = value_grad + jnp.einsum(
                "hqk,qhd->khd",
                softened.astype(jnp.bfloat16),
                grad_part,
                preferred_element_type=jnp.float32,
            )
            grad_soft = jnp.einsum(
                "qhd,khd->hqk", grad_part, value_all[row_index], preferred_element_type=jnp.float32
            )
            grad_score = (
                softened * (grad_soft - jnp.sum(softened * grad_soft, axis=-1, keepdims=True))
            ).astype(jnp.bfloat16)
            query_parts.append(
                jnp.einsum(
                    "hqk,khd->qhd",
                    grad_score,
                    key_all[row_index],
                    preferred_element_type=jnp.float32,
                )
                / root_dim
            )
            key_grad = (
                key_grad
                + jnp.einsum(
                    "hqk,qhd->khd", grad_score, query_part, preferred_element_type=jnp.float32
                )
                / root_dim
            )
        query_rows.append(jnp.concatenate(query_parts, axis=0))
        key_rows.append(key_grad)
        value_rows.append(value_grad)
    return (jnp.stack(query_rows), jnp.stack(key_rows), jnp.stack(value_rows))


def on_device_heads(
    inputs,
    segment_ids,
    valid_mask,
    teacher,
    w_query,
    w_key,
    w_value,
    w_out,
    b_query,
    b_value,
    w_up,
    b_up,
    w_down,
    ln_gains,
    ln_shifts,
):
    seq_count, piece_len, features = inputs.shape
    tp_count = lax.axis_size("tp")
    tp_rank = lax.axis_index("tp")
    length = piece_len * tp_count
    total_tokens = seq_count * length * lax.axis_size("fsdp")
    offset_own = tp_rank * piece_len
    (
        full_query,
        full_key,
        full_value,
        full_out,
        full_bquery,
        full_bvalue,
        full_up,
        full_bup,
        full_down,
        full_gains,
        full_shifts,
    ) = (
        lax.all_gather(w_query, "fsdp", axis=0, tiled=True),
        lax.all_gather(w_key, "fsdp", axis=0, tiled=True),
        lax.all_gather(w_value, "fsdp", axis=0, tiled=True),
        lax.all_gather(w_out, "fsdp", axis=1, tiled=True),
        lax.all_gather(b_query, "fsdp", axis=0, tiled=True),
        lax.all_gather(b_value, "fsdp", axis=0, tiled=True),
        lax.all_gather(w_up, "fsdp", axis=0, tiled=True),
        lax.all_gather(b_up, "fsdp", axis=0, tiled=True),
        lax.all_gather(w_down, "fsdp", axis=1, tiled=True),
        lax.all_gather(ln_gains, "fsdp", axis=1, tiled=True),
        lax.all_gather(ln_shifts, "fsdp", axis=1, tiled=True),
    )
    gains = full_gains.astype(jnp.float32)
    shifts = full_shifts.astype(jnp.float32)
    local_width = full_query.shape[1]
    head_local = local_width // HEAD_DIM
    token_count = seq_count * length
    token_full = lax.all_gather(inputs, "tp", axis=1, tiled=True)
    flat_in = token_full.reshape(token_count, features)
    query_flat = (
        jnp.dot(flat_in, full_query, preferred_element_type=jnp.float32)
        + full_bquery.astype(jnp.float32)
    ).astype(jnp.bfloat16)
    key_flat = jnp.dot(flat_in, full_key, preferred_element_type=jnp.float32).astype(jnp.bfloat16)
    value_flat = (
        jnp.dot(flat_in, full_value, preferred_element_type=jnp.float32)
        + full_bvalue.astype(jnp.float32)
    ).astype(jnp.bfloat16)
    head_shape = (seq_count, length, head_local, HEAD_DIM)
    query_heads = query_flat.reshape(head_shape)
    key_heads = key_flat.reshape(head_shape)
    value_heads = value_flat.reshape(head_shape)
    mixed_heads, summaries = attention_forward(query_heads, key_heads, value_heads, segment_ids)
    mixed_low = mixed_heads.reshape(token_count, local_width).astype(jnp.bfloat16)
    attend_part = jnp.dot(mixed_low, full_out, preferred_element_type=jnp.float32).reshape(
        seq_count, length, features
    )
    attend_all = lax.psum(attend_part.astype(jnp.bfloat16), "tp").astype(jnp.float32)
    pre_first = token_full.astype(jnp.float32) + attend_all + shifts[2]
    normed_first, unit_first, inverse_first = layer_norm_parts(pre_first, gains[0], shifts[0])
    hidden_full = normed_first.astype(jnp.bfloat16)
    normed_own = own_rows(normed_first, offset_own, piece_len)
    hidden_flat = hidden_full.reshape(token_count, features)
    up_all = jnp.dot(hidden_flat, full_up, preferred_element_type=jnp.float32) + full_bup.astype(
        jnp.float32
    )
    active = jax.nn.gelu(up_all, approximate=False).astype(jnp.bfloat16)
    down_part = jnp.dot(active, full_down, preferred_element_type=jnp.float32).reshape(
        seq_count, length, features
    )
    down_own = lax.psum_scatter(
        down_part.astype(jnp.bfloat16), "tp", scatter_dimension=1, tiled=True
    ).astype(jnp.float32)
    pre_second = normed_own + down_own + shifts[3]
    result, unit_second, inverse_second = layer_norm_parts(pre_second, gains[1], shifts[1])
    differ = result - teacher.astype(jnp.float32)
    mask_float = valid_mask.astype(jnp.float32)[..., None]
    squares, valid_count = lax.psum(
        (jnp.sum(mask_float * differ * differ), jnp.sum(mask_float)), ("fsdp", "tp")
    )
    loss_value = squares / (features * valid_count)
    grad_result = mask_float * differ * (total_tokens / valid_count)
    grad_second = norm_backward(unit_second, inverse_second, gains[1], grad_result)
    grad_down_full = lax.all_gather(grad_second.astype(jnp.bfloat16), "tp", axis=1, tiled=True)
    grad_down_flat = grad_down_full.reshape(token_count, features)
    weight_down = dot_first(active, grad_down_flat)
    grad_active = dot_last(grad_down_flat, full_down)
    gelu_back = jax.vjp(partial(jax.nn.gelu, approximate=False), up_all)[1]
    grad_up = gelu_back(grad_active)[0].astype(jnp.bfloat16)
    weight_up = dot_first(hidden_flat, grad_up)
    bias_up = jnp.sum(grad_up.astype(jnp.float32), axis=0)
    hidden_part = dot_last(grad_up, full_up).reshape(seq_count, length, features)
    current = own_rows(hidden_part, offset_own, piece_len)
    hidden_part = lax.dynamic_update_slice_in_dim(hidden_part, current + grad_second, offset_own, 1)
    grad_hidden_all = lax.psum(hidden_part.astype(jnp.bfloat16), "tp").astype(jnp.float32)
    grad_first_all = norm_backward(unit_first, inverse_first, gains[0], grad_hidden_all)
    grad_mix_full = grad_first_all.astype(jnp.bfloat16)
    grad_first_own = own_rows(grad_first_all, offset_own, piece_len)
    grad_hidden_own = own_rows(grad_hidden_all, offset_own, piece_len)
    unit_first_own = own_rows(unit_first, offset_own, piece_len)
    grad_mix_flat = grad_mix_full.reshape(token_count, features)
    weight_out = dot_first(mixed_low, grad_mix_flat)
    grad_mixed = dot_last(grad_mix_flat, full_out).astype(jnp.bfloat16).reshape(head_shape)
    grad_query, grad_key, grad_value = attention_backward(
        query_heads, key_heads, value_heads, segment_ids, summaries, grad_mixed
    )
    query_low = grad_query.astype(jnp.bfloat16).reshape(token_count, local_width)
    key_low = grad_key.astype(jnp.bfloat16).reshape(token_count, local_width)
    value_low = grad_value.astype(jnp.bfloat16).reshape(token_count, local_width)
    weight_query = dot_first(flat_in, query_low)
    weight_key = dot_first(flat_in, key_low)
    weight_value = dot_first(flat_in, value_low)
    bias_query = jnp.sum(query_low.astype(jnp.float32), axis=0)
    bias_value = jnp.sum(value_low.astype(jnp.float32), axis=0)
    input_part = (
        dot_last(query_low, full_query)
        + dot_last(key_low, full_key)
        + dot_last(value_low, full_value)
    )
    grad_inputs = (
        lax.psum_scatter(
            input_part.reshape(seq_count, length, features).astype(jnp.bfloat16),
            "tp",
            scatter_dimension=1,
            tiled=True,
        ).astype(jnp.float32)
        + grad_first_own
    )
    gain_part = jnp.stack(
        [
            jnp.sum(grad_hidden_own * unit_first_own, axis=(0, 1)),
            jnp.sum(grad_result * unit_second, axis=(0, 1)),
        ]
    )
    shift_part = jnp.stack(
        [
            jnp.sum(grad_hidden_own, axis=(0, 1)),
            jnp.sum(grad_result, axis=(0, 1)),
            jnp.sum(grad_first_own, axis=(0, 1)),
            jnp.sum(grad_second, axis=(0, 1)),
        ]
    )
    gain_sum, shift_sum = lax.psum((gain_part, shift_part), "tp")
    gradients = (
        lax.psum_scatter(
            weight_query.astype(jnp.bfloat16), "fsdp", scatter_dimension=0, tiled=True
        ).astype(jnp.float32),
        lax.psum_scatter(
            weight_key.astype(jnp.bfloat16), "fsdp", scatter_dimension=0, tiled=True
        ).astype(jnp.float32),
        lax.psum_scatter(
            weight_value.astype(jnp.bfloat16), "fsdp", scatter_dimension=0, tiled=True
        ).astype(jnp.float32),
        lax.psum_scatter(
            weight_out.astype(jnp.bfloat16), "fsdp", scatter_dimension=1, tiled=True
        ).astype(jnp.float32),
        lax.psum_scatter(
            bias_query.astype(jnp.bfloat16), "fsdp", scatter_dimension=0, tiled=True
        ).astype(jnp.float32),
        lax.psum_scatter(
            bias_value.astype(jnp.bfloat16), "fsdp", scatter_dimension=0, tiled=True
        ).astype(jnp.float32),
        lax.psum_scatter(
            weight_up.astype(jnp.bfloat16), "fsdp", scatter_dimension=0, tiled=True
        ).astype(jnp.float32),
        lax.psum_scatter(
            bias_up.astype(jnp.bfloat16), "fsdp", scatter_dimension=0, tiled=True
        ).astype(jnp.float32),
        lax.psum_scatter(
            weight_down.astype(jnp.bfloat16), "fsdp", scatter_dimension=1, tiled=True
        ).astype(jnp.float32),
        lax.psum_scatter(
            gain_sum.astype(jnp.bfloat16), "fsdp", scatter_dimension=1, tiled=True
        ).astype(jnp.float32),
        lax.psum_scatter(
            shift_sum.astype(jnp.bfloat16), "fsdp", scatter_dimension=1, tiled=True
        ).astype(jnp.float32),
    )
    return (
        result.astype(jnp.bfloat16),
        loss_value,
        grad_inputs.astype(jnp.bfloat16),
        gradients[0],
        gradients[1],
        gradients[2],
        gradients[3],
        gradients[4],
        gradients[5],
        gradients[6],
        gradients[7],
        gradients[8],
        gradients[9],
        gradients[10],
    )


BLOCK = 256
LOG2E = math.log2(math.e)
SHARD_ROWS_PARTS = 2


def rows_plan_fits(mesh):
    fsdp_count, tp_count = (mesh.shape["fsdp"], mesh.shape["tp"])
    return tp_count == 2 and fsdp_count >= 8 and fsdp_count & (fsdp_count - 1) == 0


def dot_plain(left_side, right_side):
    return lax.dot_general(
        left_side, right_side, (((1,), (0,)), ((), ())), preferred_element_type=jnp.float32
    )


def exchange(values, move):
    tp_count = lax.axis_size("tp")
    count = lax.axis_size("fsdp") * tp_count
    flip = move[0] * tp_count + move[1]
    if move[1] == 0:
        return lax.ppermute(
            values, "fsdp", [(at, at ^ move[0]) for at in range(lax.axis_size("fsdp"))]
        )
    return lax.ppermute(values, ("fsdp", "tp"), [(at, at ^ flip) for at in range(count)])


ACROSS = (0, 1)
CORE = (1, 0)
SIDE = (2, 0)


def far_moves():
    places = lax.axis_size("fsdp").bit_length() - 1
    return [(1 << place, 0) for place in range(places - 1, 1, -1)]


def gather_steps():
    far = far_moves()
    return (tuple(far) + (ACROSS, SIDE), (far[0], ACROSS, SIDE) + tuple(far[1:]))


def scatter_steps(kind):
    far = list(reversed(far_moves()))
    if kind == "late":
        return ((SIDE,), (ACROSS,), tuple(reversed(far)))
    moves = {
        "across": [ACROSS, SIDE] + far,
        "side": [SIDE, ACROSS] + far,
        "far": far[:1] + [ACROSS, SIDE] + far[1:],
        "far_side": far[:1] + [SIDE] + far[1:] + [ACROSS],
    }[kind]
    return tuple((move,) for move in moves)


def moves_of(step):
    found = [(0, 0)]
    for high, low in reversed(step):
        found = found + [(one ^ high, two ^ low) for one, two in found]
    return found


def step_masks(steps):
    masks = [(0, 0)]
    for step in steps:
        masks = [
            (high ^ one, low ^ two) for one, two in moves_of(step) for high, low in masks
        ]
    return masks


def tie(values, *others):
    return lax.optimization_barrier((values, others))[0]


class GatherChain:

    def __init__(self, parts):
        self.steps = gather_steps()
        self.held = [part[None] for part in parts]
        self.arrived = None
        self.at = 0

    def advance(self, *after):
        if self.arrived is not None:
            self.held, self.arrived = tie((self.held, self.arrived), *after)
            self.held = [
                jnp.concatenate(pair, axis=0) for pair in zip(self.held, self.arrived)
            ]
        else:
            self.held = tie(self.held, *after)
        self.arrived = [
            exchange(held, steps[self.at]) for held, steps in zip(self.held, self.steps)
        ]
        self.at += 1

    def finish(self, *after):
        if after:
            self.arrived = tie(self.arrived, *after)
        self.pieces = []
        for held, arrived in zip(self.held, self.arrived):
            near = [held, arrived]
            self.pieces.append(near + [exchange(piece, CORE) for piece in near])

    def marks(self):
        return self.held

    def sources(self):
        return [piece for part in self.pieces for piece in part]

    def places(self):
        found = []
        for part, steps in enumerate(self.steps):
            masks = step_masks([(move,) for move in steps])
            size = len(masks) // 2
            for at in range(4):
                for place, (high, low) in enumerate(masks[at % 2 * size : (at % 2 + 1) * size]):
                    flip = CORE[0] if at >= 2 else 0
                    found.append((part, part * 4 + at, place, high ^ flip, low))
        return found


def scatter_places(kinds):
    found = []
    for part, kind in enumerate(kinds):
        masks = step_masks(tuple(reversed(scatter_steps(kind))))
        for at, flip in enumerate((0, CORE[0])):
            for place, (high, low) in enumerate(masks):
                found.append((part, part * 2 + at, place, high ^ flip, low))
    return found


class ScatterChain:

    def __init__(self, kept, sent, kind):
        self.steps = scatter_steps(kind)
        self.sent = [sent]
        self.terms = [kept, exchange(sent, CORE)]
        self.size = kept.shape[0]
        self.at = 0

    def total(self, first):
        terms = [term[first : first + self.size].astype(jnp.float32) for term in self.terms]
        return sum(terms[1:], terms[0])

    def advance(self, *after):
        self.terms = tie(self.terms, *after)
        moves = moves_of(self.steps[self.at])
        self.size //= len(moves)
        self.sent = [
            self.total(at * self.size).astype(jnp.bfloat16) for at in range(1, len(moves))
        ]
        self.terms = self.terms + [
            exchange(sent, move) for sent, move in zip(self.sent, moves[1:])
        ]
        self.at += 1

    def finish(self, *after):
        self.terms = tie(self.terms, *after)
        return self.total(0)[0]

    def marks(self):
        return self.sent


def advance_all(chains, *after):
    terms = tie([chain.terms for chain in chains], *after)
    for chain, found in zip(chains, terms):
        chain.terms = found
        chain.advance()


ANYWHERE = pl.BlockSpec(memory_space=pl.ANY)
SCALARS = pl.BlockSpec(memory_space=pltpu.SMEM)
VMEM_LIMIT = 58 << 20


def cost(flops, moved, transcendentals=0):
    return pl.CostEstimate(flops=flops // 2000, bytes_accessed=moved // 2000, transcendentals=0)


def low_shape(*shape):
    return jax.ShapeDtypeStruct(shape, jnp.bfloat16)


def wide_shape(*shape):
    return jax.ShapeDtypeStruct(shape, jnp.float32)


def whole(*shape):
    return pl.BlockSpec(shape, lambda *step: (0,) * len(shape))


def block_span(block, count):
    reach = -(-WINDOW // BLOCK)
    return max(0, block - reach), min(count - 1, block + reach)


def split_three(values):
    high = values.astype(jnp.bfloat16)
    rest = values - high.astype(jnp.float32)
    mid = rest.astype(jnp.bfloat16)
    low = (rest - mid.astype(jnp.float32)).astype(jnp.bfloat16)
    return high, mid, low


def window_edge(tile, row_block, column_block):
    if (abs(row_block - column_block) + 1) * BLOCK - 1 < WINDOW:
        return tile
    row = lax.broadcasted_iota(jnp.int32, tile.shape, 0) + row_block * BLOCK
    column = lax.broadcasted_iota(jnp.int32, tile.shape, 1) + column_block * BLOCK
    return jnp.where(jnp.abs(row - column) < WINDOW, tile, MASKED)


def attend_kernel(seg_ref, q_ref, k_ref, v_ref, out_ref, qx_ref, kx_ref, held_ref):
    length = q_ref.shape[0]
    count = length // BLOCK
    lane = lax.broadcasted_iota(jnp.int32, (length, 128), 1)
    seg = seg_ref[...]
    q_heads, k_heads, v_heads = ([], [], [])
    for head in range(2):
        own = (lane < 64) if head == 0 else (lane >= 64)
        extra = lane - 64 if head == 0 else lane
        same = extra == seg
        q_extra = jnp.where(same, 1.0, 0.0).astype(jnp.bfloat16)
        k_extra = jnp.where(
            extra < 4, jnp.where(same, 0.0, MASKED), jnp.where(extra < 7, -1.0, 0.0)
        ).astype(jnp.bfloat16)
        v_extra = jnp.where(extra == 0, 1.0, 0.0).astype(jnp.bfloat16)
        q_heads.append(jnp.where(own, q_ref[...], q_extra))
        k_heads.append(jnp.where(own, k_ref[...], k_extra))
        v_heads.append(jnp.where(own, v_ref[...], v_extra))
        kx_ref[head] = k_heads[head]
    units = [(head, block) for head in range(2) for block in range(count)]

    def score(unit):
        head, block = unit
        low, high = block_span(block, count)
        rows = slice(block * BLOCK, (block + 1) * BLOCK)
        tile = dot_last(q_heads[head][rows], k_heads[head][low * BLOCK : (high + 1) * BLOCK])
        return [
            window_edge(tile[:, (at - low) * BLOCK : (at - low + 1) * BLOCK], block, at)
            for at in range(low, high + 1)
        ]

    def finish(unit, tiles):
        head, block = unit
        low, high = block_span(block, count)
        rows = slice(block * BLOCK, (block + 1) * BLOCK)
        most = tiles[0]
        for tile in tiles[1:]:
            most = jnp.maximum(most, tile)
        top = jnp.max(most, axis=1, keepdims=True)
        raised = jnp.concatenate(
            [jnp.exp2(tile - top).astype(jnp.bfloat16) for tile in tiles], axis=1
        )
        mixed = dot_plain(raised, v_heads[head][low * BLOCK : (high + 1) * BLOCK])
        norm_sum = mixed[:, 64:65] if head == 0 else mixed[:, 0:1]
        held_ref[head, rows, :] = mixed * (1.0 / norm_sum)
        first, second, third = split_three(top + jnp.log2(norm_sum))
        extra = lane[:BLOCK] - 64 if head == 0 else lane[:BLOCK]
        qx_ref[head, rows, :] = jnp.where(
            extra == 4,
            first,
            jnp.where(extra == 5, second, jnp.where(extra == 6, third, q_heads[head][rows])),
        )

    tiles = score(units[0])
    for at, unit in enumerate(units):
        following = score(units[at + 1]) if at + 1 < len(units) else None
        finish(unit, tiles)
        tiles = following
    out_ref[...] = jnp.where(lane < 64, held_ref[0], held_ref[1]).astype(jnp.bfloat16)


def attend(queries, keys, values, seg, first, count, earlier=None):
    length, width = queries.shape
    pair = pl.BlockSpec((length, 128), lambda step: (0, first + step))
    padded = pl.BlockSpec((2, length, 128), lambda step: (first + step, 0, 0))
    passed = 0 if earlier is None else 3
    operands = (seg, queries, keys, values) + (earlier or ())

    def kernel(seg_ref, q_ref, k_ref, v_ref, *refs):
        attend_kernel(seg_ref, q_ref, k_ref, v_ref, *refs[passed:])

    return pl.pallas_call(
        kernel,
        grid=(count,),
        in_specs=[pl.BlockSpec((length, 1), lambda step: (0, 0)), pair, pair, pair]
        + [pl.BlockSpec(memory_space=pl.ANY)] * passed,
        out_specs=[pair, padded, padded],
        out_shape=[
            jax.ShapeDtypeStruct((length, width), jnp.bfloat16),
            jax.ShapeDtypeStruct((width // HEAD_DIM, length, 128), jnp.bfloat16),
            jax.ShapeDtypeStruct((width // HEAD_DIM, length, 128), jnp.bfloat16),
        ],
        scratch_shapes=[pltpu.VMEM((2, length, 128), jnp.float32)],
        input_output_aliases={4 + at: at for at in range(passed)},
        compiler_params=pltpu.CompilerParams(vmem_limit_bytes=VMEM_LIMIT),
        cost_estimate=cost(3_500_000_000 * count, (2 << 20) * count),
        name="attend",
    )(*operands)


def attend_back_kernel(qx_ref, kx_ref, v_ref, out_ref, grad_ref, dq_ref, dk_ref, dv_ref, held_ref):
    length = v_ref.shape[0]
    count = length // BLOCK
    lane = lax.broadcasted_iota(jnp.int32, (length, 128), 1)
    grad = grad_ref[...]
    for head in range(2):
        mine = slice(head * 64, (head + 1) * 64)
        own = (lane < 64) if head == 0 else (lane >= 64)
        extra = lane - 64 if head == 0 else lane
        product = jnp.where(
            own, grad.astype(jnp.float32) * out_ref[...].astype(jnp.float32), 0.0
        )
        first, second, third = split_three(-jnp.sum(product, axis=1, keepdims=True))
        grad_head = jnp.where(
            own,
            grad,
            jnp.where(
                extra == 0,
                first,
                jnp.where(extra == 1, second, jnp.where(extra == 2, third, jnp.zeros_like(grad))),
            ),
        )
        v_head = jnp.where(own, v_ref[...], jnp.where(extra < 3, 1.0, 0.0).astype(jnp.bfloat16))
        q_head, k_head = (qx_ref[head], kx_ref[head])
        k_turned = k_head.T[mine]
        for block in range(count):
            low, high = block_span(block, count)
            keys = slice(block * BLOCK, (block + 1) * BLOCK)
            span = slice(low * BLOCK, (high + 1) * BLOCK)
            tile = dot_last(k_head[keys], q_head[span])
            soft = jnp.concatenate(
                [
                    jnp.exp2(
                        window_edge(tile[:, (at - low) * BLOCK : (at - low + 1) * BLOCK], block, at)
                    )
                    for at in range(low, high + 1)
                ],
                axis=1,
            )
            grad_soft = dot_last(v_head[keys], grad_head[span])
            grad_score = (soft * grad_soft).astype(jnp.bfloat16)
            grad_value = dot_plain(soft.astype(jnp.bfloat16), grad_head[span])
            grad_key = dot_plain(grad_score, q_head[span]) * (1.0 / LOG2E)
            dv_ref[keys, mine] = grad_value[:, mine].astype(jnp.bfloat16)
            dk_ref[keys, mine] = grad_key[:, mine].astype(jnp.bfloat16)
            grad_query = dot_plain(k_turned[:, keys], grad_score)
            if block == 0:
                held_ref[mine, span] = grad_query
                if high + 1 < count:
                    held_ref[mine, (high + 1) * BLOCK :] = jnp.zeros(
                        (64, length - (high + 1) * BLOCK), jnp.float32
                    )
            else:
                held_ref[mine, span] += grad_query
    dq_ref[...] = (held_ref[...] * (1.0 / math.sqrt(HEAD_DIM))).T.astype(jnp.bfloat16)


def attend_back(
    q_padded, k_padded, values, mixed, grad_mixed, first, count, out_first, out_count, earlier=None
):
    length, width = values.shape
    pair = pl.BlockSpec((length, 128), lambda step: (0, first + step))
    out_pair = pl.BlockSpec((length, 128), lambda step: (0, first - out_first + step))
    padded = pl.BlockSpec((2, length, 128), lambda step: (first + step, 0, 0))
    passed = 0 if earlier is None else 3
    operands = (q_padded, k_padded, values, mixed, grad_mixed) + tuple(earlier or ())

    def kernel(qx_ref, kx_ref, v_ref, out_ref, grad_ref, *refs):
        attend_back_kernel(qx_ref, kx_ref, v_ref, out_ref, grad_ref, *refs[passed:])

    return pl.pallas_call(
        kernel,
        grid=(count,),
        in_specs=[padded, padded, pair, pair, pair]
        + [pl.BlockSpec(memory_space=pl.ANY)] * passed,
        out_specs=[out_pair, out_pair, out_pair],
        out_shape=[jax.ShapeDtypeStruct((length, 128 * out_count), jnp.bfloat16)] * 3,
        scratch_shapes=[pltpu.VMEM((128, length), jnp.float32)],
        input_output_aliases={5 + at: at for at in range(passed)},
        compiler_params=pltpu.CompilerParams(vmem_limit_bytes=VMEM_LIMIT),
        cost_estimate=cost(5_000_000_000 * count, (2 << 20) * count),
        name="attend_back",
    )(*operands)


MASK_ROW = 16


def shards_kernel(
    place_ref, wq_ref, wk_ref, wv_ref, wo_ref, wu_ref, wd_ref, bq_ref, bv_ref, bu_ref, gain_ref,
    shift_ref, mask_ref, first_ref, second_ref, wide_ref, low_ref, high_ref,
):
    rows, width = wq_ref.shape
    half = width // 2
    first_ref[:, :width] = wq_ref[...]
    first_ref[:, width : width + half] = wk_ref[:, :half]
    second_ref[:, :half] = wk_ref[:, half:]
    second_ref[:, half:] = wv_ref[...]
    lane = lax.broadcasted_iota(jnp.int32, (1, 128), 1)

    def spread(ref):
        values = ref[...].astype(jnp.float32)
        size = values.shape[1]
        lanes = jnp.concatenate([values] * (128 // size), axis=1)
        return [
            jnp.where((row * 128 + lane) // size == place_ref[0], lanes, 0.0)
            for row in range(width // 128)
        ]

    def flat(ref):
        values = ref[...].astype(jnp.float32)
        return [
            jnp.concatenate([values[at : at + 1], values[at + 1 : at + 2]], axis=1)
            for at in range(0, values.shape[0], 2)
        ]

    count = jnp.sum(mask_ref[...].astype(jnp.float32))
    high = jnp.floor(count / 256.0)
    count_row = jnp.where(lane == 0, high, jnp.where(lane == 1, count - 256.0 * high, 0.0))
    lines = spread(bq_ref) + spread(bv_ref) + [bu_ref[...].astype(jnp.float32)]
    lines = lines + flat(gain_ref) + flat(shift_ref) + [count_row]
    lines = lines + [jnp.zeros((1, 128), jnp.float32)] * (MASK_ROW - len(lines))
    mask = mask_ref[...].astype(jnp.float32)
    for row in range(mask.shape[0]):
        lines = lines + [
            mask[row : row + 1, at : at + 128] for at in range(0, mask.shape[1], 128)
        ]
    lines = lines + [jnp.zeros((1, 128), jnp.float32)] * (rows - len(lines))
    first_ref[:, width + half :] = jnp.concatenate(lines, axis=0).astype(jnp.bfloat16)
    wide_ref[:, : wu_ref.shape[1]] = wu_ref[...]
    wide_ref[:, wu_ref.shape[1] :] = wo_ref[...]
    cut = low_ref.shape[1]
    low_ref[...] = wd_ref[:, :cut]
    high_ref[...] = wd_ref[:, cut:]


def shards(place, w_query, w_key, w_value, w_out, w_up, w_down, small):
    rows, width = w_query.shape
    hidden = w_up.shape[1]
    operands = (w_query, w_key, w_value, w_out, w_up, w_down) + small
    outs = [
        low_shape(rows, width + width // 2 + 128),
        low_shape(rows, width // 2 + width),
        low_shape(rows, hidden + width),
        low_shape(rows, hidden // 2 + 128),
        low_shape(rows, hidden // 2 - 128),
    ]
    return pl.pallas_call(
        shards_kernel,
        in_specs=[SCALARS] + [whole(*operand.shape) for operand in operands],
        out_specs=[whole(*out.shape) for out in outs],
        out_shape=outs,
        compiler_params=pltpu.CompilerParams(vmem_limit_bytes=VMEM_LIMIT),
        cost_estimate=cost(0, 2 << 20),
        name="shards",
    )(place, *operands)


def qkv_kernel(spans, places, place_ref, row_ref, *refs):
    count = 1 + max(source for _, source, _, _, _ in places)
    sources = refs[:count]
    q_ref, k_ref, v_ref, full_ref, small_out, held, small, sems, out_sem = refs[count:]
    me_fsdp, me_tp = (place_ref[0], place_ref[1])
    rows = sources[0].shape[1]
    width = q_ref.shape[1]
    fsdp_count = held.shape[0] // rows
    copies = {0: [], 1: [], 2: [], 3: []}
    for part, source, place, high, low in places:
        fsdp, tp = (me_fsdp ^ high, me_tp ^ low)
        for start, size, target, per_tp, column in spans[part]:
            if target == 3:
                from_ref = sources[source].at[place, pl.ds(0, small.shape[1]), pl.ds(start, size)]
                to_ref = small.at[tp * fsdp_count + fsdp]
            else:
                row = pl.multiple_of(fsdp * rows, rows)
                lane = pl.multiple_of(tp * per_tp + column, 128)
                from_ref = sources[source].at[place, :, pl.ds(start, size)]
                to_ref = held.at[pl.ds(row, rows), pl.ds(lane, size)]
            total = sum(len(group) for group in copies.values())
            copies[target].append(pltpu.make_async_copy(from_ref, to_ref, sems.at[total]))
            copies[target][-1].start()

    def bias(first):
        halves = [
            jnp.sum(
                small[tp * fsdp_count : (tp + 1) * fsdp_count].astype(jnp.float32), axis=0
            )
            for tp in range(2)
        ]
        count = width // 256
        lanes = [
            half[first + at : first + at + 1]
            for group in (range(count - 1), (count - 1,))
            for half in halves
            for at in group
        ]
        return jnp.concatenate(lanes, axis=1)

    scale = LOG2E / math.sqrt(HEAD_DIM)
    for copy in copies[3]:
        copy.wait()
    out_copies = [pltpu.make_async_copy(small, small_out, out_sem.at[3])]
    out_copies[0].start()
    for target, out_ref in ((0, q_ref), (1, k_ref), (2, v_ref)):
        for copy in copies[target]:
            copy.wait()
        span = pl.ds(target * width, width)
        out_copies.append(
            pltpu.make_async_copy(held.at[:, span], full_ref.at[:, span], out_sem.at[target])
        )
        out_copies[-1].start()
        added = bias(0 if target == 0 else width // 256) if target != 1 else None
        for block in range(row_ref.shape[0] // BLOCK):
            lines = slice(block * BLOCK, (block + 1) * BLOCK)
            found = dot_plain(row_ref[lines], held[:, target * width : (target + 1) * width])
            if added is not None:
                found = found + added
            if target == 0:
                found = found * scale
            out_ref[lines] = found.astype(jnp.bfloat16)
    for copy in out_copies:
        copy.wait()


def qkv_project(chain, spans, place, row_low, width, small_rows):
    length, features = row_low.shape
    sources = chain.sources()
    places = chain.places()
    devices = lax.axis_size("fsdp") * lax.axis_size("tp")
    copies = sum(len(spans[entry[0]]) for entry in places)
    return pl.pallas_call(
        partial(qkv_kernel, spans, places),
        in_specs=[SCALARS, whole(length, features)] + [ANYWHERE] * len(sources),
        out_specs=[whole(length, width)] * 3 + [ANYWHERE] * 2,
        out_shape=[low_shape(length, width)] * 3
        + [low_shape(features, 3 * width), low_shape(devices, small_rows, 128)],
        scratch_shapes=[
            pltpu.VMEM((features, 3 * width), jnp.bfloat16),
            pltpu.VMEM((devices, small_rows, 128), jnp.bfloat16),
            pltpu.SemaphoreType.DMA((copies,)),
            pltpu.SemaphoreType.DMA((4,)),
        ],
        compiler_params=pltpu.CompilerParams(vmem_limit_bytes=VMEM_LIMIT),
        cost_estimate=cost(6 * length * features * width, 24 << 20),
        name="qkv_project",
    )(place, row_low, *sources)


def unit_of(values):
    centred = values - jnp.mean(values, axis=-1, keepdims=True)
    inverse = lax.rsqrt(jnp.mean(centred * centred, axis=-1, keepdims=True) + EPSILON)
    return centred * inverse, inverse


def out_up_kernel(
    mixed_ref, row_ref, out_w_ref, up_w_ref, vector_ref, b_ref,
    active_ref, slope_ref, unit_ref, inverse_ref, hidden_ref, full_out_ref,
):
    length, features = row_ref.shape
    late = out_w_ref.shape[3] // 4
    early = 3 * late

    @pl.when(pl.program_id(0) == 0)
    def _():
        for tp in range(2):
            lanes = pl.ds(tp * early, early)
            full_out_ref[:, lanes] = out_w_ref[:, tp, :, :early].reshape(features, early)
            lanes = pl.ds(2 * early + tp * late, late)
            full_out_ref[:, lanes] = out_w_ref[:, tp, :, early:].reshape(features, late)
        for block in range(length // BLOCK):
            lines = slice(block * BLOCK, (block + 1) * BLOCK)
            before = (
                row_ref[lines].astype(jnp.float32)
                + dot_last(mixed_ref[lines], full_out_ref[...])
                + vector_ref[0:1]
            )
            unit, inverse = unit_of(before)
            unit_ref[lines] = unit
            inverse_ref[lines] = inverse
            hidden_ref[lines] = (unit * vector_ref[1:2] + vector_ref[2:3]).astype(jnp.bfloat16)

    weight = up_w_ref[:, 0].reshape(features, up_w_ref.shape[3])

    def product(block):
        lines = slice(block * BLOCK, (block + 1) * BLOCK)
        return dot_plain(hidden_ref[lines], weight) + b_ref[...]

    up = product(0)
    count = length // BLOCK
    for block in range(count):
        following = product(block + 1) if block + 1 < count else None
        lines = slice(block * BLOCK, (block + 1) * BLOCK)
        cumulative = 0.5 * (1.0 + lax.erf(up * math.sqrt(0.5)))
        density = jnp.exp2(up * up * (-0.5 * LOG2E)) * (1.0 / math.sqrt(2.0 * math.pi))
        active_ref[lines] = (up * cumulative).astype(jnp.bfloat16)
        slope_ref[lines] = (cumulative + up * density).astype(jnp.bfloat16)
        up = following


def out_up_project(mixed, row_low, gathered, vectors, bias, local_hidden, local_width):
    length, features = row_low.shape
    fsdp_count, tp_count, rows, _ = gathered.shape
    hidden_units = local_hidden * tp_count
    block_width = math.gcd(math.gcd(local_hidden, 512), local_width)
    each = local_hidden // block_width
    column = pl.BlockSpec((length, block_width), lambda step: (0, step))
    return pl.pallas_call(
        out_up_kernel,
        grid=(hidden_units // block_width,),
        in_specs=[
            whole(length, features),
            whole(length, features),
            pl.BlockSpec(
                (fsdp_count, tp_count, rows, local_width),
                lambda step: (0, 0, 0, local_hidden // local_width),
            ),
            pl.BlockSpec(
                (fsdp_count, 1, rows, block_width),
                lambda step: (0, step // each, 0, step % each),
            ),
            whole(*vectors.shape),
            pl.BlockSpec((1, block_width), lambda step: (0, step)),
        ],
        out_specs=[column, column]
        + [whole(length, features), whole(length, 1), whole(length, features)]
        + [whole(features, features)],
        out_shape=[
            low_shape(length, hidden_units),
            low_shape(length, hidden_units),
            wide_shape(length, features),
            wide_shape(length, 1),
            low_shape(length, features),
            low_shape(features, features),
        ],
        compiler_params=pltpu.CompilerParams(vmem_limit_bytes=VMEM_LIMIT),
        cost_estimate=cost(
            2 * length * features * (hidden_units + features),
            36 << 20,
            2 * length * hidden_units,
        ),
        name="out_up_project",
    )(mixed, row_low, gathered, gathered, vectors, bias)


def piece_lanes(place_ref, sources, group):
    part, low = group
    widths = [sources[0].shape[2], sources[4].shape[2]]
    return (place_ref[1] ^ low) * sum(widths) + sum(widths[:part]), widths[part]


def piece_copies(places, place_ref, sources, held, sems, group):
    rows = sources[0].shape[1]
    found = []
    for at, (part, source, place, high, low) in enumerate(places):
        if (part, low) != group:
            continue
        row = pl.multiple_of((place_ref[0] ^ high) * rows, rows)
        lane, part_width = piece_lanes(place_ref, sources, group)
        found.append(
            pltpu.make_async_copy(
                sources[source].at[place],
                held.at[pl.ds(row, rows), pl.ds(pl.multiple_of(lane, 128), part_width)],
                sems.at[at],
            )
        )
    return found


PIECE_GROUPS = [(part, low) for low in range(2) for part in range(2)]


def down_kernel(
    places, place_ref, active_ref, unit_ref, teacher_ref, weight_ref, vector_ref, *refs
):
    count = 1 + max(source for _, source, _, _, _ in places)
    sources = refs[:count]
    out_ref, grad_ref, low_ref, sums_ref, held, sems = refs[count:]
    step = pl.program_id(0)
    copies = partial(piece_copies, places, place_ref, sources, held, sems)

    @pl.when(step == 0)
    def _():
        for group in PIECE_GROUPS:
            for copy in copies(group):
                copy.start()
        sums_ref[...] = jnp.zeros_like(sums_ref)

    normed_first = unit_ref[...] * vector_ref[0:1] + vector_ref[1:2]
    before = normed_first + vector_ref[2:3]
    for group in PIECE_GROUPS:

        @pl.when(step == 0)
        def _(group=group):
            for copy in copies(group):
                copy.wait()

        lane, part_width = piece_lanes(place_ref, sources, group)
        span = pl.ds(pl.multiple_of(lane, 128), part_width)
        before = before + dot_last(active_ref[:, span], held[:, span])

    unit, inverse = unit_of(before)
    gain = vector_ref[3:4]
    result = unit * gain + vector_ref[4:5]
    out_ref[...] = result.astype(jnp.bfloat16)
    differ = result - teacher_ref[...].astype(jnp.float32)
    grad = differ * weight_ref[...]
    scaled = grad * gain
    grad_before = inverse * (
        scaled
        - jnp.mean(scaled, axis=-1, keepdims=True)
        - unit * jnp.mean(scaled * unit, axis=-1, keepdims=True)
    )
    grad_ref[...] = grad_before
    low_ref[...] = grad_before.astype(jnp.bfloat16)
    for at, term in enumerate((grad * unit, grad, grad_before, grad * differ)):
        sums_ref[at : at + 1] += jnp.sum(term, axis=0, keepdims=True)


def down_project(chain, place, active, unit, teacher, weight, vectors):
    length, hidden_units = active.shape
    features = unit.shape[1]
    sources, places = (chain.sources(), chain.places())
    line = lambda width: pl.BlockSpec((BLOCK, width), lambda step: (step, 0))
    return pl.pallas_call(
        partial(down_kernel, places),
        grid=(length // BLOCK,),
        in_specs=[SCALARS, line(hidden_units), line(features), line(features), line(1)]
        + [whole(*vectors.shape)]
        + [ANYWHERE] * len(sources),
        out_specs=[line(features), line(features), line(features), whole(8, features)],
        out_shape=[
            low_shape(length, features),
            wide_shape(length, features),
            low_shape(length, features),
            wide_shape(8, features),
        ],
        scratch_shapes=[
            pltpu.VMEM((features, hidden_units), jnp.bfloat16),
            pltpu.SemaphoreType.DMA((len(places),)),
        ],
        compiler_params=pltpu.CompilerParams(vmem_limit_bytes=VMEM_LIMIT),
        cost_estimate=cost(2 * length * features * hidden_units, 36 << 20),
        name="down_project",
    )(place, active, unit, teacher, weight, vectors, *sources)


def column_copies(places, tp_places, each, block_width, me_fsdp, held, pieces, sems, at):
    rows = pieces[0].shape[1]
    found = []
    for number, (_, output, place, high, low) in enumerate(places):
        if low:
            continue
        row = pl.multiple_of((me_fsdp ^ high) * rows, rows)
        lane = pl.multiple_of(at % each * block_width, 128)
        found.append(
            pltpu.make_async_copy(
                held.at[at, pl.ds(row, rows)],
                pieces[output].at[place + at // each * tp_places, :, pl.ds(lane, block_width)],
                sems.at[at, number],
            )
        )
    return found


def down_back_kernel(
    places, tp_places, each, place_ref, grad_ref, active_ref, kept_ref, sent_ref,
    turned, held, sems,
):
    step = pl.program_id(0)

    @pl.when(step == 0)
    def _():
        turned[...] = grad_ref[...].T

    copies = partial(
        column_copies, places, tp_places, each, active_ref.shape[1], place_ref[0], held,
        (kept_ref, sent_ref), sems,
    )
    held[step] = dot_plain(turned[...], active_ref[...]).astype(jnp.bfloat16)
    for copy in copies(step):
        copy.start()

    @pl.when(step == 2 * each - 1)
    def _():
        for at in range(2 * each):
            for copy in copies(at):
                copy.wait()


def up_back_kernel(
    places, tp_places, each, down_places, place_ref, grad_ref, hidden_ref, slope_ref, up_ref, *refs
):
    count = 1 + max(source for _, source, _, _, _ in down_places)
    sources = refs[:count]
    total_ref, bias_ref, kept_ref, sent_ref, turned, held, sems, down_held, down_sems = refs[count:]
    step = pl.program_id(0)
    down_copies = partial(piece_copies, down_places, place_ref, sources, down_held, down_sems)
    length, features = grad_ref.shape
    block_width = slope_ref.shape[1]

    @pl.when(step == 0)
    def _():
        for group in PIECE_GROUPS:
            for copy in down_copies(group):
                copy.start()
        turned[...] = hidden_ref[...].T
        total_ref[...] = jnp.zeros_like(total_ref)

    for at, group in enumerate(PIECE_GROUPS):

        @pl.when(step == at * (each // 2))
        def _(group=group):
            for copy in down_copies(group):
                copy.wait()

    copies = partial(
        column_copies, places, tp_places, each, block_width, place_ref[0], held,
        (kept_ref, sent_ref), sems,
    )
    column = (place_ref[1] ^ (step // each)) * each + step % each
    lane = pl.multiple_of(column * block_width, block_width)
    down_weight = down_held[:, pl.ds(lane, block_width)]
    up_weight = up_ref[:, 0].reshape(features, block_width)
    spans = [slice(at * BLOCK, (at + 1) * BLOCK) for at in range(length // BLOCK)]
    grads, bias = ([], jnp.zeros((1, block_width), jnp.float32))
    found = dot_plain(grad_ref[spans[0]], down_weight)
    for at, span in enumerate(spans):
        following = (
            dot_plain(grad_ref[spans[at + 1]], down_weight) if at + 1 < len(spans) else None
        )
        grad_up = found * slope_ref[span].astype(jnp.float32)
        bias = bias + jnp.sum(grad_up, axis=0, keepdims=True)
        grads.append(grad_up.astype(jnp.bfloat16))
        found = following
    bias_ref[...] = bias
    grad_up = jnp.concatenate(grads, axis=0)
    held[step] = dot_plain(turned[...], grad_up).astype(jnp.bfloat16)
    for copy in copies(step):
        copy.start()
    total_ref[...] += dot_last(grad_up, up_weight)

    @pl.when(step == 2 * each - 1)
    def _():
        for at in range(2 * each):
            for copy in copies(at):
                copy.wait()


def column_plan(kind, local_hidden):
    block_width = math.gcd(local_hidden, 512)
    each = local_hidden // block_width
    places = scatter_places([kind])
    tp_places = next(place for _, at, place, high, low in places if at == 0 and low and not high)

    def column(step, where):
        return (where[1] ^ (step // each)) * each + step % each

    return block_width, each, places, tp_places, column


def keep(*shape):
    return pl.BlockSpec(shape, lambda step, where: (0,) * len(shape))


def column_scratch(features, length, each, block_width, places):
    return [
        pltpu.VMEM((features, length), jnp.bfloat16),
        pltpu.VMEM((2 * each, features, block_width), jnp.bfloat16),
        pltpu.SemaphoreType.DMA((2 * each, len(places))),
    ]


def down_back(place, grad_down, active, rows, local_hidden, kind):
    length, features = grad_down.shape
    block_width, each, places, tp_places, column = column_plan(kind, local_hidden)
    piece = low_shape(len(places) // 2, rows, local_hidden)
    return pl.pallas_call(
        partial(down_back_kernel, places, tp_places, each),
        grid_spec=pltpu.PrefetchScalarGridSpec(
            num_scalar_prefetch=1,
            grid=(2 * each,),
            in_specs=[
                keep(length, features),
                pl.BlockSpec((length, block_width), lambda step, where: (0, column(step, where))),
            ],
            out_specs=[ANYWHERE] * 2,
            scratch_shapes=column_scratch(features, length, each, block_width, places),
        ),
        out_shape=[piece] * 2,
        compiler_params=pltpu.CompilerParams(vmem_limit_bytes=VMEM_LIMIT),
        cost_estimate=cost(4 * length * features * local_hidden, 20 << 20),
        name="down_back",
    )(place, grad_down, active)


def up_back(place, grad_down, hidden, slope, chain, gathered, kind):
    length, features = hidden.shape
    fsdp_count, tp_count, rows, _ = gathered.shape
    local_hidden = slope.shape[1] // tp_count
    sources, down_places = (chain.sources(), chain.places())
    block_width, each, places, tp_places, column = column_plan(kind, local_hidden)
    piece = low_shape(len(places) // 2, rows, local_hidden)
    block = pl.BlockSpec((length, block_width), lambda step, where: (0, column(step, where)))
    return pl.pallas_call(
        partial(up_back_kernel, places, tp_places, each, down_places),
        grid_spec=pltpu.PrefetchScalarGridSpec(
            num_scalar_prefetch=1,
            grid=(2 * each,),
            in_specs=[
                keep(length, features),
                keep(length, features),
                block,
                pl.BlockSpec(
                    (fsdp_count, 1, rows, block_width),
                    lambda step, where: (0, where[1] ^ (step // each), 0, step % each),
                ),
            ]
            + [ANYWHERE] * len(sources),
            out_specs=[
                keep(length, features),
                pl.BlockSpec((1, block_width), lambda step, where: (0, column(step, where))),
            ]
            + [ANYWHERE] * 2,
            scratch_shapes=column_scratch(features, length, each, block_width, places)
            + [
                pltpu.VMEM((features, slope.shape[1]), jnp.bfloat16),
                pltpu.SemaphoreType.DMA((len(down_places),)),
            ],
        ),
        out_shape=[wide_shape(length, features), wide_shape(1, local_hidden * tp_count)]
        + [piece] * 2,
        compiler_params=pltpu.CompilerParams(vmem_limit_bytes=VMEM_LIMIT),
        cost_estimate=cost(12 * length * features * local_hidden, 40 << 20),
        name="up_back",
    )(place, grad_down, hidden, slope, gathered, *sources)


def norm_back_kernel(
    base_ref, grad_ref, unit_ref, inverse_ref, gain_ref, weight_ref, first_ref, low_ref, mixed_ref, sums_ref
):
    @pl.when(pl.program_id(0) == 0)
    def _():
        sums_ref[...] = jnp.zeros_like(sums_ref)

    grad, unit = (base_ref[...] + grad_ref[...], unit_ref[...])
    scaled = grad * gain_ref[...]
    found = inverse_ref[...] * (
        scaled
        - jnp.mean(scaled, axis=-1, keepdims=True)
        - unit * jnp.mean(scaled * unit, axis=-1, keepdims=True)
    )
    first_ref[...] = found
    low = found.astype(jnp.bfloat16)
    low_ref[...] = low
    mixed_ref[...] = dot_plain(low, weight_ref[...]).astype(jnp.bfloat16)
    for at, term in enumerate((grad * unit, grad, found)):
        sums_ref[at : at + 1] += jnp.sum(term, axis=0, keepdims=True)


def norm_back(grad_second, grad_hidden, unit, inverse, gain, full_out):
    length, features = unit.shape
    line = lambda width: pl.BlockSpec((BLOCK, width), lambda step: (step, 0))
    return pl.pallas_call(
        norm_back_kernel,
        grid=(length // BLOCK,),
        in_specs=[line(features)] * 3 + [line(1), whole(1, features)]
        + [whole(*full_out.shape)],
        out_specs=[line(features), line(features), line(full_out.shape[1]), whole(8, features)],
        out_shape=[
            wide_shape(length, features),
            low_shape(length, features),
            low_shape(length, full_out.shape[1]),
            wide_shape(8, features),
        ],
        compiler_params=pltpu.CompilerParams(vmem_limit_bytes=VMEM_LIMIT),
        cost_estimate=cost(2 * length * features * features, 22 << 20),
        name="norm_back",
    )(grad_second, grad_hidden, unit, inverse, gain, full_out)


def weight_grad_kernel(products, spans, places, extra, place_ref, *refs):
    lefts = 1 + max(left for left, _ in products)
    rights = 1 + max(right for _, right in products)
    left_refs, right_refs = (refs[:lefts], refs[lefts : lefts + rights])
    refs = refs[lefts + rights :]
    if extra:
        extra_ref, refs = (refs[0], refs[1:])
    parts = 2 * len(spans)
    pieces, scratch = (refs[:parts], refs[parts:])
    turned, held, sems = (scratch[:lefts], scratch[lefts:-1], scratch[-1])
    me_fsdp, me_tp = (place_ref[0], place_ref[1])
    rows = pieces[0].shape[1]
    started = []

    def start(target):
        for part, output, place, high, low in places:
            fsdp, tp = (me_fsdp ^ high, me_tp ^ low)
            for begin, size, which, per_tp, column in spans[part]:
                if which != target:
                    continue
                if target == len(products):
                    fsdp_count = extra_ref.shape[0] // 2
                    from_ref = extra_ref.at[tp * fsdp_count + fsdp]
                    row_span = pl.ds(0, extra_ref.shape[1])
                else:
                    row = pl.multiple_of(fsdp * rows, rows)
                    lane = pl.multiple_of(tp * per_tp + column, 128)
                    from_ref = held[target].at[pl.ds(row, rows), pl.ds(lane, size)]
                    row_span = pl.ds(0, rows)
                copy = pltpu.make_async_copy(
                    from_ref,
                    pieces[output].at[place, row_span, pl.ds(begin, size)],
                    sems.at[len(started)],
                )
                copy.start()
                started.append(copy)

    if extra:
        start(len(products))
    for at, left in enumerate(left_refs):
        turned[at][...] = left[...].T
    for target, (left, right) in enumerate(products):
        features = held[target].shape[0]
        for block in range(features // BLOCK):
            lines = slice(block * BLOCK, (block + 1) * BLOCK)
            held[target][lines] = dot_plain(turned[left][lines], right_refs[right][...]).astype(
                jnp.bfloat16
            )
        start(target)
    for copy in started:
        copy.wait()


def weight_grads(place, lefts, rights, products, spans, kinds, rows, part_widths, extra=None):
    length, features = lefts[0].shape
    places = scatter_places(kinds)
    copies = sum(len(spans[entry[0]]) for entry in places)
    devices = lax.axis_size("fsdp") * lax.axis_size("tp")
    outs = [low_shape(devices // 2, rows, part_widths[at // 2]) for at in range(2 * len(spans))]
    operands = list(lefts) + list(rights) + ([] if extra is None else [extra])
    flops = sum(2 * length * features * rights[right].shape[1] for _, right in products)
    return pl.pallas_call(
        partial(weight_grad_kernel, products, spans, places, extra is not None),
        in_specs=[SCALARS] + [whole(*operand.shape) for operand in operands],
        out_specs=[ANYWHERE] * len(outs),
        out_shape=outs,
        scratch_shapes=[pltpu.VMEM((features, length), jnp.bfloat16) for _ in lefts]
        + [pltpu.VMEM((features, rights[right].shape[1]), jnp.bfloat16) for _, right in products]
        + [pltpu.SemaphoreType.DMA((copies,))],
        compiler_params=pltpu.CompilerParams(vmem_limit_bytes=VMEM_LIMIT),
        cost_estimate=cost(flops, 16 << 20),
        name="weight_grads",
    )(place, *operands)


def input_grad_kernel(flip, place_ref, base_ref, *refs):
    grads, weight_ref, out_ref = (refs[:-2], refs[-2], refs[-1])
    total = base_ref[...]
    at = 0
    for grad in grads:
        width = grad.shape[1]
        total = total + dot_last(grad[...], weight_ref[:, at : at + width])
        at += width
    out_ref[...] = total.astype(jnp.bfloat16)


def input_grad(place, base, grads, full_qkv, flip):
    length, features = base.shape
    half = length // 2
    each = half // BLOCK
    line = lambda width: pl.BlockSpec(
        (BLOCK, width), lambda step, where: ((where[1] ^ flip) * each + step, 0)
    )
    return pl.pallas_call(
        partial(input_grad_kernel, flip),
        grid_spec=pltpu.PrefetchScalarGridSpec(
            num_scalar_prefetch=1,
            grid=(each,),
            in_specs=[line(features)]
            + [line(grad.shape[1]) for grad in grads]
            + [pl.BlockSpec(full_qkv.shape, lambda step, where: (0, 0))],
            out_specs=pl.BlockSpec((BLOCK, features), lambda step, where: (step, 0)),
        ),
        out_shape=low_shape(half, features),
        compiler_params=pltpu.CompilerParams(vmem_limit_bytes=VMEM_LIMIT),
        cost_estimate=cost(2 * half * features * full_qkv.shape[1], 14 << 20),
        name="input_grad",
    )(place, base, *grads, full_qkv)


def swap_in(pieces, tp_rank, *after):
    mine = lax.dynamic_index_in_dim(pieces, tp_rank, 0, keepdims=False)
    theirs = lax.dynamic_index_in_dim(pieces, 1 - tp_rank, 0, keepdims=False)
    if after:
        theirs = tie(theirs, *after)
    arrived = exchange(theirs, ACROSS)
    length = mine.shape[0]
    row = jnp.zeros((2 * length,) + mine.shape[1:], mine.dtype)
    row = lax.dynamic_update_slice_in_dim(row, mine, tp_rank * length, 0)
    return lax.dynamic_update_slice_in_dim(row, arrived, (1 - tp_rank) * length, 0)


def both_rows(mine, arrived, tp_rank):
    rows = jnp.zeros((2,) + mine.shape, mine.dtype)
    rows = lax.dynamic_update_slice_in_dim(rows, mine[None], tp_rank, 0)
    return lax.dynamic_update_slice_in_dim(rows, arrived[None], 1 - tp_rank, 0)


def on_device_rows(
    inputs,
    segment_ids,
    valid_mask,
    teacher,
    w_query,
    w_key,
    w_value,
    w_out,
    b_query,
    b_value,
    w_up,
    b_up,
    w_down,
    ln_gains,
    ln_shifts,
):
    seq_count, piece_len, features = inputs.shape
    fsdp_count, tp_count = (lax.axis_size("fsdp"), lax.axis_size("tp"))
    fsdp_rank, tp_rank = (lax.axis_index("fsdp"), lax.axis_index("tp"))
    devices = fsdp_count * tp_count
    assert seq_count == tp_count
    total_tokens = seq_count * piece_len * tp_count * fsdp_count
    shard_rows, local_width = w_query.shape
    local_hidden = w_up.shape[1]
    width = local_width * tp_count
    late_width = local_width // 4
    early_width = 3 * late_width
    half = local_width // 2
    pairs = width // 128
    late_pairs = pairs // 4
    early_pairs = pairs - late_pairs
    place = jnp.stack([fsdp_rank, tp_rank]).astype(jnp.int32)

    late_at = 2 * early_width
    qkv_spans = [
        [
            (0, early_width, 0, early_width, 0),
            (early_width, late_width, 0, late_width, late_at),
            (local_width, half, 1, early_width, width),
            (local_width + half, 128, 3, 0, 0),
        ],
        [
            (0, early_width - half, 1, early_width, width + half),
            (early_width - half, late_width, 1, late_width, width + late_at),
            (half, early_width, 2, early_width, 2 * width),
            (half + early_width, late_width, 2, late_width, 2 * width + late_at),
        ],
    ]
    small_rows = 32
    small = (
        b_query[None],
        b_value[None],
        b_up[None],
        ln_gains,
        ln_shifts,
        valid_mask,
    )
    up_cut = (local_hidden + local_width) // 2
    up_rest = local_hidden - up_cut
    up_spans = [
        [(0, up_cut, 0, local_hidden, 0)],
        [
            (0, up_rest, 0, local_hidden, up_cut),
            (up_rest, early_width, 1, early_width, 0),
            (up_rest + early_width, late_width, 1, late_width, late_at),
        ],
    ]
    qkv_first, qkv_second, up_shard, down_first, down_second = shards(
        place, w_query, w_key, w_value, w_out.T, w_up, w_down.T, small
    )
    chain_qkv = GatherChain([qkv_first, qkv_second])
    chain_down = GatherChain([down_first, down_second])
    row_low = swap_in(inputs, tp_rank)
    seg = lax.dynamic_index_in_dim(segment_ids, tp_rank, 0, keepdims=False)[:, None]
    chain_qkv.advance()
    chain_qkv.advance()
    chain_qkv.advance(row_low)
    gathered = lax.all_gather(
        tie(up_shard, chain_qkv.marks()), ("fsdp", "tp"), axis=0, tiled=False
    ).reshape(fsdp_count, tp_count, shard_rows, local_hidden + local_width)
    teacher_row = swap_in(teacher, tp_rank, chain_qkv.marks())
    chain_qkv.advance()
    chain_qkv.finish()
    chain_down.advance(chain_qkv.arrived)
    queries, keys, values, full_qkv, small_all = qkv_project(
        chain_qkv, qkv_spans, tie(place, chain_down.marks(), teacher_row), row_low, width, small_rows
    )
    valid_row = (
        lax.dynamic_slice(
            small_all.reshape(tp_count, fsdp_count, small_rows, 128),
            (0, fsdp_rank, MASK_ROW + tp_rank * (piece_len // 128), 0),
            (tp_count, 1, piece_len // 128, 128),
        )
        .reshape(-1)
        .astype(jnp.float32)
    )
    small_all = small_all.astype(jnp.float32)
    small_at = 2 * (local_width // 128)
    bias_up = small_all[:, small_at].reshape(1, -1)

    def feature_rows(columns, rows):
        return (
            columns[:fsdp_count]
            .reshape(fsdp_count, rows, features // fsdp_count)
            .transpose(1, 0, 2)
            .reshape(rows, features)
        )

    gains = feature_rows(small_all[:, small_at + 1], 2)
    shifts = feature_rows(small_all[:, small_at + 2 : small_at + 4], 4)
    valid_count = jnp.sum(small_all[:, small_at + 4, 0] * 256.0 + small_all[:, small_at + 4, 1])

    chain_down.advance(queries)
    queries = tie(queries, chain_down.marks())
    attended = attend(queries, keys, values, seg, 0, pairs // 2)
    chain_down.advance(attended)
    mixed, q_padded, k_padded = attend(
        queries, keys, tie(values, chain_down.marks()), seg, pairs // 2, pairs // 2, attended
    )
    weight = (valid_row * (total_tokens / valid_count))[:, None]
    chain_down.advance(mixed)
    vectors = jnp.stack([shifts[2], gains[0], shifts[0]])
    active, slope, unit_first, inverse_first, hidden_low, full_out = out_up_project(
        tie(mixed, chain_down.marks(), weight),
        row_low,
        gathered,
        vectors,
        bias_up,
        local_hidden,
        local_width,
    )
    chain_down.finish(active)
    vectors = jnp.stack([gains[0], shifts[0], shifts[3], gains[1], shifts[1]])
    result_low, grad_second, grad_down, sums_second = down_project(
        chain_down, place, active, unit_first, teacher_row, weight, vectors
    )

    weight_chain = chain_down
    chain_down = ScatterChain(
        *down_back(place, grad_down, active, shard_rows, local_hidden, "across"), "across"
    )
    mine = lax.dynamic_slice_in_dim(result_low, tp_rank * piece_len, piece_len, 0)
    theirs = lax.dynamic_slice_in_dim(result_low, (1 - tp_rank) * piece_len, piece_len, 0)
    arrived_out = exchange(theirs, ACROSS)
    grad_hidden, grad_b_up, kept, sent = up_back(
        place, tie(grad_down, chain_down.marks(), arrived_out), hidden_low, slope, weight_chain, gathered, "far"
    )
    chain_up = ScatterChain(kept, sent, "far")
    chain_down.advance(grad_hidden)
    grad_first, grad_attend, grad_mixed, sums_first = norm_back(
        grad_second, tie(grad_hidden, chain_down.marks(), chain_up.marks()), unit_first, inverse_first, gains[:1], full_out
    )
    back = partial(attend_back, q_padded, k_padded, values, mixed)
    chain_up.advance(grad_mixed)
    attend_grads = back(tie(grad_mixed, chain_up.marks()), 0, pairs, 0, pairs)
    advance_all([chain_up], attend_grads)

    def feature_pieces(rows):
        pieces = rows.reshape(rows.shape[0], fsdp_count, -1).transpose(1, 0, 2)
        pieces = pieces.reshape(fsdp_count, -1, 128)
        return jnp.concatenate([pieces] * tp_count, axis=0)

    def bias_pieces(grad):
        sums = jnp.sum(grad.astype(jnp.float32), axis=0)
        sums = [
            sums[:late_at].reshape(tp_count, -1),
            sums[late_at:].reshape(tp_count, -1),
        ]
        return jnp.concatenate(sums, axis=1).reshape(devices, -1)

    bias_pair = jnp.concatenate(
        [bias_pieces(attend_grads[0]), bias_pieces(attend_grads[2])], axis=1
    )
    bias_pair = jnp.pad(bias_pair, ((0, 0), (0, 128 - bias_pair.shape[1])))
    squares = jnp.sum(sums_second[3]) * (valid_count / total_tokens)
    lane = lax.broadcasted_iota(jnp.int32, (1, 128), 1)
    square_rows = jnp.concatenate(
        [
            jnp.where(lane == tp_rank * fsdp_count + fsdp_rank, term.astype(jnp.float32), 0.0)
            for term in split_three(squares)
        ],
        axis=0,
    )
    small = jnp.concatenate(
        [
            bias_pair[:, None],
            grad_b_up.reshape(devices, 1, 128),
            feature_pieces(
                jnp.stack(
                    [
                        sums_first[0],
                        sums_second[0],
                        sums_first[1],
                        sums_second[1],
                        sums_first[2],
                        sums_second[2],
                    ]
                )
            ),
            jnp.broadcast_to(square_rows[None], (devices, 3, 128)),
        ],
        axis=1,
    )
    small = jnp.pad(small, ((0, 0), (0, 16 - small.shape[1]), (0, 0)))
    def spans_of(start, target):
        return [
            (start, early_width, target, early_width, 0),
            (start + early_width, late_width, target, late_width, late_at),
        ]

    grad_spans = [
        spans_of(0, 0) + spans_of(local_width, 1) + [(2 * local_width, 128, 4, 0, 0)],
        spans_of(0, 2) + spans_of(local_width, 3),
    ]
    grad_kinds = ["side", "far_side"]
    pieces = weight_grads(
        place,
        [grad_attend, tie(row_low, chain_up.marks())],
        [mixed] + list(attend_grads),
        [(0, 0), (1, 1), (1, 2), (1, 3)],
        grad_spans,
        grad_kinds,
        shard_rows,
        [2 * local_width + 128, 2 * local_width],
        small.astype(jnp.bfloat16),
    )
    attend_chains = [
        ScatterChain(pieces[2 * at], pieces[2 * at + 1], kind)
        for at, kind in enumerate(grad_kinds)
    ]
    advance_all([chain_down], pieces)
    input_theirs = input_grad(
        place,
        tie(grad_first, chain_down.marks(), attend_chains[0].sent),
        attend_grads,
        full_qkv,
        1,
    )
    arrived_inputs = exchange(input_theirs, ACROSS)
    advance_all(attend_chains, input_theirs)
    input_mine = input_grad(
        place,
        tie(grad_first, [chain.marks() for chain in attend_chains]),
        attend_grads,
        full_qkv,
        0,
    )
    advance_all([chain_up, chain_down], input_mine)
    mine, arrived_out = tie((mine, arrived_out), chain_up.marks())
    hidden_out = both_rows(mine, arrived_out, tp_rank)
    advance_all(attend_chains, hidden_out)
    sent = [chain.marks() for chain in attend_chains]
    advance_all([chain_up, chain_down], sent)
    arrived_inputs = tie(arrived_inputs, sent)
    grad_inputs = both_rows(input_mine, arrived_inputs, tp_rank)
    while attend_chains[0].at < len(attend_chains[0].steps):
        advance_all(attend_chains, grad_inputs)
    sent = [chain.marks() for chain in attend_chains]
    grad_w_down = chain_down.finish(sent)
    grad_w_up = chain_up.finish(sent)
    first, second = [chain.finish() for chain in attend_chains]
    grad_w_out = first[:, :local_width].T
    grad_w_query = first[:, local_width : 2 * local_width]
    grad_w_key, grad_w_value = (second[:, :local_width], second[:, local_width:])
    own = first[:, 2 * local_width :]
    bias_size, row = (b_query.shape[0], 2)
    gain_rows = ln_gains.size // 128
    shift_rows = ln_shifts.size // 128
    loss_row = row + gain_rows + shift_rows
    loss_value = jnp.sum(own[loss_row : loss_row + 3]) / (features * valid_count)
    return (
        hidden_out,
        loss_value,
        grad_inputs,
        grad_w_query,
        grad_w_key,
        grad_w_value,
        grad_w_out,
        own[0, :bias_size],
        own[0, bias_size : 2 * bias_size],
        grad_w_up,
        own[1],
        grad_w_down.T,
        own[row : row + gain_rows].reshape(ln_gains.shape),
        own[row + gain_rows : loss_row].reshape(ln_shifts.shape),
    )


def solution(mesh):
    in_specs = (
        P("fsdp", "tp", None),
        P("fsdp", None),
        P("fsdp", "tp"),
        P("fsdp", "tp", None),
        P("fsdp", "tp"),
        P("fsdp", "tp"),
        P("fsdp", "tp"),
        P("tp", "fsdp"),
        P(("tp", "fsdp")),
        P(("tp", "fsdp")),
        P("fsdp", "tp"),
        P(("tp", "fsdp")),
        P("tp", "fsdp"),
        P(None, "fsdp"),
        P(None, "fsdp"),
    )
    out_specs = (
        P("fsdp", "tp", None),
        P(),
        P("fsdp", "tp", None),
        P("fsdp", "tp"),
        P("fsdp", "tp"),
        P("fsdp", "tp"),
        P("tp", "fsdp"),
        P(("tp", "fsdp")),
        P(("tp", "fsdp")),
        P("fsdp", "tp"),
        P(("tp", "fsdp")),
        P("tp", "fsdp"),
        P(None, "fsdp"),
        P(None, "fsdp"),
    )
    rows_plan = rows_plan_fits(mesh)
    return jax.shard_map(
        on_device_rows if rows_plan else on_device_heads, mesh=mesh, in_specs=in_specs, out_specs=out_specs, check_vma=False
    )
```

```python
from functools import partial
import math

import jax
import jax.numpy as jnp
from jax import lax
from jax.experimental import pallas as pl
from jax.experimental.pallas import tpu as pltpu
from jax.sharding import PartitionSpec as P

HEAD_DIM = 64
WINDOW = 512


EPSILON = 1e-05
MASKED = -1e30


def layer_norm_parts(values, gain_row, shift_row):
    centre = jnp.mean(values, axis=-1, keepdims=True)
    centred = values - centre
    inverse = lax.rsqrt(jnp.mean(centred * centred, axis=-1, keepdims=True) + EPSILON)
    normed = centred * inverse
    return (normed * gain_row + shift_row, normed, inverse)


def norm_backward(normed, inverse, gain_row, grad_out):
    scaled = grad_out * gain_row
    return inverse * (
        scaled
        - jnp.mean(scaled, axis=-1, keepdims=True)
        - normed * jnp.mean(scaled * normed, axis=-1, keepdims=True)
    )


def dot_first(left_side, right_side):
    return lax.dot_general(
        left_side, right_side, (((0,), (0,)), ((), ())), preferred_element_type=jnp.float32
    )


def dot_last(left_side, right_side):
    return lax.dot_general(
        left_side, right_side, (((1,), (1,)), ((), ())), preferred_element_type=jnp.float32
    )


def own_rows(source, offset_own, piece_len):
    return lax.dynamic_slice_in_dim(source, offset_own, piece_len, 1)


def allowed_mask(seg_row, offset, block_len):
    length = seg_row.shape[0]
    position = jnp.arange(length, dtype=jnp.int32)
    query_pos = offset + jnp.arange(block_len, dtype=jnp.int32)
    same_doc = seg_row[offset : offset + block_len][:, None] == seg_row[None, :]
    return same_doc & (jnp.abs(query_pos[:, None] - position[None, :]) < WINDOW)


def block_scores(query_part, key_heads, allowed):
    scores = jnp.einsum(
        "qhd,khd->hqk", query_part, key_heads, preferred_element_type=jnp.float32
    ) / math.sqrt(HEAD_DIM)
    return jnp.where(allowed[None], scores, MASKED)


def attention_forward(queries, key_all, value_all, segment_ids):
    seq_count, length = (queries.shape[0], queries.shape[1])
    block_len = min(512, length)
    outputs, summaries = ([], [])
    for row_index in range(seq_count):
        row_out, row_lse = ([], [])
        for offset in range(0, length, block_len):
            allowed = allowed_mask(segment_ids[row_index], offset, block_len)
            scores = block_scores(
                queries[row_index, offset : offset + block_len], key_all[row_index], allowed
            )
            row_top = jnp.max(scores, axis=-1, keepdims=True)
            raised = jnp.exp(scores - row_top)
            norm_sum = jnp.sum(raised, axis=-1, keepdims=True)
            softened = (raised / norm_sum).astype(jnp.bfloat16)
            row_out.append(
                jnp.einsum(
                    "hqk,khd->qhd",
                    softened,
                    value_all[row_index],
                    preferred_element_type=jnp.float32,
                )
            )
            row_lse.append(row_top + jnp.log(norm_sum))
        outputs.append(jnp.concatenate(row_out, axis=0))
        summaries.append(jnp.concatenate(row_lse, axis=1))
    return (jnp.stack(outputs), jnp.stack(summaries))


def attention_backward(queries, key_all, value_all, segment_ids, summaries, grad_mixed):
    seq_count, length = (queries.shape[0], queries.shape[1])
    block_len = min(512, length)
    root_dim = math.sqrt(HEAD_DIM)
    query_rows, key_rows, value_rows = ([], [], [])
    for row_index in range(seq_count):
        key_grad = jnp.zeros(key_all.shape[1:], jnp.float32)
        value_grad = jnp.zeros(value_all.shape[1:], jnp.float32)
        query_parts = []
        for offset in range(0, length, block_len):
            allowed = allowed_mask(segment_ids[row_index], offset, block_len)
            query_part = queries[row_index, offset : offset + block_len]
            scores = block_scores(query_part, key_all[row_index], allowed)
            softened = jnp.exp(scores - summaries[row_index, :, offset : offset + block_len])
            grad_part = grad_mixed[row_index, offset : offset + block_len]
            value_grad = value_grad + jnp.einsum(
                "hqk,qhd->khd",
                softened.astype(jnp.bfloat16),
                grad_part,
                preferred_element_type=jnp.float32,
            )
            grad_soft = jnp.einsum(
                "qhd,khd->hqk", grad_part, value_all[row_index], preferred_element_type=jnp.float32
            )
            grad_score = (
                softened * (grad_soft - jnp.sum(softened * grad_soft, axis=-1, keepdims=True))
            ).astype(jnp.bfloat16)
            query_parts.append(
                jnp.einsum(
                    "hqk,khd->qhd",
                    grad_score,
                    key_all[row_index],
                    preferred_element_type=jnp.float32,
                )
                / root_dim
            )
            key_grad = (
                key_grad
                + jnp.einsum(
                    "hqk,qhd->khd", grad_score, query_part, preferred_element_type=jnp.float32
                )
                / root_dim
            )
        query_rows.append(jnp.concatenate(query_parts, axis=0))
        key_rows.append(key_grad)
        value_rows.append(value_grad)
    return (jnp.stack(query_rows), jnp.stack(key_rows), jnp.stack(value_rows))


def on_device_heads(
    inputs,
    segment_ids,
    valid_mask,
    teacher,
    w_query,
    w_key,
    w_value,
    w_out,
    b_query,
    b_value,
    w_up,
    b_up,
    w_down,
    ln_gains,
    ln_shifts,
):
    seq_count, piece_len, features = inputs.shape
    tp_count = lax.axis_size("tp")
    tp_rank = lax.axis_index("tp")
    length = piece_len * tp_count
    total_tokens = seq_count * length * lax.axis_size("fsdp")
    offset_own = tp_rank * piece_len
    (
        full_query,
        full_key,
        full_value,
        full_out,
        full_bquery,
        full_bvalue,
        full_up,
        full_bup,
        full_down,
        full_gains,
        full_shifts,
    ) = (
        lax.all_gather(w_query, "fsdp", axis=0, tiled=True),
        lax.all_gather(w_key, "fsdp", axis=0, tiled=True),
        lax.all_gather(w_value, "fsdp", axis=0, tiled=True),
        lax.all_gather(w_out, "fsdp", axis=1, tiled=True),
        lax.all_gather(b_query, "fsdp", axis=0, tiled=True),
        lax.all_gather(b_value, "fsdp", axis=0, tiled=True),
        lax.all_gather(w_up, "fsdp", axis=0, tiled=True),
        lax.all_gather(b_up, "fsdp", axis=0, tiled=True),
        lax.all_gather(w_down, "fsdp", axis=1, tiled=True),
        lax.all_gather(ln_gains, "fsdp", axis=1, tiled=True),
        lax.all_gather(ln_shifts, "fsdp", axis=1, tiled=True),
    )
    gains = full_gains.astype(jnp.float32)
    shifts = full_shifts.astype(jnp.float32)
    local_width = full_query.shape[1]
    head_local = local_width // HEAD_DIM
    token_count = seq_count * length
    token_full = lax.all_gather(inputs, "tp", axis=1, tiled=True)
    flat_in = token_full.reshape(token_count, features)
    query_flat = (
        jnp.dot(flat_in, full_query, preferred_element_type=jnp.float32)
        + full_bquery.astype(jnp.float32)
    ).astype(jnp.bfloat16)
    key_flat = jnp.dot(flat_in, full_key, preferred_element_type=jnp.float32).astype(jnp.bfloat16)
    value_flat = (
        jnp.dot(flat_in, full_value, preferred_element_type=jnp.float32)
        + full_bvalue.astype(jnp.float32)
    ).astype(jnp.bfloat16)
    head_shape = (seq_count, length, head_local, HEAD_DIM)
    query_heads = query_flat.reshape(head_shape)
    key_heads = key_flat.reshape(head_shape)
    value_heads = value_flat.reshape(head_shape)
    mixed_heads, summaries = attention_forward(query_heads, key_heads, value_heads, segment_ids)
    mixed_low = mixed_heads.reshape(token_count, local_width).astype(jnp.bfloat16)
    attend_part = jnp.dot(mixed_low, full_out, preferred_element_type=jnp.float32).reshape(
        seq_count, length, features
    )
    attend_all = lax.psum(attend_part.astype(jnp.bfloat16), "tp").astype(jnp.float32)
    pre_first = token_full.astype(jnp.float32) + attend_all + shifts[2]
    normed_first, unit_first, inverse_first = layer_norm_parts(pre_first, gains[0], shifts[0])
    hidden_full = normed_first.astype(jnp.bfloat16)
    normed_own = own_rows(normed_first, offset_own, piece_len)
    hidden_flat = hidden_full.reshape(token_count, features)
    up_all = jnp.dot(hidden_flat, full_up, preferred_element_type=jnp.float32) + full_bup.astype(
        jnp.float32
    )
    active = jax.nn.gelu(up_all, approximate=False).astype(jnp.bfloat16)
    down_part = jnp.dot(active, full_down, preferred_element_type=jnp.float32).reshape(
        seq_count, length, features
    )
    down_own = lax.psum_scatter(
        down_part.astype(jnp.bfloat16), "tp", scatter_dimension=1, tiled=True
    ).astype(jnp.float32)
    pre_second = normed_own + down_own + shifts[3]
    result, unit_second, inverse_second = layer_norm_parts(pre_second, gains[1], shifts[1])
    differ = result - teacher.astype(jnp.float32)
    mask_float = valid_mask.astype(jnp.float32)[..., None]
    squares, valid_count = lax.psum(
        (jnp.sum(mask_float * differ * differ), jnp.sum(mask_float)), ("fsdp", "tp")
    )
    loss_value = squares / (features * valid_count)
    grad_result = mask_float * differ * (total_tokens / valid_count)
    grad_second = norm_backward(unit_second, inverse_second, gains[1], grad_result)
    grad_down_full = lax.all_gather(grad_second.astype(jnp.bfloat16), "tp", axis=1, tiled=True)
    grad_down_flat = grad_down_full.reshape(token_count, features)
    weight_down = dot_first(active, grad_down_flat)
    grad_active = dot_last(grad_down_flat, full_down)
    gelu_back = jax.vjp(partial(jax.nn.gelu, approximate=False), up_all)[1]
    grad_up = gelu_back(grad_active)[0].astype(jnp.bfloat16)
    weight_up = dot_first(hidden_flat, grad_up)
    bias_up = jnp.sum(grad_up.astype(jnp.float32), axis=0)
    hidden_part = dot_last(grad_up, full_up).reshape(seq_count, length, features)
    current = own_rows(hidden_part, offset_own, piece_len)
    hidden_part = lax.dynamic_update_slice_in_dim(hidden_part, current + grad_second, offset_own, 1)
    grad_hidden_all = lax.psum(hidden_part.astype(jnp.bfloat16), "tp").astype(jnp.float32)
    grad_first_all = norm_backward(unit_first, inverse_first, gains[0], grad_hidden_all)
    grad_mix_full = grad_first_all.astype(jnp.bfloat16)
    grad_first_own = own_rows(grad_first_all, offset_own, piece_len)
    grad_hidden_own = own_rows(grad_hidden_all, offset_own, piece_len)
    unit_first_own = own_rows(unit_first, offset_own, piece_len)
    grad_mix_flat = grad_mix_full.reshape(token_count, features)
    weight_out = dot_first(mixed_low, grad_mix_flat)
    grad_mixed = dot_last(grad_mix_flat, full_out).astype(jnp.bfloat16).reshape(head_shape)
    grad_query, grad_key, grad_value = attention_backward(
        query_heads, key_heads, value_heads, segment_ids, summaries, grad_mixed
    )
    query_low = grad_query.astype(jnp.bfloat16).reshape(token_count, local_width)
    key_low = grad_key.astype(jnp.bfloat16).reshape(token_count, local_width)
    value_low = grad_value.astype(jnp.bfloat16).reshape(token_count, local_width)
    weight_query = dot_first(flat_in, query_low)
    weight_key = dot_first(flat_in, key_low)
    weight_value = dot_first(flat_in, value_low)
    bias_query = jnp.sum(query_low.astype(jnp.float32), axis=0)
    bias_value = jnp.sum(value_low.astype(jnp.float32), axis=0)
    input_part = (
        dot_last(query_low, full_query)
        + dot_last(key_low, full_key)
        + dot_last(value_low, full_value)
    )
    grad_inputs = (
        lax.psum_scatter(
            input_part.reshape(seq_count, length, features).astype(jnp.bfloat16),
            "tp",
            scatter_dimension=1,
            tiled=True,
        ).astype(jnp.float32)
        + grad_first_own
    )
    gain_part = jnp.stack(
        [
            jnp.sum(grad_hidden_own * unit_first_own, axis=(0, 1)),
            jnp.sum(grad_result * unit_second, axis=(0, 1)),
        ]
    )
    shift_part = jnp.stack(
        [
            jnp.sum(grad_hidden_own, axis=(0, 1)),
            jnp.sum(grad_result, axis=(0, 1)),
            jnp.sum(grad_first_own, axis=(0, 1)),
            jnp.sum(grad_second, axis=(0, 1)),
        ]
    )
    gain_sum, shift_sum = lax.psum((gain_part, shift_part), "tp")
    gradients = (
        lax.psum_scatter(
            weight_query.astype(jnp.bfloat16), "fsdp", scatter_dimension=0, tiled=True
        ).astype(jnp.float32),
        lax.psum_scatter(
            weight_key.astype(jnp.bfloat16), "fsdp", scatter_dimension=0, tiled=True
        ).astype(jnp.float32),
        lax.psum_scatter(
            weight_value.astype(jnp.bfloat16), "fsdp", scatter_dimension=0, tiled=True
        ).astype(jnp.float32),
        lax.psum_scatter(
            weight_out.astype(jnp.bfloat16), "fsdp", scatter_dimension=1, tiled=True
        ).astype(jnp.float32),
        lax.psum_scatter(
            bias_query.astype(jnp.bfloat16), "fsdp", scatter_dimension=0, tiled=True
        ).astype(jnp.float32),
        lax.psum_scatter(
            bias_value.astype(jnp.bfloat16), "fsdp", scatter_dimension=0, tiled=True
        ).astype(jnp.float32),
        lax.psum_scatter(
            weight_up.astype(jnp.bfloat16), "fsdp", scatter_dimension=0, tiled=True
        ).astype(jnp.float32),
        lax.psum_scatter(
            bias_up.astype(jnp.bfloat16), "fsdp", scatter_dimension=0, tiled=True
        ).astype(jnp.float32),
        lax.psum_scatter(
            weight_down.astype(jnp.bfloat16), "fsdp", scatter_dimension=1, tiled=True
        ).astype(jnp.float32),
        lax.psum_scatter(
            gain_sum.astype(jnp.bfloat16), "fsdp", scatter_dimension=1, tiled=True
        ).astype(jnp.float32),
        lax.psum_scatter(
            shift_sum.astype(jnp.bfloat16), "fsdp", scatter_dimension=1, tiled=True
        ).astype(jnp.float32),
    )
    return (
        result.astype(jnp.bfloat16),
        loss_value,
        grad_inputs.astype(jnp.bfloat16),
        gradients[0],
        gradients[1],
        gradients[2],
        gradients[3],
        gradients[4],
        gradients[5],
        gradients[6],
        gradients[7],
        gradients[8],
        gradients[9],
        gradients[10],
    )


BLOCK = 256
LOG2E = math.log2(math.e)
SHARD_ROWS_PARTS = 2


def rows_plan_fits(mesh):
    fsdp_count, tp_count = (mesh.shape["fsdp"], mesh.shape["tp"])
    return tp_count == 2 and fsdp_count >= 8 and fsdp_count & (fsdp_count - 1) == 0


def dot_plain(left_side, right_side):
    return lax.dot_general(
        left_side, right_side, (((1,), (0,)), ((), ())), preferred_element_type=jnp.float32
    )


def exchange(values, move):
    tp_count = lax.axis_size("tp")
    count = lax.axis_size("fsdp") * tp_count
    flip = move[0] * tp_count + move[1]
    if move[1] == 0:
        return lax.ppermute(
            values, "fsdp", [(at, at ^ move[0]) for at in range(lax.axis_size("fsdp"))]
        )
    return lax.ppermute(values, ("fsdp", "tp"), [(at, at ^ flip) for at in range(count)])


ACROSS = (0, 1)
CORE = (1, 0)
SIDE = (2, 0)


def far_moves():
    places = lax.axis_size("fsdp").bit_length() - 1
    return [(1 << place, 0) for place in range(places - 1, 1, -1)]


def gather_steps():
    far = far_moves()
    return (tuple(far) + (ACROSS, SIDE), (far[0], ACROSS, SIDE) + tuple(far[1:]))


def scatter_steps(kind):
    far = list(reversed(far_moves()))
    if kind == "late":
        return ((SIDE,), (ACROSS,), tuple(reversed(far)))
    moves = {
        "across": [ACROSS, SIDE] + far,
        "side": [SIDE, ACROSS] + far,
        "far": far[:1] + [ACROSS, SIDE] + far[1:],
        "far_side": far[:1] + [SIDE] + far[1:] + [ACROSS],
    }[kind]
    return tuple((move,) for move in moves)


def moves_of(step):
    found = [(0, 0)]
    for high, low in reversed(step):
        found = found + [(one ^ high, two ^ low) for one, two in found]
    return found


def step_masks(steps):
    masks = [(0, 0)]
    for step in steps:
        masks = [
            (high ^ one, low ^ two) for one, two in moves_of(step) for high, low in masks
        ]
    return masks


def tie(values, *others):
    return lax.optimization_barrier((values, others))[0]


class GatherChain:

    def __init__(self, parts):
        self.steps = gather_steps()
        self.held = [part[None] for part in parts]
        self.arrived = None
        self.at = 0

    def advance(self, *after):
        if self.arrived is not None:
            self.held, self.arrived = tie((self.held, self.arrived), *after)
            self.held = [
                jnp.concatenate(pair, axis=0) for pair in zip(self.held, self.arrived)
            ]
        else:
            self.held = tie(self.held, *after)
        self.arrived = [
            exchange(held, steps[self.at]) for held, steps in zip(self.held, self.steps)
        ]
        self.at += 1

    def finish(self, *after):
        if after:
            self.arrived = tie(self.arrived, *after)
        self.pieces = []
        for held, arrived in zip(self.held, self.arrived):
            near = [held, arrived]
            self.pieces.append(near + [exchange(piece, CORE) for piece in near])

    def marks(self):
        return self.held

    def sources(self):
        return [piece for part in self.pieces for piece in part]

    def places(self):
        found = []
        for part, steps in enumerate(self.steps):
            masks = step_masks([(move,) for move in steps])
            size = len(masks) // 2
            for at in range(4):
                for place, (high, low) in enumerate(masks[at % 2 * size : (at % 2 + 1) * size]):
                    flip = CORE[0] if at >= 2 else 0
                    found.append((part, part * 4 + at, place, high ^ flip, low))
        return found


def scatter_places(kinds):
    found = []
    for part, kind in enumerate(kinds):
        masks = step_masks(tuple(reversed(scatter_steps(kind))))
        for at, flip in enumerate((0, CORE[0])):
            for place, (high, low) in enumerate(masks):
                found.append((part, part * 2 + at, place, high ^ flip, low))
    return found


class ScatterChain:

    def __init__(self, kept, sent, kind):
        self.steps = scatter_steps(kind)
        self.sent = [sent]
        self.terms = [kept, exchange(sent, CORE)]
        self.size = kept.shape[0]
        self.at = 0

    def total(self, first):
        terms = [term[first : first + self.size].astype(jnp.float32) for term in self.terms]
        return sum(terms[1:], terms[0])

    def advance(self, *after):
        self.terms = tie(self.terms, *after)
        moves = moves_of(self.steps[self.at])
        self.size //= len(moves)
        self.sent = [
            self.total(at * self.size).astype(jnp.bfloat16) for at in range(1, len(moves))
        ]
        self.terms = self.terms + [
            exchange(sent, move) for sent, move in zip(self.sent, moves[1:])
        ]
        self.at += 1

    def finish(self, *after):
        self.terms = tie(self.terms, *after)
        return self.total(0)[0]

    def marks(self):
        return self.sent


def advance_all(chains, *after):
    terms = tie([chain.terms for chain in chains], *after)
    for chain, found in zip(chains, terms):
        chain.terms = found
        chain.advance()


ANYWHERE = pl.BlockSpec(memory_space=pl.ANY)
SCALARS = pl.BlockSpec(memory_space=pltpu.SMEM)
VMEM_LIMIT = 58 << 20


def cost(flops, moved, transcendentals=0):
    return pl.CostEstimate(flops=flops // 2000, bytes_accessed=moved // 2000, transcendentals=0)


def low_shape(*shape):
    return jax.ShapeDtypeStruct(shape, jnp.bfloat16)


def wide_shape(*shape):
    return jax.ShapeDtypeStruct(shape, jnp.float32)


def whole(*shape):
    return pl.BlockSpec(shape, lambda *step: (0,) * len(shape))


def block_span(block, count):
    reach = -(-WINDOW // BLOCK)
    return max(0, block - reach), min(count - 1, block + reach)


def split_three(values):
    high = values.astype(jnp.bfloat16)
    rest = values - high.astype(jnp.float32)
    mid = rest.astype(jnp.bfloat16)
    low = (rest - mid.astype(jnp.float32)).astype(jnp.bfloat16)
    return high, mid, low


def window_edge(tile, row_block, column_block):
    if (abs(row_block - column_block) + 1) * BLOCK - 1 < WINDOW:
        return tile
    row = lax.broadcasted_iota(jnp.int32, tile.shape, 0) + row_block * BLOCK
    column = lax.broadcasted_iota(jnp.int32, tile.shape, 1) + column_block * BLOCK
    return jnp.where(jnp.abs(row - column) < WINDOW, tile, MASKED)


def attend_kernel(seg_ref, q_ref, k_ref, v_ref, out_ref, qx_ref, kx_ref, held_ref):
    length = q_ref.shape[0]
    count = length // BLOCK
    lane = lax.broadcasted_iota(jnp.int32, (length, 128), 1)
    seg = seg_ref[...]
    q_heads, k_heads, v_heads = ([], [], [])
    for head in range(2):
        own = (lane < 64) if head == 0 else (lane >= 64)
        extra = lane - 64 if head == 0 else lane
        same = extra == seg
        q_extra = jnp.where(same, 1.0, 0.0).astype(jnp.bfloat16)
        k_extra = jnp.where(
            extra < 4, jnp.where(same, 0.0, MASKED), jnp.where(extra < 7, -1.0, 0.0)
        ).astype(jnp.bfloat16)
        v_extra = jnp.where(extra == 0, 1.0, 0.0).astype(jnp.bfloat16)
        q_heads.append(jnp.where(own, q_ref[...], q_extra))
        k_heads.append(jnp.where(own, k_ref[...], k_extra))
        v_heads.append(jnp.where(own, v_ref[...], v_extra))
        kx_ref[head] = k_heads[head]
    units = [(head, block) for head in range(2) for block in range(count)]

    def score(unit):
        head, block = unit
        low, high = block_span(block, count)
        rows = slice(block * BLOCK, (block + 1) * BLOCK)
        tile = dot_last(q_heads[head][rows], k_heads[head][low * BLOCK : (high + 1) * BLOCK])
        return [
            window_edge(tile[:, (at - low) * BLOCK : (at - low + 1) * BLOCK], block, at)
            for at in range(low, high + 1)
        ]

    def finish(unit, tiles):
        head, block = unit
        low, high = block_span(block, count)
        rows = slice(block * BLOCK, (block + 1) * BLOCK)
        most = tiles[0]
        for tile in tiles[1:]:
            most = jnp.maximum(most, tile)
        top = jnp.max(most, axis=1, keepdims=True)
        raised = jnp.concatenate(
            [jnp.exp2(tile - top).astype(jnp.bfloat16) for tile in tiles], axis=1
        )
        mixed = dot_plain(raised, v_heads[head][low * BLOCK : (high + 1) * BLOCK])
        norm_sum = mixed[:, 64:65] if head == 0 else mixed[:, 0:1]
        held_ref[head, rows, :] = mixed * (1.0 / norm_sum)
        first, second, third = split_three(top + jnp.log2(norm_sum))
        extra = lane[:BLOCK] - 64 if head == 0 else lane[:BLOCK]
        qx_ref[head, rows, :] = jnp.where(
            extra == 4,
            first,
            jnp.where(extra == 5, second, jnp.where(extra == 6, third, q_heads[head][rows])),
        )

    tiles = score(units[0])
    for at, unit in enumerate(units):
        following = score(units[at + 1]) if at + 1 < len(units) else None
        finish(unit, tiles)
        tiles = following
    out_ref[...] = jnp.where(lane < 64, held_ref[0], held_ref[1]).astype(jnp.bfloat16)


def attend(queries, keys, values, seg, first, count, earlier=None):
    length, width = queries.shape
    pair = pl.BlockSpec((length, 128), lambda step: (0, first + step))
    padded = pl.BlockSpec((2, length, 128), lambda step: (first + step, 0, 0))
    passed = 0 if earlier is None else 3
    operands = (seg, queries, keys, values) + (earlier or ())

    def kernel(seg_ref, q_ref, k_ref, v_ref, *refs):
        attend_kernel(seg_ref, q_ref, k_ref, v_ref, *refs[passed:])

    return pl.pallas_call(
        kernel,
        grid=(count,),
        in_specs=[pl.BlockSpec((length, 1), lambda step: (0, 0)), pair, pair, pair]
        + [pl.BlockSpec(memory_space=pl.ANY)] * passed,
        out_specs=[pair, padded, padded],
        out_shape=[
            jax.ShapeDtypeStruct((length, width), jnp.bfloat16),
            jax.ShapeDtypeStruct((width // HEAD_DIM, length, 128), jnp.bfloat16),
            jax.ShapeDtypeStruct((width // HEAD_DIM, length, 128), jnp.bfloat16),
        ],
        scratch_shapes=[pltpu.VMEM((2, length, 128), jnp.float32)],
        input_output_aliases={4 + at: at for at in range(passed)},
        compiler_params=pltpu.CompilerParams(vmem_limit_bytes=VMEM_LIMIT),
        cost_estimate=cost(3_500_000_000 * count, (2 << 20) * count),
        name="attend",
    )(*operands)


def attend_back_kernel(qx_ref, kx_ref, v_ref, out_ref, grad_ref, dq_ref, dk_ref, dv_ref, held_ref):
    length = v_ref.shape[0]
    count = length // BLOCK
    lane = lax.broadcasted_iota(jnp.int32, (length, 128), 1)
    grad = grad_ref[...]
    for head in range(2):
        mine = slice(head * 64, (head + 1) * 64)
        own = (lane < 64) if head == 0 else (lane >= 64)
        extra = lane - 64 if head == 0 else lane
        product = jnp.where(
            own, grad.astype(jnp.float32) * out_ref[...].astype(jnp.float32), 0.0
        )
        first, second, third = split_three(-jnp.sum(product, axis=1, keepdims=True))
        grad_head = jnp.where(
            own,
            grad,
            jnp.where(
                extra == 0,
                first,
                jnp.where(extra == 1, second, jnp.where(extra == 2, third, jnp.zeros_like(grad))),
            ),
        )
        v_head = jnp.where(own, v_ref[...], jnp.where(extra < 3, 1.0, 0.0).astype(jnp.bfloat16))
        q_head, k_head = (qx_ref[head], kx_ref[head])
        k_turned = k_head.T[mine]
        for block in range(count):
            low, high = block_span(block, count)
            keys = slice(block * BLOCK, (block + 1) * BLOCK)
            span = slice(low * BLOCK, (high + 1) * BLOCK)
            tile = dot_last(k_head[keys], q_head[span])
            soft = jnp.concatenate(
                [
                    jnp.exp2(
                        window_edge(tile[:, (at - low) * BLOCK : (at - low + 1) * BLOCK], block, at)
                    )
                    for at in range(low, high + 1)
                ],
                axis=1,
            )
            grad_soft = dot_last(v_head[keys], grad_head[span])
            grad_score = (soft * grad_soft).astype(jnp.bfloat16)
            grad_value = dot_plain(soft.astype(jnp.bfloat16), grad_head[span])
            grad_key = dot_plain(grad_score, q_head[span]) * (1.0 / LOG2E)
            dv_ref[keys, mine] = grad_value[:, mine].astype(jnp.bfloat16)
            dk_ref[keys, mine] = grad_key[:, mine].astype(jnp.bfloat16)
            grad_query = dot_plain(k_turned[:, keys], grad_score)
            if block == 0:
                held_ref[mine, span] = grad_query
                if high + 1 < count:
                    held_ref[mine, (high + 1) * BLOCK :] = jnp.zeros(
                        (64, length - (high + 1) * BLOCK), jnp.float32
                    )
            else:
                held_ref[mine, span] += grad_query
    dq_ref[...] = (held_ref[...] * (1.0 / math.sqrt(HEAD_DIM))).T.astype(jnp.bfloat16)


def attend_back(
    q_padded, k_padded, values, mixed, grad_mixed, first, count, out_first, out_count, earlier=None
):
    length, width = values.shape
    pair = pl.BlockSpec((length, 128), lambda step: (0, first + step))
    out_pair = pl.BlockSpec((length, 128), lambda step: (0, first - out_first + step))
    padded = pl.BlockSpec((2, length, 128), lambda step: (first + step, 0, 0))
    passed = 0 if earlier is None else 3
    operands = (q_padded, k_padded, values, mixed, grad_mixed) + tuple(earlier or ())

    def kernel(qx_ref, kx_ref, v_ref, out_ref, grad_ref, *refs):
        attend_back_kernel(qx_ref, kx_ref, v_ref, out_ref, grad_ref, *refs[passed:])

    return pl.pallas_call(
        kernel,
        grid=(count,),
        in_specs=[padded, padded, pair, pair, pair]
        + [pl.BlockSpec(memory_space=pl.ANY)] * passed,
        out_specs=[out_pair, out_pair, out_pair],
        out_shape=[jax.ShapeDtypeStruct((length, 128 * out_count), jnp.bfloat16)] * 3,
        scratch_shapes=[pltpu.VMEM((128, length), jnp.float32)],
        input_output_aliases={5 + at: at for at in range(passed)},
        compiler_params=pltpu.CompilerParams(vmem_limit_bytes=VMEM_LIMIT),
        cost_estimate=cost(5_000_000_000 * count, (2 << 20) * count),
        name="attend_back",
    )(*operands)


MASK_ROW = 16


def shards_kernel(
    place_ref, wq_ref, wk_ref, wv_ref, wo_ref, wu_ref, wd_ref, bq_ref, bv_ref, bu_ref, gain_ref,
    shift_ref, mask_ref, first_ref, second_ref, wide_ref, low_ref, high_ref,
):
    rows, width = wq_ref.shape
    half = width // 2
    first_ref[:, :width] = wq_ref[...]
    first_ref[:, width : width + half] = wk_ref[:, :half]
    second_ref[:, :half] = wk_ref[:, half:]
    second_ref[:, half:] = wv_ref[...]
    lane = lax.broadcasted_iota(jnp.int32, (1, 128), 1)

    def spread(ref):
        values = ref[...].astype(jnp.float32)
        size = values.shape[1]
        lanes = jnp.concatenate([values] * (128 // size), axis=1)
        return [
            jnp.where((row * 128 + lane) // size == place_ref[0], lanes, 0.0)
            for row in range(width // 128)
        ]

    def flat(ref):
        values = ref[...].astype(jnp.float32)
        return [
            jnp.concatenate([values[at : at + 1], values[at + 1 : at + 2]], axis=1)
            for at in range(0, values.shape[0], 2)
        ]

    count = jnp.sum(mask_ref[...].astype(jnp.float32))
    high = jnp.floor(count / 256.0)
    count_row = jnp.where(lane == 0, high, jnp.where(lane == 1, count - 256.0 * high, 0.0))
    lines = spread(bq_ref) + spread(bv_ref) + [bu_ref[...].astype(jnp.float32)]
    lines = lines + flat(gain_ref) + flat(shift_ref) + [count_row]
    lines = lines + [jnp.zeros((1, 128), jnp.float32)] * (MASK_ROW - len(lines))
    mask = mask_ref[...].astype(jnp.float32)
    for row in range(mask.shape[0]):
        lines = lines + [
            mask[row : row + 1, at : at + 128] for at in range(0, mask.shape[1], 128)
        ]
    lines = lines + [jnp.zeros((1, 128), jnp.float32)] * (rows - len(lines))
    first_ref[:, width + half :] = jnp.concatenate(lines, axis=0).astype(jnp.bfloat16)
    wide_ref[:, : wu_ref.shape[1]] = wu_ref[...]
    wide_ref[:, wu_ref.shape[1] :] = wo_ref[...]
    cut = low_ref.shape[1]
    low_ref[...] = wd_ref[:, :cut]
    high_ref[...] = wd_ref[:, cut:]


def shards(place, w_query, w_key, w_value, w_out, w_up, w_down, small):
    rows, width = w_query.shape
    hidden = w_up.shape[1]
    operands = (w_query, w_key, w_value, w_out, w_up, w_down) + small
    outs = [
        low_shape(rows, width + width // 2 + 128),
        low_shape(rows, width // 2 + width),
        low_shape(rows, hidden + width),
        low_shape(rows, hidden // 2 + 128),
        low_shape(rows, hidden // 2 - 128),
    ]
    return pl.pallas_call(
        shards_kernel,
        in_specs=[SCALARS] + [whole(*operand.shape) for operand in operands],
        out_specs=[whole(*out.shape) for out in outs],
        out_shape=outs,
        compiler_params=pltpu.CompilerParams(vmem_limit_bytes=VMEM_LIMIT),
        cost_estimate=cost(0, 2 << 20),
        name="shards",
    )(place, *operands)


def qkv_kernel(spans, places, place_ref, row_ref, *refs):
    count = 1 + max(source for _, source, _, _, _ in places)
    sources = refs[:count]
    q_ref, k_ref, v_ref, full_ref, small_out, held, small, sems, out_sem = refs[count:]
    me_fsdp, me_tp = (place_ref[0], place_ref[1])
    rows = sources[0].shape[1]
    width = q_ref.shape[1]
    fsdp_count = held.shape[0] // rows
    copies = {0: [], 1: [], 2: [], 3: []}
    for part, source, place, high, low in places:
        fsdp, tp = (me_fsdp ^ high, me_tp ^ low)
        for start, size, target, per_tp, column in spans[part]:
            if target == 3:
                from_ref = sources[source].at[place, pl.ds(0, small.shape[1]), pl.ds(start, size)]
                to_ref = small.at[tp * fsdp_count + fsdp]
            else:
                row = pl.multiple_of(fsdp * rows, rows)
                lane = pl.multiple_of(tp * per_tp + column, 128)
                from_ref = sources[source].at[place, :, pl.ds(start, size)]
                to_ref = held.at[pl.ds(row, rows), pl.ds(lane, size)]
            total = sum(len(group) for group in copies.values())
            copies[target].append(pltpu.make_async_copy(from_ref, to_ref, sems.at[total]))
            copies[target][-1].start()

    def bias(first):
        halves = [
            jnp.sum(
                small[tp * fsdp_count : (tp + 1) * fsdp_count].astype(jnp.float32), axis=0
            )
            for tp in range(2)
        ]
        count = width // 256
        lanes = [
            half[first + at : first + at + 1]
            for group in (range(count - 1), (count - 1,))
            for half in halves
            for at in group
        ]
        return jnp.concatenate(lanes, axis=1)

    scale = LOG2E / math.sqrt(HEAD_DIM)
    for copy in copies[3]:
        copy.wait()
    out_copies = [pltpu.make_async_copy(small, small_out, out_sem.at[3])]
    out_copies[0].start()
    for target, out_ref in ((0, q_ref), (1, k_ref), (2, v_ref)):
        for copy in copies[target]:
            copy.wait()
        span = pl.ds(target * width, width)
        out_copies.append(
            pltpu.make_async_copy(held.at[:, span], full_ref.at[:, span], out_sem.at[target])
        )
        out_copies[-1].start()
        added = bias(0 if target == 0 else width // 256) if target != 1 else None
        for block in range(row_ref.shape[0] // BLOCK):
            lines = slice(block * BLOCK, (block + 1) * BLOCK)
            found = dot_plain(row_ref[lines], held[:, target * width : (target + 1) * width])
            if added is not None:
                found = found + added
            if target == 0:
                found = found * scale
            out_ref[lines] = found.astype(jnp.bfloat16)
    for copy in out_copies:
        copy.wait()


def qkv_project(chain, spans, place, row_low, width, small_rows):
    length, features = row_low.shape
    sources = chain.sources()
    places = chain.places()
    devices = lax.axis_size("fsdp") * lax.axis_size("tp")
    copies = sum(len(spans[entry[0]]) for entry in places)
    return pl.pallas_call(
        partial(qkv_kernel, spans, places),
        in_specs=[SCALARS, whole(length, features)] + [ANYWHERE] * len(sources),
        out_specs=[whole(length, width)] * 3 + [ANYWHERE] * 2,
        out_shape=[low_shape(length, width)] * 3
        + [low_shape(features, 3 * width), low_shape(devices, small_rows, 128)],
        scratch_shapes=[
            pltpu.VMEM((features, 3 * width), jnp.bfloat16),
            pltpu.VMEM((devices, small_rows, 128), jnp.bfloat16),
            pltpu.SemaphoreType.DMA((copies,)),
            pltpu.SemaphoreType.DMA((4,)),
        ],
        compiler_params=pltpu.CompilerParams(vmem_limit_bytes=VMEM_LIMIT),
        cost_estimate=cost(6 * length * features * width, 24 << 20),
        name="qkv_project",
    )(place, row_low, *sources)


def unit_of(values):
    centred = values - jnp.mean(values, axis=-1, keepdims=True)
    inverse = lax.rsqrt(jnp.mean(centred * centred, axis=-1, keepdims=True) + EPSILON)
    return centred * inverse, inverse


def out_up_kernel(
    mixed_ref, row_ref, out_w_ref, up_w_ref, vector_ref, b_ref,
    active_ref, slope_ref, unit_ref, inverse_ref, hidden_ref, full_out_ref,
):
    length, features = row_ref.shape
    late = out_w_ref.shape[3] // 4
    early = 3 * late

    @pl.when(pl.program_id(0) == 0)
    def _():
        for tp in range(2):
            lanes = pl.ds(tp * early, early)
            full_out_ref[:, lanes] = out_w_ref[:, tp, :, :early].reshape(features, early)
            lanes = pl.ds(2 * early + tp * late, late)
            full_out_ref[:, lanes] = out_w_ref[:, tp, :, early:].reshape(features, late)
        for block in range(length // BLOCK):
            lines = slice(block * BLOCK, (block + 1) * BLOCK)
            before = (
                row_ref[lines].astype(jnp.float32)
                + dot_last(mixed_ref[lines], full_out_ref[...])
                + vector_ref[0:1]
            )
            unit, inverse = unit_of(before)
            unit_ref[lines] = unit
            inverse_ref[lines] = inverse
            hidden_ref[lines] = (unit * vector_ref[1:2] + vector_ref[2:3]).astype(jnp.bfloat16)

    weight = up_w_ref[:, 0].reshape(features, up_w_ref.shape[3])

    def product(block):
        lines = slice(block * BLOCK, (block + 1) * BLOCK)
        return dot_plain(hidden_ref[lines], weight) + b_ref[...]

    up = product(0)
    count = length // BLOCK
    for block in range(count):
        following = product(block + 1) if block + 1 < count else None
        lines = slice(block * BLOCK, (block + 1) * BLOCK)
        cumulative = 0.5 * (1.0 + lax.erf(up * math.sqrt(0.5)))
        density = jnp.exp2(up * up * (-0.5 * LOG2E)) * (1.0 / math.sqrt(2.0 * math.pi))
        active_ref[lines] = (up * cumulative).astype(jnp.bfloat16)
        slope_ref[lines] = (cumulative + up * density).astype(jnp.bfloat16)
        up = following


def out_up_project(mixed, row_low, gathered, vectors, bias, local_hidden, local_width):
    length, features = row_low.shape
    fsdp_count, tp_count, rows, _ = gathered.shape
    hidden_units = local_hidden * tp_count
    block_width = math.gcd(math.gcd(local_hidden, 512), local_width)
    each = local_hidden // block_width
    column = pl.BlockSpec((length, block_width), lambda step: (0, step))
    return pl.pallas_call(
        out_up_kernel,
        grid=(hidden_units // block_width,),
        in_specs=[
            whole(length, features),
            whole(length, features),
            pl.BlockSpec(
                (fsdp_count, tp_count, rows, local_width),
                lambda step: (0, 0, 0, local_hidden // local_width),
            ),
            pl.BlockSpec(
                (fsdp_count, 1, rows, block_width),
                lambda step: (0, step // each, 0, step % each),
            ),
            whole(*vectors.shape),
            pl.BlockSpec((1, block_width), lambda step: (0, step)),
        ],
        out_specs=[column, column]
        + [whole(length, features), whole(length, 1), whole(length, features)]
        + [whole(features, features)],
        out_shape=[
            low_shape(length, hidden_units),
            low_shape(length, hidden_units),
            wide_shape(length, features),
            wide_shape(length, 1),
            low_shape(length, features),
            low_shape(features, features),
        ],
        compiler_params=pltpu.CompilerParams(vmem_limit_bytes=VMEM_LIMIT),
        cost_estimate=cost(
            2 * length * features * (hidden_units + features),
            36 << 20,
            2 * length * hidden_units,
        ),
        name="out_up_project",
    )(mixed, row_low, gathered, gathered, vectors, bias)


def piece_lanes(place_ref, sources, group):
    part, low = group
    widths = [sources[0].shape[2], sources[4].shape[2]]
    return (place_ref[1] ^ low) * sum(widths) + sum(widths[:part]), widths[part]


def piece_copies(places, place_ref, sources, held, sems, group):
    rows = sources[0].shape[1]
    found = []
    for at, (part, source, place, high, low) in enumerate(places):
        if (part, low) != group:
            continue
        row = pl.multiple_of((place_ref[0] ^ high) * rows, rows)
        lane, part_width = piece_lanes(place_ref, sources, group)
        found.append(
            pltpu.make_async_copy(
                sources[source].at[place],
                held.at[pl.ds(row, rows), pl.ds(pl.multiple_of(lane, 128), part_width)],
                sems.at[at],
            )
        )
    return found


PIECE_GROUPS = [(part, low) for low in range(2) for part in range(2)]


def down_kernel(
    places, place_ref, active_ref, unit_ref, teacher_ref, weight_ref, vector_ref, *refs
):
    count = 1 + max(source for _, source, _, _, _ in places)
    sources = refs[:count]
    out_ref, grad_ref, low_ref, sums_ref, held, sems = refs[count:]
    step = pl.program_id(0)
    copies = partial(piece_copies, places, place_ref, sources, held, sems)

    @pl.when(step == 0)
    def _():
        for group in PIECE_GROUPS:
            for copy in copies(group):
                copy.start()
        sums_ref[...] = jnp.zeros_like(sums_ref)

    normed_first = unit_ref[...] * vector_ref[0:1] + vector_ref[1:2]
    before = normed_first + vector_ref[2:3]
    for group in PIECE_GROUPS:

        @pl.when(step == 0)
        def _(group=group):
            for copy in copies(group):
                copy.wait()

        lane, part_width = piece_lanes(place_ref, sources, group)
        span = pl.ds(pl.multiple_of(lane, 128), part_width)
        before = before + dot_last(active_ref[:, span], held[:, span])

    unit, inverse = unit_of(before)
    gain = vector_ref[3:4]
    result = unit * gain + vector_ref[4:5]
    out_ref[...] = result.astype(jnp.bfloat16)
    differ = result - teacher_ref[...].astype(jnp.float32)
    grad = differ * weight_ref[...]
    scaled = grad * gain
    grad_before = inverse * (
        scaled
        - jnp.mean(scaled, axis=-1, keepdims=True)
        - unit * jnp.mean(scaled * unit, axis=-1, keepdims=True)
    )
    grad_ref[...] = grad_before
    low_ref[...] = grad_before.astype(jnp.bfloat16)
    for at, term in enumerate((grad * unit, grad, grad_before, grad * differ)):
        sums_ref[at : at + 1] += jnp.sum(term, axis=0, keepdims=True)


def down_project(chain, place, active, unit, teacher, weight, vectors):
    length, hidden_units = active.shape
    features = unit.shape[1]
    sources, places = (chain.sources(), chain.places())
    line = lambda width: pl.BlockSpec((BLOCK, width), lambda step: (step, 0))
    return pl.pallas_call(
        partial(down_kernel, places),
        grid=(length // BLOCK,),
        in_specs=[SCALARS, line(hidden_units), line(features), line(features), line(1)]
        + [whole(*vectors.shape)]
        + [ANYWHERE] * len(sources),
        out_specs=[line(features), line(features), line(features), whole(8, features)],
        out_shape=[
            low_shape(length, features),
            wide_shape(length, features),
            low_shape(length, features),
            wide_shape(8, features),
        ],
        scratch_shapes=[
            pltpu.VMEM((features, hidden_units), jnp.bfloat16),
            pltpu.SemaphoreType.DMA((len(places),)),
        ],
        compiler_params=pltpu.CompilerParams(vmem_limit_bytes=VMEM_LIMIT),
        cost_estimate=cost(2 * length * features * hidden_units, 36 << 20),
        name="down_project",
    )(place, active, unit, teacher, weight, vectors, *sources)


def column_copies(places, tp_places, each, block_width, me_fsdp, held, pieces, sems, at):
    rows = pieces[0].shape[1]
    found = []
    for number, (_, output, place, high, low) in enumerate(places):
        if low:
            continue
        row = pl.multiple_of((me_fsdp ^ high) * rows, rows)
        lane = pl.multiple_of(at % each * block_width, 128)
        found.append(
            pltpu.make_async_copy(
                held.at[at, pl.ds(row, rows)],
                pieces[output].at[place + at // each * tp_places, :, pl.ds(lane, block_width)],
                sems.at[at, number],
            )
        )
    return found


def down_back_kernel(
    places, tp_places, each, place_ref, grad_ref, active_ref, kept_ref, sent_ref,
    turned, held, sems,
):
    step = pl.program_id(0)

    @pl.when(step == 0)
    def _():
        turned[...] = grad_ref[...].T

    copies = partial(
        column_copies, places, tp_places, each, active_ref.shape[1], place_ref[0], held,
        (kept_ref, sent_ref), sems,
    )
    held[step] = dot_plain(turned[...], active_ref[...]).astype(jnp.bfloat16)
    for copy in copies(step):
        copy.start()

    @pl.when(step == 2 * each - 1)
    def _():
        for at in range(2 * each):
            for copy in copies(at):
                copy.wait()


def up_back_kernel(
    places, tp_places, each, down_places, place_ref, grad_ref, hidden_ref, slope_ref, up_ref, *refs
):
    count = 1 + max(source for _, source, _, _, _ in down_places)
    sources = refs[:count]
    total_ref, bias_ref, kept_ref, sent_ref, turned, held, sems, down_held, down_sems = refs[count:]
    step = pl.program_id(0)
    down_copies = partial(piece_copies, down_places, place_ref, sources, down_held, down_sems)
    length, features = grad_ref.shape
    block_width = slope_ref.shape[1]

    @pl.when(step == 0)
    def _():
        for group in PIECE_GROUPS:
            for copy in down_copies(group):
                copy.start()
        turned[...] = hidden_ref[...].T
        total_ref[...] = jnp.zeros_like(total_ref)

    for at, group in enumerate(PIECE_GROUPS):

        @pl.when(step == at * (each // 2))
        def _(group=group):
            for copy in down_copies(group):
                copy.wait()

    copies = partial(
        column_copies, places, tp_places, each, block_width, place_ref[0], held,
        (kept_ref, sent_ref), sems,
    )
    column = (place_ref[1] ^ (step // each)) * each + step % each
    lane = pl.multiple_of(column * block_width, block_width)
    down_weight = down_held[:, pl.ds(lane, block_width)]
    up_weight = up_ref[:, 0].reshape(features, block_width)
    spans = [slice(at * BLOCK, (at + 1) * BLOCK) for at in range(length // BLOCK)]
    grads, bias = ([], jnp.zeros((1, block_width), jnp.float32))
    found = dot_plain(grad_ref[spans[0]], down_weight)
    for at, span in enumerate(spans):
        following = (
            dot_plain(grad_ref[spans[at + 1]], down_weight) if at + 1 < len(spans) else None
        )
        grad_up = found * slope_ref[span].astype(jnp.float32)
        bias = bias + jnp.sum(grad_up, axis=0, keepdims=True)
        grads.append(grad_up.astype(jnp.bfloat16))
        found = following
    bias_ref[...] = bias
    grad_up = jnp.concatenate(grads, axis=0)
    held[step] = dot_plain(turned[...], grad_up).astype(jnp.bfloat16)
    for copy in copies(step):
        copy.start()
    total_ref[...] += dot_last(grad_up, up_weight)

    @pl.when(step == 2 * each - 1)
    def _():
        for at in range(2 * each):
            for copy in copies(at):
                copy.wait()


def column_plan(kind, local_hidden):
    block_width = math.gcd(local_hidden, 512)
    each = local_hidden // block_width
    places = scatter_places([kind])
    tp_places = next(place for _, at, place, high, low in places if at == 0 and low and not high)

    def column(step, where):
        return (where[1] ^ (step // each)) * each + step % each

    return block_width, each, places, tp_places, column


def keep(*shape):
    return pl.BlockSpec(shape, lambda step, where: (0,) * len(shape))


def column_scratch(features, length, each, block_width, places):
    return [
        pltpu.VMEM((features, length), jnp.bfloat16),
        pltpu.VMEM((2 * each, features, block_width), jnp.bfloat16),
        pltpu.SemaphoreType.DMA((2 * each, len(places))),
    ]


def down_back(place, grad_down, active, rows, local_hidden, kind):
    length, features = grad_down.shape
    block_width, each, places, tp_places, column = column_plan(kind, local_hidden)
    piece = low_shape(len(places) // 2, rows, local_hidden)
    return pl.pallas_call(
        partial(down_back_kernel, places, tp_places, each),
        grid_spec=pltpu.PrefetchScalarGridSpec(
            num_scalar_prefetch=1,
            grid=(2 * each,),
            in_specs=[
                keep(length, features),
                pl.BlockSpec((length, block_width), lambda step, where: (0, column(step, where))),
            ],
            out_specs=[ANYWHERE] * 2,
            scratch_shapes=column_scratch(features, length, each, block_width, places),
        ),
        out_shape=[piece] * 2,
        compiler_params=pltpu.CompilerParams(vmem_limit_bytes=VMEM_LIMIT),
        cost_estimate=cost(4 * length * features * local_hidden, 20 << 20),
        name="down_back",
    )(place, grad_down, active)


def up_back(place, grad_down, hidden, slope, chain, gathered, kind):
    length, features = hidden.shape
    fsdp_count, tp_count, rows, _ = gathered.shape
    local_hidden = slope.shape[1] // tp_count
    sources, down_places = (chain.sources(), chain.places())
    block_width, each, places, tp_places, column = column_plan(kind, local_hidden)
    piece = low_shape(len(places) // 2, rows, local_hidden)
    block = pl.BlockSpec((length, block_width), lambda step, where: (0, column(step, where)))
    return pl.pallas_call(
        partial(up_back_kernel, places, tp_places, each, down_places),
        grid_spec=pltpu.PrefetchScalarGridSpec(
            num_scalar_prefetch=1,
            grid=(2 * each,),
            in_specs=[
                keep(length, features),
                keep(length, features),
                block,
                pl.BlockSpec(
                    (fsdp_count, 1, rows, block_width),
                    lambda step, where: (0, where[1] ^ (step // each), 0, step % each),
                ),
            ]
            + [ANYWHERE] * len(sources),
            out_specs=[
                keep(length, features),
                pl.BlockSpec((1, block_width), lambda step, where: (0, column(step, where))),
            ]
            + [ANYWHERE] * 2,
            scratch_shapes=column_scratch(features, length, each, block_width, places)
            + [
                pltpu.VMEM((features, slope.shape[1]), jnp.bfloat16),
                pltpu.SemaphoreType.DMA((len(down_places),)),
            ],
        ),
        out_shape=[wide_shape(length, features), wide_shape(1, local_hidden * tp_count)]
        + [piece] * 2,
        compiler_params=pltpu.CompilerParams(vmem_limit_bytes=VMEM_LIMIT),
        cost_estimate=cost(12 * length * features * local_hidden, 40 << 20),
        name="up_back",
    )(place, grad_down, hidden, slope, gathered, *sources)


def norm_back_kernel(
    base_ref, grad_ref, unit_ref, inverse_ref, gain_ref, weight_ref, first_ref, low_ref, mixed_ref, sums_ref
):
    @pl.when(pl.program_id(0) == 0)
    def _():
        sums_ref[...] = jnp.zeros_like(sums_ref)

    grad, unit = (base_ref[...] + grad_ref[...], unit_ref[...])
    scaled = grad * gain_ref[...]
    found = inverse_ref[...] * (
        scaled
        - jnp.mean(scaled, axis=-1, keepdims=True)
        - unit * jnp.mean(scaled * unit, axis=-1, keepdims=True)
    )
    first_ref[...] = found
    low = found.astype(jnp.bfloat16)
    low_ref[...] = low
    mixed_ref[...] = dot_plain(low, weight_ref[...]).astype(jnp.bfloat16)
    for at, term in enumerate((grad * unit, grad, found)):
        sums_ref[at : at + 1] += jnp.sum(term, axis=0, keepdims=True)


def norm_back(grad_second, grad_hidden, unit, inverse, gain, full_out):
    length, features = unit.shape
    line = lambda width: pl.BlockSpec((BLOCK, width), lambda step: (step, 0))
    return pl.pallas_call(
        norm_back_kernel,
        grid=(length // BLOCK,),
        in_specs=[line(features)] * 3 + [line(1), whole(1, features)]
        + [whole(*full_out.shape)],
        out_specs=[line(features), line(features), line(full_out.shape[1]), whole(8, features)],
        out_shape=[
            wide_shape(length, features),
            low_shape(length, features),
            low_shape(length, full_out.shape[1]),
            wide_shape(8, features),
        ],
        compiler_params=pltpu.CompilerParams(vmem_limit_bytes=VMEM_LIMIT),
        cost_estimate=cost(2 * length * features * features, 22 << 20),
        name="norm_back",
    )(grad_second, grad_hidden, unit, inverse, gain, full_out)


def weight_grad_kernel(products, spans, places, extra, place_ref, *refs):
    lefts = 1 + max(left for left, _ in products)
    rights = 1 + max(right for _, right in products)
    left_refs, right_refs = (refs[:lefts], refs[lefts : lefts + rights])
    refs = refs[lefts + rights :]
    if extra:
        extra_ref, refs = (refs[0], refs[1:])
    parts = 2 * len(spans)
    pieces, scratch = (refs[:parts], refs[parts:])
    turned, held, sems = (scratch[:lefts], scratch[lefts:-1], scratch[-1])
    me_fsdp, me_tp = (place_ref[0], place_ref[1])
    rows = pieces[0].shape[1]
    started = []

    def start(target):
        for part, output, place, high, low in places:
            fsdp, tp = (me_fsdp ^ high, me_tp ^ low)
            for begin, size, which, per_tp, column in spans[part]:
                if which != target:
                    continue
                if target == len(products):
                    fsdp_count = extra_ref.shape[0] // 2
                    from_ref = extra_ref.at[tp * fsdp_count + fsdp]
                    row_span = pl.ds(0, extra_ref.shape[1])
                else:
                    row = pl.multiple_of(fsdp * rows, rows)
                    lane = pl.multiple_of(tp * per_tp + column, 128)
                    from_ref = held[target].at[pl.ds(row, rows), pl.ds(lane, size)]
                    row_span = pl.ds(0, rows)
                copy = pltpu.make_async_copy(
                    from_ref,
                    pieces[output].at[place, row_span, pl.ds(begin, size)],
                    sems.at[len(started)],
                )
                copy.start()
                started.append(copy)

    if extra:
        start(len(products))
    for at, left in enumerate(left_refs):
        turned[at][...] = left[...].T
    for target, (left, right) in enumerate(products):
        features = held[target].shape[0]
        for block in range(features // BLOCK):
            lines = slice(block * BLOCK, (block + 1) * BLOCK)
            held[target][lines] = dot_plain(turned[left][lines], right_refs[right][...]).astype(
                jnp.bfloat16
            )
        start(target)
    for copy in started:
        copy.wait()


def weight_grads(place, lefts, rights, products, spans, kinds, rows, part_widths, extra=None):
    length, features = lefts[0].shape
    places = scatter_places(kinds)
    copies = sum(len(spans[entry[0]]) for entry in places)
    devices = lax.axis_size("fsdp") * lax.axis_size("tp")
    outs = [low_shape(devices // 2, rows, part_widths[at // 2]) for at in range(2 * len(spans))]
    operands = list(lefts) + list(rights) + ([] if extra is None else [extra])
    flops = sum(2 * length * features * rights[right].shape[1] for _, right in products)
    return pl.pallas_call(
        partial(weight_grad_kernel, products, spans, places, extra is not None),
        in_specs=[SCALARS] + [whole(*operand.shape) for operand in operands],
        out_specs=[ANYWHERE] * len(outs),
        out_shape=outs,
        scratch_shapes=[pltpu.VMEM((features, length), jnp.bfloat16) for _ in lefts]
        + [pltpu.VMEM((features, rights[right].shape[1]), jnp.bfloat16) for _, right in products]
        + [pltpu.SemaphoreType.DMA((copies,))],
        compiler_params=pltpu.CompilerParams(vmem_limit_bytes=VMEM_LIMIT),
        cost_estimate=cost(flops, 16 << 20),
        name="weight_grads",
    )(place, *operands)


def input_grad_kernel(flip, place_ref, base_ref, *refs):
    grads, weight_ref, out_ref = (refs[:-2], refs[-2], refs[-1])
    total = base_ref[...]
    at = 0
    for grad in grads:
        width = grad.shape[1]
        total = total + dot_last(grad[...], weight_ref[:, at : at + width])
        at += width
    out_ref[...] = total.astype(jnp.bfloat16)


def input_grad(place, base, grads, full_qkv, flip):
    length, features = base.shape
    half = length // 2
    each = half // BLOCK
    line = lambda width: pl.BlockSpec(
        (BLOCK, width), lambda step, where: ((where[1] ^ flip) * each + step, 0)
    )
    return pl.pallas_call(
        partial(input_grad_kernel, flip),
        grid_spec=pltpu.PrefetchScalarGridSpec(
            num_scalar_prefetch=1,
            grid=(each,),
            in_specs=[line(features)]
            + [line(grad.shape[1]) for grad in grads]
            + [pl.BlockSpec(full_qkv.shape, lambda step, where: (0, 0))],
            out_specs=pl.BlockSpec((BLOCK, features), lambda step, where: (step, 0)),
        ),
        out_shape=low_shape(half, features),
        compiler_params=pltpu.CompilerParams(vmem_limit_bytes=VMEM_LIMIT),
        cost_estimate=cost(2 * half * features * full_qkv.shape[1], 14 << 20),
        name="input_grad",
    )(place, base, *grads, full_qkv)


def swap_in(pieces, tp_rank, *after):
    mine = lax.dynamic_index_in_dim(pieces, tp_rank, 0, keepdims=False)
    theirs = lax.dynamic_index_in_dim(pieces, 1 - tp_rank, 0, keepdims=False)
    if after:
        theirs = tie(theirs, *after)
    arrived = exchange(theirs, ACROSS)
    length = mine.shape[0]
    row = jnp.zeros((2 * length,) + mine.shape[1:], mine.dtype)
    row = lax.dynamic_update_slice_in_dim(row, mine, tp_rank * length, 0)
    return lax.dynamic_update_slice_in_dim(row, arrived, (1 - tp_rank) * length, 0)


def both_rows(mine, arrived, tp_rank):
    rows = jnp.zeros((2,) + mine.shape, mine.dtype)
    rows = lax.dynamic_update_slice_in_dim(rows, mine[None], tp_rank, 0)
    return lax.dynamic_update_slice_in_dim(rows, arrived[None], 1 - tp_rank, 0)


def on_device_rows(
    inputs,
    segment_ids,
    valid_mask,
    teacher,
    w_query,
    w_key,
    w_value,
    w_out,
    b_query,
    b_value,
    w_up,
    b_up,
    w_down,
    ln_gains,
    ln_shifts,
):
    seq_count, piece_len, features = inputs.shape
    fsdp_count, tp_count = (lax.axis_size("fsdp"), lax.axis_size("tp"))
    fsdp_rank, tp_rank = (lax.axis_index("fsdp"), lax.axis_index("tp"))
    devices = fsdp_count * tp_count
    assert seq_count == tp_count
    total_tokens = seq_count * piece_len * tp_count * fsdp_count
    shard_rows, local_width = w_query.shape
    local_hidden = w_up.shape[1]
    width = local_width * tp_count
    late_width = local_width // 4
    early_width = 3 * late_width
    half = local_width // 2
    pairs = width // 128
    late_pairs = pairs // 4
    early_pairs = pairs - late_pairs
    place = jnp.stack([fsdp_rank, tp_rank]).astype(jnp.int32)

    late_at = 2 * early_width
    qkv_spans = [
        [
            (0, early_width, 0, early_width, 0),
            (early_width, late_width, 0, late_width, late_at),
            (local_width, half, 1, early_width, width),
            (local_width + half, 128, 3, 0, 0),
        ],
        [
            (0, early_width - half, 1, early_width, width + half),
            (early_width - half, late_width, 1, late_width, width + late_at),
            (half, early_width, 2, early_width, 2 * width),
            (half + early_width, late_width, 2, late_width, 2 * width + late_at),
        ],
    ]
    small_rows = 32
    small = (
        b_query[None],
        b_value[None],
        b_up[None],
        ln_gains,
        ln_shifts,
        valid_mask,
    )
    up_cut = (local_hidden + local_width) // 2
    up_rest = local_hidden - up_cut
    up_spans = [
        [(0, up_cut, 0, local_hidden, 0)],
        [
            (0, up_rest, 0, local_hidden, up_cut),
            (up_rest, early_width, 1, early_width, 0),
            (up_rest + early_width, late_width, 1, late_width, late_at),
        ],
    ]
    qkv_first, qkv_second, up_shard, down_first, down_second = shards(
        place, w_query, w_key, w_value, w_out.T, w_up, w_down.T, small
    )
    chain_qkv = GatherChain([qkv_first, qkv_second])
    chain_down = GatherChain([down_first, down_second])
    row_low = swap_in(inputs, tp_rank)
    seg = lax.dynamic_index_in_dim(segment_ids, tp_rank, 0, keepdims=False)[:, None]
    chain_qkv.advance()
    chain_qkv.advance()
    chain_qkv.advance(row_low)
    gathered = lax.all_gather(
        tie(up_shard, chain_qkv.marks()), ("fsdp", "tp"), axis=0, tiled=False
    ).reshape(fsdp_count, tp_count, shard_rows, local_hidden + local_width)
    chain_qkv.advance()
    chain_qkv.finish()
    chain_down.advance(chain_qkv.arrived)
    queries, keys, values, full_qkv, small_all = qkv_project(
        chain_qkv, qkv_spans, tie(place, chain_down.marks()), row_low, width, small_rows
    )
    valid_row = (
        lax.dynamic_slice(
            small_all.reshape(tp_count, fsdp_count, small_rows, 128),
            (0, fsdp_rank, MASK_ROW + tp_rank * (piece_len // 128), 0),
            (tp_count, 1, piece_len // 128, 128),
        )
        .reshape(-1)
        .astype(jnp.float32)
    )
    small_all = small_all.astype(jnp.float32)
    small_at = 2 * (local_width // 128)
    bias_up = small_all[:, small_at].reshape(1, -1)

    def feature_rows(columns, rows):
        return (
            columns[:fsdp_count]
            .reshape(fsdp_count, rows, features // fsdp_count)
            .transpose(1, 0, 2)
            .reshape(rows, features)
        )

    gains = feature_rows(small_all[:, small_at + 1], 2)
    shifts = feature_rows(small_all[:, small_at + 2 : small_at + 4], 4)
    valid_count = jnp.sum(small_all[:, small_at + 4, 0] * 256.0 + small_all[:, small_at + 4, 1])

    chain_down.advance(queries)
    queries = tie(queries, chain_down.marks())
    attended = attend(queries, keys, values, seg, 0, pairs // 2)
    teacher_row = swap_in(teacher, tp_rank, attended)
    chain_down.advance(attended)
    mixed, q_padded, k_padded = attend(
        queries, keys, tie(values, chain_down.marks()), seg, pairs // 2, pairs // 2, attended
    )
    weight = (valid_row * (total_tokens / valid_count))[:, None]
    chain_down.advance(mixed)
    vectors = jnp.stack([shifts[2], gains[0], shifts[0]])
    active, slope, unit_first, inverse_first, hidden_low, full_out = out_up_project(
        tie(mixed, chain_down.marks(), weight),
        row_low,
        gathered,
        vectors,
        bias_up,
        local_hidden,
        local_width,
    )
    chain_down.finish(active)
    vectors = jnp.stack([gains[0], shifts[0], shifts[3], gains[1], shifts[1]])
    result_low, grad_second, grad_down, sums_second = down_project(
        chain_down, place, active, unit_first, teacher_row, weight, vectors
    )

    weight_chain = chain_down
    chain_down = ScatterChain(
        *down_back(place, grad_down, active, shard_rows, local_hidden, "across"), "across"
    )
    mine = lax.dynamic_slice_in_dim(result_low, tp_rank * piece_len, piece_len, 0)
    theirs = lax.dynamic_slice_in_dim(result_low, (1 - tp_rank) * piece_len, piece_len, 0)
    arrived_out = exchange(theirs, ACROSS)
    grad_hidden, grad_b_up, kept, sent = up_back(
        place, tie(grad_down, chain_down.marks(), arrived_out), hidden_low, slope, weight_chain, gathered, "far"
    )
    chain_up = ScatterChain(kept, sent, "far")
    chain_down.advance(grad_hidden)
    grad_first, grad_attend, grad_mixed, sums_first = norm_back(
        grad_second, tie(grad_hidden, chain_down.marks(), chain_up.marks()), unit_first, inverse_first, gains[:1], full_out
    )
    back = partial(attend_back, q_padded, k_padded, values, mixed)
    chain_up.advance(grad_mixed)
    attend_grads = back(tie(grad_mixed, chain_up.marks()), 0, pairs, 0, pairs)
    advance_all([chain_up], attend_grads)

    def feature_pieces(rows):
        pieces = rows.reshape(rows.shape[0], fsdp_count, -1).transpose(1, 0, 2)
        pieces = pieces.reshape(fsdp_count, -1, 128)
        return jnp.concatenate([pieces] * tp_count, axis=0)

    def bias_pieces(grad):
        sums = jnp.sum(grad.astype(jnp.float32), axis=0)
        sums = [
            sums[:late_at].reshape(tp_count, -1),
            sums[late_at:].reshape(tp_count, -1),
        ]
        return jnp.concatenate(sums, axis=1).reshape(devices, -1)

    bias_pair = jnp.concatenate(
        [bias_pieces(attend_grads[0]), bias_pieces(attend_grads[2])], axis=1
    )
    bias_pair = jnp.pad(bias_pair, ((0, 0), (0, 128 - bias_pair.shape[1])))
    squares = jnp.sum(sums_second[3]) * (valid_count / total_tokens)
    lane = lax.broadcasted_iota(jnp.int32, (1, 128), 1)
    square_rows = jnp.concatenate(
        [
            jnp.where(lane == tp_rank * fsdp_count + fsdp_rank, term.astype(jnp.float32), 0.0)
            for term in split_three(squares)
        ],
        axis=0,
    )
    small = jnp.concatenate(
        [
            bias_pair[:, None],
            grad_b_up.reshape(devices, 1, 128),
            feature_pieces(
                jnp.stack(
                    [
                        sums_first[0],
                        sums_second[0],
                        sums_first[1],
                        sums_second[1],
                        sums_first[2],
                        sums_second[2],
                    ]
                )
            ),
            jnp.broadcast_to(square_rows[None], (devices, 3, 128)),
        ],
        axis=1,
    )
    small = jnp.pad(small, ((0, 0), (0, 16 - small.shape[1]), (0, 0)))
    def spans_of(start, target):
        return [
            (start, early_width, target, early_width, 0),
            (start + early_width, late_width, target, late_width, late_at),
        ]

    grad_spans = [
        spans_of(0, 0) + spans_of(local_width, 1) + [(2 * local_width, 128, 4, 0, 0)],
        spans_of(0, 2) + spans_of(local_width, 3),
    ]
    grad_kinds = ["side", "far_side"]
    pieces = weight_grads(
        place,
        [grad_attend, tie(row_low, chain_up.marks())],
        [mixed] + list(attend_grads),
        [(0, 0), (1, 1), (1, 2), (1, 3)],
        grad_spans,
        grad_kinds,
        shard_rows,
        [2 * local_width + 128, 2 * local_width],
        small.astype(jnp.bfloat16),
    )
    attend_chains = [
        ScatterChain(pieces[2 * at], pieces[2 * at + 1], kind)
        for at, kind in enumerate(grad_kinds)
    ]
    advance_all([chain_down], pieces)
    input_theirs = input_grad(
        place,
        tie(grad_first, chain_down.marks(), attend_chains[0].sent),
        attend_grads,
        full_qkv,
        1,
    )
    arrived_inputs = exchange(input_theirs, ACROSS)
    advance_all(attend_chains, input_theirs)
    input_mine = input_grad(
        place,
        tie(grad_first, [chain.marks() for chain in attend_chains]),
        attend_grads,
        full_qkv,
        0,
    )
    advance_all([chain_up, chain_down], input_mine)
    mine, arrived_out = tie((mine, arrived_out), chain_up.marks())
    hidden_out = both_rows(mine, arrived_out, tp_rank)
    advance_all(attend_chains, hidden_out)
    sent = [chain.marks() for chain in attend_chains]
    advance_all([chain_up, chain_down], sent)
    arrived_inputs = tie(arrived_inputs, sent)
    grad_inputs = both_rows(input_mine, arrived_inputs, tp_rank)
    while attend_chains[0].at < len(attend_chains[0].steps):
        advance_all(attend_chains, grad_inputs)
    sent = [chain.marks() for chain in attend_chains]
    grad_w_down = chain_down.finish(sent)
    grad_w_up = chain_up.finish(sent)
    first, second = [chain.finish() for chain in attend_chains]
    grad_w_out = first[:, :local_width].T
    grad_w_query = first[:, local_width : 2 * local_width]
    grad_w_key, grad_w_value = (second[:, :local_width], second[:, local_width:])
    own = first[:, 2 * local_width :]
    bias_size, row = (b_query.shape[0], 2)
    gain_rows = ln_gains.size // 128
    shift_rows = ln_shifts.size // 128
    loss_row = row + gain_rows + shift_rows
    loss_value = jnp.sum(own[loss_row : loss_row + 3]) / (features * valid_count)
    return (
        hidden_out,
        loss_value,
        grad_inputs,
        grad_w_query,
        grad_w_key,
        grad_w_value,
        grad_w_out,
        own[0, :bias_size],
        own[0, bias_size : 2 * bias_size],
        grad_w_up,
        own[1],
        grad_w_down.T,
        own[row : row + gain_rows].reshape(ln_gains.shape),
        own[row + gain_rows : loss_row].reshape(ln_shifts.shape),
    )


def solution(mesh):
    in_specs = (
        P("fsdp", "tp", None),
        P("fsdp", None),
        P("fsdp", "tp"),
        P("fsdp", "tp", None),
        P("fsdp", "tp"),
        P("fsdp", "tp"),
        P("fsdp", "tp"),
        P("tp", "fsdp"),
        P(("tp", "fsdp")),
        P(("tp", "fsdp")),
        P("fsdp", "tp"),
        P(("tp", "fsdp")),
        P("tp", "fsdp"),
        P(None, "fsdp"),
        P(None, "fsdp"),
    )
    out_specs = (
        P("fsdp", "tp", None),
        P(),
        P("fsdp", "tp", None),
        P("fsdp", "tp"),
        P("fsdp", "tp"),
        P("fsdp", "tp"),
        P("tp", "fsdp"),
        P(("tp", "fsdp")),
        P(("tp", "fsdp")),
        P("fsdp", "tp"),
        P(("tp", "fsdp")),
        P("tp", "fsdp"),
        P(None, "fsdp"),
        P(None, "fsdp"),
    )
    rows_plan = rows_plan_fits(mesh)
    return jax.shard_map(
        on_device_rows if rows_plan else on_device_heads, mesh=mesh, in_specs=in_specs, out_specs=out_specs, check_vma=False
    )
```
